32 devices in a mesh: gx: 8 (over z, x), gy: 4 (over y, core).
Axes of the slice: x: 2, y: 2, z: 4, core: 2. Of those that a mesh axis runs over, the one named last changes fastest.
Arguments:
- features: bfloat16 [16, 8, 16, 128], P('gx', 'gy'), may hold values from -6 to 6
- positions: float32 [16, 8, 3, 16], P('gx', 'gy')
- species: int32 [16, 8, 16], P('gx', 'gy'), may hold values from 0 to 5
- neighbours: int32 [16, 8, 16, 32], P('gx', 'gy'), may hold values from 0 to 143, as said below
- counts: int32 [16, 8, 16], P('gx', 'gy'), may hold values from 0 to 32, as said below
- species_gain: float32 [6, 128], replicated, may hold values from 0.1 to 1.9
- radial_in: float32 [2, 8, 64], replicated, may hold values from -4 to 4
- radial_out: float32 [2, 64, 384], replicated, may hold values from -1 to 1
- mixing: float32 [2, 384, 128], replicated, may hold values from -0.3125 to 0.3125
- readout: float32 [128], replicated, may hold values from -0.5 to 0.5
Outputs:
- energy: float32 [16, 8, 16], P('gx', 'gy')
- forces: float32 [16, 8, 3, 16], P('gx', 'gy')
- feature_grad: float32 [16, 8, 16, 128], P('gx', 'gy')
The draws below stay inside these ranges and needn't reach their ends.
Inputs may be any that keep to these rules, and one draw needn't show every extreme that they name: `neighbours`: A code n names the atom in slot n % 16 of the column displaced by ((n // 16) // 3 - 1, (n // 16) % 3 - 1) columns, periodically; the codes of one atom are distinct and never name the atom itself. Neighbour slots 0 to counts - 1 of an atom are live, the rest padding.
All inputs are finite; a program needn't handle non-finite values.
Results may differ from the reference program's by a relative error of at most 0.007.
Values may be sent and summed in bfloat16 or wider, within the bound.
No kernel may reach another device: no remote copies, remote signals or barrier semaphores. Data moves between devices by JAX's collectives and lax.ppermute only.
A program may use at most 64 MiB of HBM per device.

```python
import jax
import jax.numpy as jnp
from jax import lax

SLOTS = 16
NEIGH = 32
CHANNELS = 128
RADIAL = 64
BASIS = 8
KINDS = 6
LAYERS = 2
GRID_X = 16
GRID_Y = 8


def lattice_sites(key):
    column_count = GRID_X * GRID_Y
    column_keys = jax.random.split(jax.random.fold_in(key, 31), column_count)
    orders = jax.vmap(lambda single: jax.random.permutation(single, 64))(column_keys)
    chosen = orders[:, :SLOTS].astype(jnp.int32).reshape(GRID_X, GRID_Y, SLOTS)
    return (chosen // 16, chosen // 4 % 4, chosen % 4)


def neighbour_table(key):
    site_x, site_y, site_z = lattice_sites(key)
    cand_x = []
    cand_y = []
    cand_z = []
    for offset in range(9):
        step_x = offset // 3 - 1
        step_y = offset % 3 - 1
        cand_x.append(jnp.roll(site_x, (-step_x, -step_y), (0, 1)) + 4 * step_x)
        cand_y.append(jnp.roll(site_y, (-step_x, -step_y), (0, 1)) + 4 * step_y)
        cand_z.append(jnp.roll(site_z, (-step_x, -step_y), (0, 1)))
    far_x = jnp.stack(cand_x, axis=2).reshape(GRID_X, GRID_Y, 1, 9 * SLOTS)
    far_y = jnp.stack(cand_y, axis=2).reshape(GRID_X, GRID_Y, 1, 9 * SLOTS)
    far_z = jnp.stack(cand_z, axis=2).reshape(GRID_X, GRID_Y, 1, 9 * SLOTS)
    diff_x = far_x - site_x[..., None]
    diff_y = far_y - site_y[..., None]
    diff_z = far_z - site_z[..., None]
    lattice_sq = diff_x * diff_x + diff_y * diff_y + diff_z * diff_z
    codes = jnp.arange(9 * SLOTS, dtype=jnp.int32)
    self_code = 4 * SLOTS + jnp.arange(SLOTS, dtype=jnp.int32)
    is_self = codes[None, None, None, :] == self_code[None, None, :, None]
    within = jnp.logical_and(lattice_sq <= 5, jnp.logical_not(is_self))
    scores = jnp.where(within, lattice_sq * 1024 + codes, lattice_sq * 1024 + 1073741824 + codes)
    scores = jnp.where(is_self, 2 * 1073741824 - 1, scores)
    ranked = jnp.argsort(scores, axis=-1)[..., :NEIGH].astype(jnp.int32)
    live = jnp.minimum(jnp.sum(within.astype(jnp.int32), axis=-1), NEIGH).astype(jnp.int32)
    live = live.at[0, 0, 0].set(NEIGH)
    return (ranked, live)


def draw_neighbours(key, part):
    ranked, live = neighbour_table(key)
    return ranked


def draw_counts(key, part):
    ranked, live = neighbour_table(key)
    return live


def draw_positions(key, part):
    site_x, site_y, site_z = lattice_sites(key)
    centres = jnp.stack([site_x, site_y, site_z], axis=2).astype(jnp.float32)
    centres = (centres + 0.5) * 1.5
    jitter_key = jax.random.fold_in(key, 47)
    jitter = jnp.clip(0.1 * jax.random.normal(jitter_key, centres.shape, jnp.float32), -0.3, 0.3)
    return (centres + jitter).astype(jnp.float32)


def touch_ends(array, stream_key, least, largest):
    longest = array.shape.index(max(array.shape))
    spots = []
    for shift in (0, 1):
        where = [jax.random.randint(jax.random.fold_in(stream_key, axis), (), 0, length) for axis, length in enumerate(array.shape)]
        where[longest] = (where[longest] + shift) % array.shape[longest]
        spots.append(tuple(where))
    return array.at[spots[0]].set(least).at[spots[1]].set(largest)


def level_of(stream_key, shape, cuts, least, largest):
    gain, own = 1.0, jax.random.fold_in(stream_key, 6)
    for position, blocks in cuts:
        draws = jnp.exp(jax.random.uniform(jax.random.fold_in(own, position), (blocks,), jnp.float32, least / len(cuts), largest / len(cuts)))
        gain = gain * jnp.repeat(draws, shape[position] // blocks).reshape([-1 if axis == position else 1 for axis in range(len(shape))])
    return gain


def normal_values(rng, shape, deviation, reach, pieces=(), kind=jnp.bfloat16):
    result = deviation * jax.random.normal(rng, shape, jnp.float32)
    if pieces:
        result = result * level_of(rng, shape, pieces, -0.22, 0.18)
    return jnp.clip(result, -reach, reach).astype(kind)


def setup_inputs(seed: int = 0) -> dict:
    streams_of = jax.random.split(jax.random.key(seed), 11)
    return {
        "features": normal_values(streams_of[0], (GRID_X, GRID_Y, SLOTS, CHANNELS), 1.0, 6.0, ((0, 8), (1, 4))),
        "positions": draw_positions(jax.random.fold_in(streams_of[10], 71), 0),
        "species": touch_ends(jax.random.randint(streams_of[2], (GRID_X, GRID_Y, SLOTS), 0, KINDS), jax.random.fold_in(streams_of[2], 1), 0, KINDS - 1).astype(jnp.int32),
        "neighbours": draw_neighbours(jax.random.fold_in(streams_of[10], 71), 0),
        "counts": draw_counts(jax.random.fold_in(streams_of[10], 71), 0),
        "species_gain": jnp.clip(1.0 + 0.18 * jax.random.normal(streams_of[5], (KINDS, CHANNELS), jnp.float32), 0.1, 1.9),
        "radial_in": normal_values(streams_of[6], (LAYERS, BASIS, RADIAL), (BASIS // 4) ** -0.5, 4.0, (), jnp.float32),
        "radial_out": normal_values(streams_of[7], (LAYERS, RADIAL, 3 * CHANNELS), (RADIAL // 2) ** -0.5, 1.0, (), jnp.float32),
        "mixing": normal_values(streams_of[8], (LAYERS, 3 * CHANNELS, CHANNELS), (3 * CHANNELS) ** -0.5, 0.3125, (), jnp.float32),
        "readout": normal_values(streams_of[9], (CHANNELS,), CHANNELS ** -0.5, 0.5, (), jnp.float32),
    }


column = 6.0
cutoff = 6.0
softening = 0.01
root_three = 3.0 ** 0.5
highest = lax.Precision.HIGHEST

def harmonics(unit_x, unit_y, unit_z):
    square = unit_x * unit_x + unit_y * unit_y + unit_z * unit_z
    return jnp.stack([jnp.ones_like(unit_x), unit_x, unit_y, unit_z, root_three * unit_x * unit_y, root_three * unit_y * unit_z, 0.5 * (3.0 * unit_z * unit_z - square), root_three * unit_x * unit_z, 0.5 * root_three * (unit_x * unit_x - unit_y * unit_y)], axis=1)

def layer_block(own_x, own_y, own_z, own_feat, other_x, other_y, other_z, other_feat, live_mask, weights):
    weight_in, weight_out, weight_mix = weights
    sep_x = other_x - own_x[:, None]
    sep_y = other_y - own_y[:, None]
    sep_z = other_z - own_z[:, None]
    dist_sq = sep_x * sep_x + sep_y * sep_y + sep_z * sep_z
    distance = jnp.sqrt(dist_sq + softening)
    envelope = jnp.square(jnp.maximum(1.0 - dist_sq / (cutoff * cutoff), 0.0)) * live_mask
    basis_count = weight_in.shape[0]
    spacing = cutoff / (basis_count - 1)
    centres = spacing * jnp.arange(basis_count, dtype=jnp.float32)
    radial_basis = jnp.exp(-jnp.square((distance[..., None] - centres) / spacing))
    hidden = jax.nn.silu(jnp.einsum('bkn,nh->bkh', radial_basis, weight_in, precision=highest))
    radial = jnp.einsum('bkh,hq->bkq', hidden, weight_out, precision=highest) * envelope[..., None]
    channels = other_feat.shape[-1]
    angular = harmonics(sep_x / cutoff, sep_y / cutoff, sep_z / cutoff)
    scalar = jnp.einsum('bmk,bkc->bmc', angular[:, 0:1], radial[..., :channels] * other_feat, precision=highest)[:, 0]
    vector = jnp.einsum('bmk,bkc->bmc', angular[:, 1:4], radial[..., channels:2 * channels] * other_feat, precision=highest)
    tensor = jnp.einsum('bmk,bkc->bmc', angular[:, 4:9], radial[..., 2 * channels:] * other_feat, precision=highest)
    invariants = jnp.concatenate([scalar, lax.optimization_barrier(jnp.sum(vector * vector, axis=1)), lax.optimization_barrier(jnp.sum(tensor * tensor, axis=1))], axis=-1)
    return jnp.dot(invariants, weight_mix, precision=highest) + own_feat

def layer(pos_all, feat_all, own_pos, own_feat, edge_lists, weights):
    channels = feat_all.shape[-1]
    slot_count = own_feat.shape[2]
    columns = own_feat.shape[0] * own_feat.shape[1]
    flat_x = pos_all[:, :, 0, :].reshape(-1)
    flat_y = pos_all[:, :, 1, :].reshape(-1)
    flat_z = pos_all[:, :, 2, :].reshape(-1)
    flat_feat = feat_all.reshape(-1, channels)
    owned = (own_pos[:, :, 0, :].reshape(columns, slot_count), own_pos[:, :, 1, :].reshape(columns, slot_count), own_pos[:, :, 2, :].reshape(columns, slot_count), own_feat.reshape(columns, slot_count, channels))

    def one_column(column_items):
        other_index, move_x, move_y, live_mask, own_x, own_y, own_z, own_rows = column_items
        return layer_block(own_x, own_y, own_z, own_rows, flat_x[other_index] + move_x, flat_y[other_index] + move_y, flat_z[other_index], flat_feat[other_index], live_mask, weights)
    return lax.map(jax.checkpoint(one_column), edge_lists + owned).reshape(-1, channels)

def reference(features, positions, species, neighbours, counts, species_gain, radial_in, radial_out, mixing, readout):
    kind_count = species_gain.shape[0]
    onehot = (species[..., None] == jnp.arange(kind_count, dtype=jnp.int32)).astype(jnp.float32)
    gain_rows = jnp.einsum('abse,ec->absc', onehot, species_gain, precision=highest)
    layer_one = (features.astype(jnp.float32) * gain_rows).astype(jnp.bfloat16)
    offsets = neighbours // SLOTS
    slot_of = neighbours % SLOTS
    step_x = offsets // 3 - 1
    step_y = offsets % 3 - 1
    col_x = jnp.arange(GRID_X, dtype=jnp.int32)[:, None, None, None]
    col_y = jnp.arange(GRID_Y, dtype=jnp.int32)[None, :, None, None]
    other_atom = ((col_x + step_x) % GRID_X * GRID_Y + (col_y + step_y) % GRID_Y) * SLOTS + slot_of
    shift_x = step_x.astype(jnp.float32) * column
    shift_y = step_y.astype(jnp.float32) * column
    validity = (jnp.arange(NEIGH, dtype=jnp.int32) < counts[..., None]).astype(jnp.float32)
    columns = GRID_X * GRID_Y
    edge_lists = (other_atom.reshape(columns, SLOTS, NEIGH), shift_x.reshape(columns, SLOTS, NEIGH), shift_y.reshape(columns, SLOTS, NEIGH), validity.reshape(columns, SLOTS, NEIGH))
    weights_one = (radial_in[0], radial_out[0], mixing[0])
    weights_two = (radial_in[1], radial_out[1], mixing[1])

    def first_layer(coords, values):
        return layer(coords, values, coords, values, edge_lists, weights_one)

    def second_layer(coords, values):
        return layer(coords, values, coords, values, edge_lists, weights_two)
    z_one, back_one = jax.vjp(first_layer, positions, layer_one.astype(jnp.float32))
    layer_two = z_one.astype(jnp.bfloat16).reshape(GRID_X, GRID_Y, SLOTS, CHANNELS)
    z_two, back_two = jax.vjp(second_layer, positions, layer_two.astype(jnp.float32))
    energy = jnp.dot(jax.nn.silu(z_two), readout, precision=highest)
    sigmoid = jax.nn.sigmoid(z_two)
    z_grad = sigmoid * (1.0 + z_two * (1.0 - sigmoid)) * readout
    pos_two, feat_two = back_two(z_grad)
    pos_one, feat_one = back_one(feat_two.reshape(-1, CHANNELS))
    forces = -(pos_one + pos_two)
    return (energy.reshape(GRID_X, GRID_Y, SLOTS), forces, feat_one)
```

```python
import functools

import jax
import jax.numpy as jnp
from jax import lax
from jax.experimental import pallas as pl
from jax.experimental.pallas import tpu as pltpu
from jax.sharding import PartitionSpec as P

column = 6.0
cutoff = 6.0
softening = 0.01
root_three = 3.0**0.5
f32 = jnp.float32
bf16 = jnp.bfloat16
dead_code = 255
code_lane = 32


def mm(a, b):
    return lax.dot_general(a, b, (((1,), (0,)), ((), ())), preferred_element_type=f32)


def nt(a, b):
    return lax.dot_general(a, b, (((1,), (1,)), ((), ())), preferred_element_type=f32)


def split(x):
    high = x.astype(bf16)
    return high, (x - high.astype(f32)).astype(bf16)


def three(product, a, b):
    a_high, a_low = split(a)
    b_high, b_low = split(b)
    return product(a_high, b_high) + product(a_low, b_high) + product(a_high, b_low)


def widened_in(weight):
    high, low = split(weight)
    high, low = high.astype(f32), low.astype(f32)
    stacked = jnp.concatenate([high, high, low, jnp.zeros_like(high)], axis=0)
    return stacked.T.astype(bf16)


def widened_out(weight):
    high, low = split(weight)
    high, low = high.astype(f32), low.astype(f32)
    stacked = jnp.concatenate([high, high, low], axis=0)
    return stacked.T.astype(bf16)


def atom_mask(slots, edges, neigh):
    lane = lax.broadcasted_iota(jnp.int32, (slots, edges), 1)
    row = lax.broadcasted_iota(jnp.int32, (slots, edges), 0)
    return (lane // neigh == row).astype(f32)


def harmonic_rows(ux, uy, uz):
    square = ux * ux + uy * uy + uz * uz
    return [
        jnp.ones_like(ux),
        ux,
        uy,
        uz,
        root_three * ux * uy,
        root_three * uy * uz,
        0.5 * (3.0 * uz * uz - square),
        root_three * ux * uz,
        0.5 * root_three * (ux * ux - uy * uy),
    ]


class Sizes:
    def __init__(self, cols_x, cols_y, slots, neigh, channels, basis, hidden):
        self.cols_x, self.cols_y = cols_x, cols_y
        self.slots, self.neigh, self.channels = slots, neigh, channels
        self.basis, self.hidden = basis, hidden
        self.inner_x, self.inner_y = cols_x + 2, cols_y + 2
        self.outer_y = cols_y + 4
        self.inner = self.inner_x * self.inner_y
        self.edges = slots * neigh
        self.window = 9 * slots

    def place(self, col):
        return lax.div(col, jnp.int32(self.inner_y)), lax.rem(col, jnp.int32(self.inner_y))

    def outer_row(self, a, b):
        return pl.multiple_of((a * self.outer_y + b) * self.slots, self.slots)

    def inner_row(self, a, b):
        return pl.multiple_of((a * self.inner_y + b) * self.slots, self.slots)


def loop(count, body, unroll):
    def step(i, carry):
        body(i)
        return carry

    lax.fori_loop(0, count, step, 0, unroll=unroll)


def gather_columns(sz, table, mask, mask_bf, code, sep, hot, xt):
    lane = lax.broadcasted_iota(jnp.int32, (sz.channels, sz.edges), 1)
    row = lax.broadcasted_iota(jnp.int32, (sz.channels, sz.edges), 0)
    spread = (row == code_lane + lane % sz.neigh).astype(bf16)
    target = lax.broadcasted_iota(jnp.int32, (sz.window, sz.edges), 0)
    ch, run = sz.channels, 3 * sz.slots

    def body(col):
        a, b = sz.place(col)
        meta = table[pl.ds(sz.outer_row(a + 1, b + 1), sz.slots), ch : 2 * ch]
        codes = jnp.sum(mm(meta, spread) * mask, axis=0, keepdims=True).astype(jnp.int32)
        code[pl.ds(col, 1), :] = codes
        one_hot = (target == codes).astype(f32).astype(bf16)
        hot[col] = one_hot
        own = mm(meta.astype(f32).T[:24].astype(bf16), mask_bf)
        window = jnp.concatenate(
            [table[pl.ds(sz.outer_row(a + d, b), run), :] for d in range(3)], axis=0
        )
        turned = window.astype(f32).T.astype(bf16)[: ch + 32]
        found = mm(turned, one_hot)
        xt[col] = found[:ch]
        diff = found[ch : ch + 24] - own
        total = diff[0:8] + diff[8:16] + diff[16:24]
        for d in range(3):
            sep[d, pl.ds(col, 1), :] = total[d : d + 1]

    loop(sz.inner, body, 4)


def geometry(code, sep, angular, dist, env):
    offset = code[...] >> 4
    step_x = (offset * 11) >> 5
    step_y = offset - 3 * step_x
    live = (code[...] != dead_code).astype(f32)
    sep_x = sep[0] + column * (step_x - 1).astype(f32)
    sep_y = sep[1] + column * (step_y - 1).astype(f32)
    sep_z = sep[2]
    sep[0] = sep_x
    sep[1] = sep_y
    dist_sq = sep_x * sep_x + sep_y * sep_y + sep_z * sep_z
    dist[...] = jnp.sqrt(dist_sq + softening)
    env[...] = jnp.square(jnp.maximum(1.0 - dist_sq / (cutoff * cutoff), 0.0)) * live
    rows = harmonic_rows(sep_x / cutoff, sep_y / cutoff, sep_z / cutoff)
    for m, value in enumerate(rows):
        angular[m] = value


def basis_rows(sz, dist_row):
    spacing = cutoff / (sz.basis - 1)
    centre = lax.broadcasted_iota(jnp.int32, (sz.basis, sz.edges), 0).astype(f32) * spacing
    shifted = (dist_row - centre) / spacing
    return jnp.exp(-shifted * shifted), shifted


def hidden_rows(sz, dist_row, env_row, weight_in):
    basis, _ = basis_rows(sz, dist_row)
    high = basis.astype(bf16).astype(f32)
    stacked = jnp.concatenate([high, basis - high, high, jnp.zeros_like(high)], axis=0)
    pre = mm(weight_in, stacked.astype(bf16))
    gate = 1.0 / (1.0 + jnp.exp(-pre))
    value = pre * gate
    weighted = value * env_row
    high, low = split(weighted)
    return jnp.concatenate([high, low, high], axis=0), value, gate * (1.0 + pre * (1.0 - gate))


def harmonic_blocks(sz, angular, col, mask):
    rows = [angular[m, pl.ds(col, 1), :] * mask for m in range(9)]
    return jnp.concatenate(rows, axis=0)


def messages(sz, blocks, radial, xt):
    ch, n = sz.channels, sz.slots
    high, low = split(blocks)
    out = []
    for l, (first, last) in enumerate(((0, 1), (1, 4), (4, 9))):
        product = (radial[l * ch : (l + 1) * ch] * xt).astype(bf16)
        both = jnp.concatenate(
            [high[first * n : last * n], low[first * n : last * n]], axis=0
        )
        got = nt(both, product)
        rows = (last - first) * n
        out.append(got[:rows] + got[rows:])
    return out


def invariants(sz, parts):
    n = sz.slots
    scalar, vector, tensor = parts
    squares = vector * vector
    second = squares[:n] + squares[n : 2 * n] + squares[2 * n :]
    squares = tensor * tensor
    third = squares[:n]
    for m in range(1, 5):
        third = third + squares[m * n : (m + 1) * n]
    return jnp.concatenate([scalar, second, third], axis=1)


def layer_forward(sz, col, angular, dist, env, mask, weight_in, weight_out, xt):
    dist_row, env_row = dist[pl.ds(col, 1), :], env[pl.ds(col, 1), :]
    weighted, _, _ = hidden_rows(sz, dist_row, env_row, weight_in)
    radial = mm(weight_out, weighted)
    return messages(sz, harmonic_blocks(sz, angular, col, mask), radial, xt)


def layer_backward(
    sz, col, angular, dist, env, mask, weight_in, weight_out, back_in, back_out, xt, one_hot,
    message, cotangent, ang_grad, dist_grad, env_grad,
):
    ch, n = sz.channels, sz.slots
    dist_row, env_row = dist[pl.ds(col, 1), :], env[pl.ds(col, 1), :]
    weighted, value, slope = hidden_rows(sz, dist_row, env_row, weight_in)
    radial = mm(weight_out, weighted)
    blocks = harmonic_blocks(sz, angular, col, mask).astype(bf16)
    scalar_cot = cotangent[:, :ch]
    vector_cot = 2.0 * cotangent[:, ch : 2 * ch]
    tensor_cot = 2.0 * cotangent[:, 2 * ch :]
    grads = [scalar_cot]
    grads += [message[m * n : (m + 1) * n] * vector_cot for m in range(1, 4)]
    grads += [message[m * n : (m + 1) * n] * tensor_cot for m in range(4, 9)]
    message_grad = jnp.concatenate(grads, axis=0)
    turned = message_grad.T
    grad_bf = message_grad.astype(bf16)
    lane = lax.broadcasted_iota(jnp.int32, turned.shape, 1)
    row_grads = []
    radial_grads = []
    input_grad = None
    for l, (first, last) in enumerate(((0, 1), (1, 4), (4, 9))):
        mine = jnp.where((lane >= first * n) & (lane < last * n), turned, 0.0).astype(bf16)
        product_grad = mm(mine, blocks)
        part = radial[l * ch : (l + 1) * ch]
        product = (part * xt).astype(bf16)
        row_grads.append(mm(grad_bf[first * n : last * n], product))
        radial_grads.append((product_grad * xt).astype(bf16))
        term = product_grad * part
        input_grad = term if input_grad is None else input_grad + term
    for l, (first, last) in enumerate(((0, 1), (1, 4), (4, 9))):
        for m in range(first, last):
            if m:
                got = row_grads[l][(m - first) * n : (m - first + 1) * n] * mask
                ang_grad[m, pl.ds(col, 1), :] = jnp.sum(got, axis=0, keepdims=True)
    both = mm(back_out, jnp.concatenate(radial_grads, axis=0))
    weighted_grad = both[: sz.hidden] + both[sz.hidden :]
    env_grad[pl.ds(col, 1), :] = jnp.sum(weighted_grad * value, axis=0, keepdims=True)
    pre_grad = (weighted_grad * env_row * slope).astype(bf16)
    both = mm(back_in, pre_grad)
    basis_grad = both[: sz.basis] + both[sz.basis : 2 * sz.basis]
    basis, shifted = basis_rows(sz, dist_row)
    spacing = cutoff / (sz.basis - 1)
    dist_grad[pl.ds(col, 1), :] = jnp.sum(
        basis_grad * basis * shifted * (-2.0 / spacing), axis=0, keepdims=True
    )
    return nt(one_hot, input_grad.astype(bf16))


def separation_grads(code, sep, dist, ang_grad, dist_grad, env_grad):
    sep_x, sep_y, sep_z = sep
    live = (code != dead_code).astype(f32)
    ux, uy, uz = sep_x / cutoff, sep_y / cutoff, sep_z / cutoff
    dist_sq = sep_x * sep_x + sep_y * sep_y + sep_z * sep_z
    inside = jnp.maximum(1.0 - dist_sq / (cutoff * cutoff), 0.0)
    sq_grad = dist_grad * (0.5 / dist) - env_grad * live * inside * (2.0 / (cutoff * cutoff))
    g = ang_grad
    r3 = root_three
    grad_x = g[1] + r3 * (uy * g[4] + uz * g[7] + ux * g[8]) - ux * g[6]
    grad_y = g[2] + r3 * (ux * g[4] + uz * g[5] - uy * g[8]) - uy * g[6]
    grad_z = g[3] + r3 * (uy * g[5] + ux * g[7]) + 2.0 * uz * g[6]
    return (
        2.0 * sep_x * sq_grad + grad_x / cutoff,
        2.0 * sep_y * sq_grad + grad_y / cutoff,
        2.0 * sep_z * sq_grad + grad_z / cutoff,
    )


def stacked_seps(sz, sep_grad, col):
    rows = [sep_grad[d, pl.ds(col, 1), :] for d in range(3)]
    full = jnp.concatenate(rows + [jnp.zeros((5, sz.edges), f32)], axis=0)
    high = full.astype(bf16).astype(f32)
    return jnp.concatenate([high, full - high], axis=0).astype(bf16)


def signed_hot(sz, one_hot, mask_bf):
    first = 4 * sz.slots
    return jnp.concatenate(
        [one_hot[:first], one_hot[first : first + sz.slots] - mask_bf, one_hot[first + sz.slots :]],
        axis=0,
    )


def stacked_back(weight):
    high, low = split(weight)
    return jnp.concatenate([high, low], axis=0)


def first_kernel(
    sz, table, radial_in, radial_out, mixing, readout,
    energy, back, kept,
    code, sep, hot, xt, angular, dist, env, inv, second, second_hot, second_xt, second_msg,
    ang_grad, dist_grad, env_grad, sep_grad, acc, acc_pos,
):
    ch, n = sz.channels, sz.slots
    run = 3 * n
    mask = atom_mask(n, sz.edges, sz.neigh)
    mask_bf = mask.astype(bf16)
    gather_columns(sz, table, mask, mask_bf, code, sep, hot, xt)
    geometry(code, sep, angular, dist, env)
    in_one, out_one = widened_in(radial_in[0]), widened_out(radial_out[0])

    def one(col):
        parts = layer_forward(
            sz, col, angular, dist, env, mask, in_one, out_one, xt[col]
        )
        kept[col] = jnp.concatenate(parts, axis=0)
        inv[pl.ds(pl.multiple_of(col * n, n), n), :] = invariants(sz, parts)

    loop(sz.inner, one, 2)
    own_rows = [
        table[(a * sz.outer_y + 1) * n : (a * sz.outer_y + 1 + sz.inner_y) * n, :ch]
        for a in range(1, 1 + sz.inner_x)
    ]
    first_out = three(mm, inv[...], mixing[0]) + jnp.concatenate(own_rows, axis=0).astype(f32)
    second[...] = first_out.astype(bf16)

    in_two, out_two = widened_in(radial_in[1]), widened_out(radial_out[1])
    back_in, back_out = stacked_back(radial_in[1]), stacked_back(radial_out[1])
    target = lax.broadcasted_iota(jnp.int32, (sz.window, sz.edges), 0)

    def spot(k):
        a = lax.div(k, jnp.int32(sz.cols_y)) + 1
        b = lax.rem(k, jnp.int32(sz.cols_y)) + 1
        return a, b, a * sz.inner_y + b

    owned = sz.cols_x * sz.cols_y

    def two(k):
        a, b, col = spot(k)
        window = jnp.concatenate(
            [second[pl.ds(sz.inner_row(a - 1 + d, b - 1), run), :] for d in range(3)], axis=0
        )
        turned = window.astype(f32).T.astype(bf16)
        found = mm(turned, hot[col])
        second_xt[k] = found
        parts = layer_forward(sz, col, angular, dist, env, mask, in_two, out_two, found)
        second_msg[k] = jnp.concatenate(parts, axis=0)
        inv[pl.ds(pl.multiple_of(k * n, n), n), :] = invariants(sz, parts)

    loop(owned, two, 2)
    own_rows = [
        second[(a * sz.inner_y + 1) * n : (a * sz.inner_y + 1 + sz.cols_y) * n, :]
        for a in range(1, 1 + sz.cols_x)
    ]
    out = three(mm, inv[: owned * n], mixing[1]) + jnp.concatenate(own_rows, axis=0).astype(f32)
    gate = 1.0 / (1.0 + jnp.exp(-out))
    weights = readout[...]
    energy[...] = three(nt, jnp.ones((8, ch), f32), out * gate * weights)
    out_grad = gate * (1.0 + out * (1.0 - gate)) * weights
    inv[: owned * n] = three(nt, out_grad, mixing[1])
    acc[...] = jnp.zeros_like(acc)
    acc_pos[...] = jnp.zeros_like(acc_pos)
    for a in range(sz.cols_x):
        first = ((a + 1) * sz.inner_y + 1) * n
        acc[first : first + sz.cols_y * n] = out_grad[a * sz.cols_y * n : (a + 1) * sz.cols_y * n]

    def two_back(k):
        a, b, col = spot(k)
        got = layer_backward(
            sz, col, angular, dist, env, mask, in_two, out_two, back_in, back_out,
            second_xt[k], hot[col], second_msg[k],
            inv[pl.ds(pl.multiple_of(k * n, n), n), :], ang_grad, dist_grad, env_grad,
        )
        for d in range(3):
            acc[pl.ds(sz.inner_row(a - 1 + d, b - 1), run), :] += got[d * run : (d + 1) * run]

    loop(owned, two_back, 2)
    grads = separation_grads(
        code[...], (sep[0], sep[1], sep[2]), dist[...], ang_grad, dist_grad[...], env_grad[...]
    )
    for d in range(3):
        sep_grad[d] = grads[d]

    def two_pos(k):
        a, b, col = spot(k)
        got = nt(signed_hot(sz, hot[col], mask_bf), stacked_seps(sz, sep_grad, col))
        got = got[:, :8] + got[:, 8:]
        for d in range(3):
            acc_pos[pl.ds(sz.inner_row(a - 1 + d, b - 1), run), :] += got[d * run : (d + 1) * run]

    loop(owned, two_pos, 4)
    back[:, :ch] = acc[...].astype(bf16)
    high = acc_pos[...].astype(bf16)
    low = (acc_pos[...] - high.astype(f32)).astype(f32)
    filler = jnp.zeros((acc_pos.shape[0], ch - 16), f32)
    back[:, ch:] = jnp.concatenate([high.astype(f32), low, filler], axis=1).astype(bf16)


def second_kernel(
    sz, table, cotangent, kept, radial_in, radial_out, mixing,
    feature_grad, forces,
    code, sep, hot, xt, angular, dist, env, inv,
    ang_grad, dist_grad, env_grad, sep_grad, acc, acc_pos,
):
    ch, n = sz.channels, sz.slots
    run = 3 * n
    mask = atom_mask(n, sz.edges, sz.neigh)
    mask_bf = mask.astype(bf16)
    gather_columns(sz, table, mask, mask_bf, code, sep, hot, xt)
    geometry(code, sep, angular, dist, env)
    in_one, out_one = widened_in(radial_in[0]), widened_out(radial_out[0])
    back_in, back_out = stacked_back(radial_in[0]), stacked_back(radial_out[0])
    inv[...] = three(nt, cotangent[:, :ch], mixing[0])
    acc[...] = jnp.zeros_like(acc)
    acc_pos[...] = jnp.zeros_like(acc_pos)

    def one_back(col):
        a, b = sz.place(col)
        got = layer_backward(
            sz, col, angular, dist, env, mask, in_one, out_one, back_in, back_out,
            xt[col], hot[col], kept[col],
            inv[pl.ds(pl.multiple_of(col * n, n), n), :], ang_grad, dist_grad, env_grad,
        )
        for d in range(3):
            acc[pl.ds(sz.outer_row(a + d, b), run), :] += got[d * run : (d + 1) * run]

    loop(sz.inner, one_back, 2)
    grads = separation_grads(
        code[...], (sep[0], sep[1], sep[2]), dist[...], ang_grad, dist_grad[...], env_grad[...]
    )
    for d in range(3):
        sep_grad[d] = grads[d]

    def one_pos(col):
        a, b = sz.place(col)
        got = nt(signed_hot(sz, hot[col], mask_bf), stacked_seps(sz, sep_grad, col))
        got = got[:, :8] + got[:, 8:]
        for d in range(3):
            acc_pos[pl.ds(sz.outer_row(a + d, b), run), :] += got[d * run : (d + 1) * run]

    loop(sz.inner, one_pos, 4)
    for a in range(sz.cols_x):
        outer = ((a + 2) * sz.outer_y + 2) * n
        inner = ((a + 1) * sz.inner_y + 1) * n
        rows = sz.cols_y * n
        feature_grad[a * rows : (a + 1) * rows] = (
            acc[outer : outer + rows] + cotangent[inner : inner + rows, :ch]
        )
        extra = cotangent[inner : inner + rows, ch : ch + 16]
        total = acc_pos[outer : outer + rows] + extra[:, :8] + extra[:, 8:]
        for b in range(sz.cols_y):
            forces[a * sz.cols_y + b] = -(total[b * n : (b + 1) * n].T)[:3]


def ring(axis):
    devices = lax.axis_size(axis)
    up = [(i, (i + 1) % devices) for i in range(devices)]
    return up, [(j, i) for i, j in up]


def extended(x, sides):
    for axis, dim in sides:
        up, down = ring(axis)
        length = x.shape[dim]
        last = lax.slice_in_dim(x, length - 2, length, axis=dim)
        initial = lax.slice_in_dim(x, 0, 2, axis=dim)
        before = lax.ppermute(last, axis, up)
        after = lax.ppermute(initial, axis, down)
        x = jnp.concatenate([before, x, after], axis=dim)
    return x


def summed(x, sides):
    total = x.astype(f32)
    for axis, dim in sides:
        up, down = ring(axis)
        length = x.shape[dim]
        sent = total.astype(bf16)
        last = lax.slice_in_dim(sent, length - 2, length, axis=dim)
        initial = lax.slice_in_dim(sent, 0, 2, axis=dim)
        before = lax.ppermute(last, axis, up).astype(f32)
        after = lax.ppermute(initial, axis, down).astype(f32)
        shape = list(x.shape)
        shape[dim] = length - 4
        parts = [before] + ([jnp.zeros(shape, f32)] if length > 4 else []) + [after]
        total = total + jnp.concatenate(parts, axis=dim)
    return total


def rounded(x):
    return lax.reduce_precision(x, 8, 7)


def shards(
    features, positions, species, neighbours, counts, species_gain, radial_in, radial_out, mixing, readout
):
    cols_x, cols_y, slots, channels = features.shape
    neigh = neighbours.shape[-1]
    kinds = species_gain.shape[0]
    basis, hidden = radial_in.shape[1:]
    sz = Sizes(cols_x, cols_y, slots, neigh, channels, basis, hidden)
    gain = jnp.zeros(features.shape, f32)
    for kind in range(kinds):
        gain = jnp.where((species == kind)[..., None], species_gain[kind], gain)
    layer_one = (features.astype(f32) * gain).astype(bf16)
    live = jnp.arange(neigh, dtype=jnp.int32) < counts[..., None]
    codes = jnp.where(live, neighbours, dead_code).astype(bf16)
    atoms = positions.transpose(0, 1, 3, 2)
    high = rounded(atoms)
    middle = rounded(atoms - high)
    low = atoms - high - middle
    gap = jnp.zeros(atoms.shape[:-1] + (5,), bf16)
    tail = jnp.zeros(atoms.shape[:-1] + (channels - code_lane - neigh,), bf16)
    block = jnp.concatenate(
        [
            layer_one,
            high.astype(bf16), gap, middle.astype(bf16), gap, low.astype(bf16), gap,
            jnp.zeros(atoms.shape[:-1] + (code_lane - 24,), bf16),
            codes,
            tail,
        ],
        axis=-1,
    )
    sides = (("gx", 0), ("gy", 1))
    table = extended(block, sides).reshape(-1, 2 * channels)

    inner_atoms = sz.inner * slots
    owned = cols_x * cols_y
    edges = sz.edges
    shared = [
        pltpu.VMEM((sz.inner, edges), jnp.int32),
        pltpu.VMEM((3, sz.inner, edges), f32),
        pltpu.VMEM((sz.inner, sz.window, edges), bf16),
        pltpu.VMEM((sz.inner, channels, edges), f32),
        pltpu.VMEM((9, sz.inner, edges), f32),
        pltpu.VMEM((sz.inner, edges), f32),
        pltpu.VMEM((sz.inner, edges), f32),
        pltpu.VMEM((inner_atoms, 3 * channels), f32),
    ]
    grads = [
        pltpu.VMEM((9, sz.inner, edges), f32),
        pltpu.VMEM((sz.inner, edges), f32),
        pltpu.VMEM((sz.inner, edges), f32),
        pltpu.VMEM((3, sz.inner, edges), f32),
    ]
    vmem = pl.BlockSpec(memory_space=pltpu.VMEM)
    params = pltpu.CompilerParams(vmem_limit_bytes=48 * 1024 * 1024)
    energy, back, kept = pl.pallas_call(
        functools.partial(first_kernel, sz),
        out_shape=(
            jax.ShapeDtypeStruct((8, owned * slots), f32),
            jax.ShapeDtypeStruct((inner_atoms, 2 * channels), bf16),
            jax.ShapeDtypeStruct((sz.inner, sz.window, channels), f32),
        ),
        in_specs=[vmem] * 5,
        out_specs=(vmem,) * 3,
        scratch_shapes=shared
        + [
            pltpu.VMEM((inner_atoms, channels), bf16),
            pltpu.VMEM((1, 8, 128), f32),
            pltpu.VMEM((owned, channels, edges), f32),
            pltpu.VMEM((owned, sz.window, channels), f32),
        ]
        + grads
        + [pltpu.VMEM((inner_atoms, channels), f32), pltpu.VMEM((inner_atoms, 8), f32)],
        compiler_params=params,
        name="forward_and_second_back",
    )(table, radial_in, radial_out, mixing, readout.reshape(1, -1))

    back = back.reshape(sz.inner_x, sz.inner_y, slots, 2 * channels)
    cotangent = summed(back, sides).reshape(inner_atoms, 2 * channels)
    outer_atoms = table.shape[0]
    feature_grad, forces = pl.pallas_call(
        functools.partial(second_kernel, sz),
        out_shape=(
            jax.ShapeDtypeStruct((owned * slots, channels), f32),
            jax.ShapeDtypeStruct((owned, 3, slots), f32),
        ),
        in_specs=[vmem] * 6,
        out_specs=(vmem,) * 2,
        scratch_shapes=shared
        + grads
        + [pltpu.VMEM((outer_atoms, channels), f32), pltpu.VMEM((outer_atoms, 8), f32)],
        compiler_params=params,
        name="first_back",
    )(table, cotangent, kept, radial_in, radial_out, mixing)
    return (
        energy[0].reshape(cols_x, cols_y, slots),
        forces.reshape(cols_x, cols_y, 3, slots),
        feature_grad.reshape(cols_x, cols_y, slots, channels),
    )


def solution(mesh):
    placed = (
        P("gx", "gy", None, None),
        P("gx", "gy", None, None),
        P("gx", "gy", None),
        P("gx", "gy", None, None),
        P("gx", "gy", None),
        P(),
        P(),
        P(),
        P(),
        P(),
    )
    return jax.shard_map(
        shards,
        mesh=mesh,
        in_specs=placed,
        out_specs=(P("gx", "gy", None), P("gx", "gy", None, None), P("gx", "gy", None, None)),
        check_vma=False,
    )
```

```python
import functools

import jax
import jax.numpy as jnp
from jax import lax
from jax.experimental import pallas as pl
from jax.experimental.pallas import tpu as pltpu
from jax.sharding import PartitionSpec as P

column = 6.0
cutoff = 6.0
softening = 0.01
root_three = 3.0**0.5
f32 = jnp.float32
bf16 = jnp.bfloat16
dead_code = 255
code_lane = 32
halo_lanes = 128


def mm(a, b):
    return lax.dot_general(a, b, (((1,), (0,)), ((), ())), preferred_element_type=f32)


def nt(a, b):
    return lax.dot_general(a, b, (((1,), (1,)), ((), ())), preferred_element_type=f32)


def split(x):
    high = x.astype(bf16)
    return high, (x - high.astype(f32)).astype(bf16)


def three(product, a, b):
    a_high, a_low = split(a)
    b_high, b_low = split(b) if b.dtype == f32 else (b[0], b[1])
    return product(a_high, b_high) + product(a_low, b_high) + product(a_high, b_low)


def parted(x):
    high = lax.reduce_precision(x, 8, 7)
    return high, x - high


def prepared(radial_in, radial_out, mixing):
    high, low = parted(radial_in)
    turned = jnp.concatenate([high, high, low, jnp.zeros_like(high)], axis=1).swapaxes(1, 2)
    back_in = jnp.concatenate([high, low], axis=1)
    high, low = parted(radial_out)
    wide = jnp.concatenate([high, high, low], axis=1).swapaxes(1, 2)
    high_mix, low_mix = parted(mixing)
    mix = jnp.stack([high_mix, low_mix], axis=1)
    return [x.astype(bf16) for x in (turned, wide, back_in, high, mix)]


def atom_mask(slots, edges, neigh):
    lane = lax.broadcasted_iota(jnp.int32, (slots, edges), 1)
    row = lax.broadcasted_iota(jnp.int32, (slots, edges), 0)
    return (lane // neigh == row).astype(f32)


def harmonic_rows(ux, uy, uz):
    square = ux * ux + uy * uy + uz * uz
    return [
        jnp.ones_like(ux),
        ux,
        uy,
        uz,
        root_three * ux * uy,
        root_three * uy * uz,
        0.5 * (3.0 * uz * uz - square),
        root_three * ux * uz,
        0.5 * root_three * (ux * ux - uy * uy),
    ]


class Sizes:
    def __init__(self, cols_x, cols_y, slots, neigh, channels, basis, hidden):
        self.cols_x, self.cols_y = cols_x, cols_y
        self.slots, self.neigh, self.channels = slots, neigh, channels
        self.basis, self.hidden = basis, hidden
        self.inner_x, self.inner_y = cols_x + 2, cols_y + 2
        self.outer_y = cols_y + 4
        self.inner = self.inner_x * self.inner_y
        self.edges = slots * neigh
        self.window = 9 * slots

        cells = [(a, b) for a in range(self.inner_x) for b in range(self.inner_y)]
        self.own = [c for c in cells if self.is_own(*c)]
        self.halo = [c for c in cells if not self.is_own(*c)]
        self.order = self.own + self.halo

    def is_own(self, a, b):
        return 1 <= a <= self.cols_x and 1 <= b <= self.cols_y

    def outer_row(self, a, b):
        return (a * self.outer_y + b) * self.slots

    def inner_row(self, a, b):
        return (a * self.inner_y + b) * self.slots


def each(compute):
    return lambda items: [compute(item) for item in items]


def loop(count, group, compute, store):
    for first in range(0, count, group):
        items = list(range(first, min(first + group, count)))
        for item, value in zip(items, compute(items)):
            store(item, value)


def window_of(sz, table, a, b):
    run = 3 * sz.slots
    return jnp.concatenate(
        [table[pl.ds(sz.outer_row(a + d, b), run), :] for d in range(3)], axis=0
    )


def gather_columns(sz, table, mask, mask_bf, code, sep, hot, xt):
    lane = lax.broadcasted_iota(jnp.int32, (sz.channels, sz.edges), 1)
    row = lax.broadcasted_iota(jnp.int32, (sz.channels, sz.edges), 0)
    spread = (row == code_lane + lane % sz.neigh).astype(bf16)
    target = lax.broadcasted_iota(jnp.int32, (sz.window, sz.edges), 0)
    ch = sz.channels

    def one(col):
        a, b = sz.order[col]
        meta = table[pl.ds(sz.outer_row(a + 1, b + 1), sz.slots), ch : 2 * ch]
        codes = jnp.sum(mm(meta, spread) * mask, axis=0, keepdims=True).astype(jnp.int32)
        one_hot = (target == codes).astype(f32).astype(bf16)
        own = mm(meta.astype(f32).T[:24].astype(bf16), mask_bf)
        window = window_of(sz, table, a, b)
        turned = window.astype(f32).T.astype(bf16)[: ch + 32]
        found = mm(turned, one_hot)
        diff = found[ch : ch + 24] - own
        return codes, one_hot, found[:ch], diff[0:8] + diff[8:16] + diff[16:24]

    def store(col, value):
        code[pl.ds(col, 1), :], one_hot, found, total = value
        if col < len(sz.own):
            hot[col] = one_hot
        xt[col] = found
        for d in range(3):
            sep[d, pl.ds(col, 1), :] = total[d : d + 1]

    loop(sz.inner, 4, each(one), store)


def shifted_seps(code, sep):
    offset = code[...] >> 4
    step_x = (offset * 11) >> 5
    step_y = offset - 3 * step_x
    sep[0] = sep[0] + column * (step_x - 1).astype(f32)
    sep[1] = sep[1] + column * (step_y - 1).astype(f32)


def geometry(live, seps, angular, dist, env):
    sep_x, sep_y, sep_z = seps
    dist_sq = sep_x * sep_x + sep_y * sep_y + sep_z * sep_z
    dist[...] = jnp.sqrt(dist_sq + softening)
    env[...] = jnp.square(jnp.maximum(1.0 - dist_sq / (cutoff * cutoff), 0.0)) * live
    rows = harmonic_rows(sep_x / cutoff, sep_y / cutoff, sep_z / cutoff)
    for m, value in enumerate(rows):
        angular[m] = value


def live_rows(code):
    return (code != dead_code).astype(f32)


def basis_rows(sz, dist_row):
    width = dist_row.shape[1]
    spacing = cutoff / (sz.basis - 1)
    centre = lax.broadcasted_iota(jnp.int32, (sz.basis, width), 0).astype(f32) * spacing
    shifted = (dist_row - centre) * (1.0 / spacing)
    return jnp.exp(-shifted * shifted), shifted


def sigmoid(x):
    return 0.5 * jnp.tanh(0.5 * x) + 0.5


def hidden_rows(sz, dist_row, env_row, weight_in):
    basis, _ = basis_rows(sz, dist_row)
    high = basis.astype(bf16).astype(f32)
    stacked = jnp.concatenate([high, basis - high, high, jnp.zeros_like(high)], axis=0)
    pre = mm(weight_in, stacked.astype(bf16))
    gate = sigmoid(pre)
    value = pre * gate
    weighted = value * env_row
    high, low = split(weighted)
    slope = gate * (1.0 + pre * (1.0 - gate)) * env_row
    return jnp.concatenate([high, low, high], axis=0), value, slope


def half_rows(sz, angular, col, half, first):
    edges = sz.edges // 2
    mask = atom_mask(sz.slots // 2, edges, sz.neigh)
    span = slice(half * edges, (half + 1) * edges)
    return [angular[m, pl.ds(col, 1), span] * mask for m in range(first, 9)]


def layer_forward(sz, cols, angular, dist, env, mask_bf, weight_in, weight_out, inputs):
    rows = [jnp.concatenate([ref[pl.ds(c, 1), :] for c in cols], axis=1) for ref in (dist, env)]
    weighted, value, slope = hidden_rows(sz, *rows, weight_in)
    out = []
    for k, (col, xt) in enumerate(zip(cols, inputs)):
        span = slice(k * sz.edges, (k + 1) * sz.edges)
        radial = mm(weight_out, weighted[:, span])
        parts = column_messages(sz, col, angular, mask_bf, radial, xt)
        kept = (weighted[: 2 * sz.hidden, span], value[:, span], slope[:, span])
        out.append((radial, kept, parts))
    return out


def column_messages(sz, col, angular, mask_bf, radial, xt):
    ch, edges = sz.channels, sz.edges // 2
    product = [(radial[l * ch : (l + 1) * ch] * xt).astype(bf16) for l in range(3)]
    scalar = nt(product[0], mask_bf).T
    count = 4 * sz.slots
    lane = lax.broadcasted_iota(jnp.int32, (ch, 2 * count), 1)
    vector_lane = lax.rem(lane, count) < 3 * sz.slots // 2
    out = [scalar]
    for half in range(2):
        span = slice(half * edges, (half + 1) * edges)
        blocks = jnp.concatenate(half_rows(sz, angular, col, half, 1), axis=0)
        high = blocks.astype(bf16).astype(f32)
        both = jnp.concatenate([high, blocks - high], axis=0).astype(bf16)
        got = jnp.where(vector_lane, nt(product[1][:, span], both), nt(product[2][:, span], both)).T
        out.append(got[:count] + got[count:])
    return out


def half_messages(sz, message, half):
    n = sz.slots // 2
    first = sz.slots + half * 8 * n
    return [message[first + m * n : first + (m + 1) * n] for m in range(8)]


def invariants(sz, parts):
    n = sz.slots // 2
    rows = []
    for half in range(2):
        squares = parts[1 + half] * parts[1 + half]
        got = [squares[m * n : (m + 1) * n] for m in range(8)]
        rows.append(
            jnp.concatenate(
                [
                    parts[0][half * n : (half + 1) * n],
                    got[0] + got[1] + got[2],
                    got[3] + got[4] + got[5] + got[6] + got[7],
                ],
                axis=1,
            )
        )
    return jnp.concatenate(rows, axis=0)


def radial_products(sz, product_grad, radial, xt):
    ch = sz.channels
    products, mine, input_grad = [], [], None
    for l in range(3):
        grad, part = product_grad[l * ch : (l + 1) * ch], radial[l * ch : (l + 1) * ch]
        if l:
            products.append((part * xt).astype(bf16))
        mine.append((grad * xt).astype(bf16))
        term = grad * part
        input_grad = term if input_grad is None else input_grad + term
    return products, jnp.concatenate(mine, axis=0), input_grad.astype(bf16)


def radial_backward(sz, dist_row, radial_grad, value, slope, back_in, back_out):
    weighted_grad = mm(back_out, radial_grad)
    env_row_grad = jnp.sum(weighted_grad * value, axis=0, keepdims=True)
    both = mm(back_in, (weighted_grad * slope).astype(bf16))
    basis_grad = both[: sz.basis] + both[sz.basis : 2 * sz.basis]
    basis, shifted = basis_rows(sz, dist_row)
    spacing = cutoff / (sz.basis - 1)
    dist_row_grad = jnp.sum(
        basis_grad * basis * shifted * (-2.0 / spacing), axis=0, keepdims=True
    )
    return dist_row_grad, env_row_grad


def layer_backward(
    sz, col, angular, dist, back_in, back_out, radial, value, slope, xt, one_hot,
    message, cotangent,
):
    ch, n, edges = sz.channels, sz.slots // 2, sz.edges // 2
    mask = atom_mask(n, edges, sz.neigh)
    input_grads, radial_grads, ang_grads = [], [], []
    for half in range(2):
        span = slice(half * edges, (half + 1) * edges)
        blocks = jnp.concatenate(half_rows(sz, angular, col, half, 0), axis=0).astype(bf16)
        cot = cotangent[half * n : (half + 1) * n]
        twice = 2.0 * cot[:, ch:]
        got = half_messages(sz, message, half)
        grads = [got[m] * (twice[:, :ch] if m < 3 else twice[:, ch:]) for m in range(8)]
        filler = jnp.zeros((ch - 9 * n, ch), f32)
        turned = jnp.concatenate([cot[:, :ch]] + grads + [filler], axis=0).T[:, : 9 * n]
        lane = lax.broadcasted_iota(jnp.int32, turned.shape, 1)
        lhs = jnp.concatenate(
            [
                jnp.where(lane < n, turned, 0.0),
                jnp.where((lane >= n) & (lane < 4 * n), turned, 0.0),
                jnp.where(lane >= 4 * n, turned, 0.0),
            ],
            axis=0,
        ).astype(bf16)
        product_grad = mm(lhs, blocks)
        products, mine, input_grad = radial_products(
            sz, product_grad, radial[:, span], xt[:, span]
        )
        input_grads.append(input_grad)
        radial_grads.append(mine)
        empty = jnp.zeros((n, ch), f32)
        wide = [
            jnp.concatenate([g, empty] if m < 3 else [empty, g], axis=1)
            for m, g in enumerate(grads)
        ]
        got = mm(jnp.concatenate(wide, axis=0).astype(bf16), jnp.concatenate(products, axis=0))
        ang_grads.append(
            [
                jnp.sum(got[m * n : (m + 1) * n] * mask, axis=0, keepdims=True)
                for m in range(8)
            ]
        )
    dist_row_grad, env_row_grad = radial_backward(
        sz, dist[pl.ds(col, 1), :], jnp.concatenate(radial_grads, axis=1),
        value, slope, back_in, back_out,
    )
    got = nt(one_hot, jnp.concatenate(input_grads, axis=1))
    return got, ang_grads, dist_row_grad, env_row_grad


def store_grads(sz, col, value, ang_grad, dist_grad, env_grad):
    got, ang_grads, dist_row_grad, env_row_grad = value
    edges = sz.edges // 2
    for half in range(2):
        for m in range(8):
            ang_grad[m + 1, pl.ds(col, 1), half * edges : (half + 1) * edges] = ang_grads[half][m]
    dist_grad[pl.ds(col, 1), :] = dist_row_grad
    env_grad[pl.ds(col, 1), :] = env_row_grad
    return got


def separation_grads(live, sep, dist, ang_grad, dist_grad, env_grad):
    sep_x, sep_y, sep_z = sep
    ux, uy, uz = sep_x / cutoff, sep_y / cutoff, sep_z / cutoff
    dist_sq = sep_x * sep_x + sep_y * sep_y + sep_z * sep_z
    inside = jnp.maximum(1.0 - dist_sq / (cutoff * cutoff), 0.0)
    sq_grad = dist_grad * (0.5 / dist) - env_grad * live * inside * (2.0 / (cutoff * cutoff))
    g = ang_grad
    r3 = root_three
    grad_x = g[1] + r3 * (uy * g[4] + uz * g[7] + ux * g[8]) - ux * g[6]
    grad_y = g[2] + r3 * (ux * g[4] + uz * g[5] - uy * g[8]) - uy * g[6]
    grad_z = g[3] + r3 * (uy * g[5] + ux * g[7]) + 2.0 * uz * g[6]
    return (
        2.0 * sep_x * sq_grad + grad_x / cutoff,
        2.0 * sep_y * sq_grad + grad_y / cutoff,
        2.0 * sep_z * sq_grad + grad_z / cutoff,
    )


def stacked_seps(rows):
    full = jnp.concatenate(rows + [jnp.zeros((5, rows[0].shape[1]), f32)], axis=0)
    high = full.astype(bf16).astype(f32)
    return jnp.concatenate([high, full - high], axis=0).astype(bf16)


def own_positions(
    sz, mask_bf, code, sep, dist, hot, ang_grad, dist_grad, env_grad, sep_grad, acc_pos
):
    owned, run = len(sz.own), 3 * sz.slots
    grads = separation_grads(
        live_rows(code[:owned]),
        [sep[d, :owned] for d in range(3)],
        dist[:owned],
        ang_grad,
        dist_grad[...],
        env_grad[...],
    )
    for d in range(3):
        sep_grad[d] = grads[d]
    for k, (a, b) in enumerate(sz.own):
        rows = [sep_grad[d, pl.ds(k, 1), :] for d in range(3)]
        got = nt(signed_hot(sz, hot[k], mask_bf), stacked_seps(rows))
        got = got[:, :8] + got[:, 8:]
        for d in range(3):
            acc_pos[pl.ds(sz.inner_row(a - 1 + d, b - 1), run), :] += got[d * run : (d + 1) * run]


def signed_hot(sz, one_hot, mask_bf):
    first = 4 * sz.slots
    return jnp.concatenate(
        [one_hot[:first], one_hot[first : first + sz.slots] - mask_bf, one_hot[first + sz.slots :]],
        axis=0,
    )


def fetch(sources, targets, sems):
    copies = [
        pltpu.make_async_copy(source, target, sems.at[k])
        for k, (source, target) in enumerate(zip(sources, targets))
    ]
    for copy in copies:
        copy.start()
    return copies


def block_kernel(sz, kinds, *refs):
    sources, block, held, sems = refs[:6], refs[6], refs[7:13], refs[13]
    for copy in fetch(sources, held, sems):
        copy.wait()
    features, positions, species, neighbours, counts, species_gain = held
    ch, n = sz.channels, sz.slots
    gains = species_gain[...]
    gain_high = gains.astype(bf16).astype(f32)
    rest = gains - gain_high
    gain_middle = rest.astype(bf16).astype(f32)
    parts = [gain_high, gain_middle, rest - gain_middle]
    above, below = jnp.zeros((24, ch), f32), jnp.zeros((8 - kinds, ch), f32)
    parts = [jnp.concatenate([above, part, below], axis=0).astype(bf16) for part in parts]
    kind = lax.broadcasted_iota(jnp.int32, (8, n), 0)
    neigh_lane = lax.broadcasted_iota(jnp.int32, (n, sz.neigh), 1)
    lane = lax.broadcasted_iota(jnp.int32, (n, code_lane), 1)
    gap = jnp.zeros((5, n), f32)
    for a in range(sz.cols_x):
        for b in range(sz.cols_y):
            atoms = positions[a, :, b, :]
            high = atoms.astype(bf16).astype(f32)
            rest = atoms - high
            middle = rest.astype(bf16).astype(f32)
            count = counts[a, pl.ds(b, 1), :]
            chosen = (kind == species[a, pl.ds(b, 1), :]).astype(f32)
            last = jnp.where(kind == 7, count.astype(f32), chosen)
            rows = [high, gap, middle, gap, rest - middle, gap, last]
            turned = jnp.concatenate(rows, axis=0).T
            picked = jnp.where((lane >= 24) & (lane < 24 + kinds), turned, 0.0).astype(bf16)
            gain = mm(picked, parts[0]) + mm(picked, parts[1]) + mm(picked, parts[2])
            live = neigh_lane.astype(f32) < turned[:, 31:32]
            codes = jnp.where(live, neighbours[a, b], dead_code).astype(f32)
            place = jnp.where(lane < 24, turned, 0.0)
            filler = jnp.zeros((n, ch - code_lane - sz.neigh), f32)
            block[a, b, :, :ch] = (features[a, b].astype(f32) * gain).astype(bf16)
            block[a, b, :, ch:] = jnp.concatenate([place, codes, filler], axis=1).astype(bf16)


def first_kernel(
    sz, table, wide_in, wide_out, turned_in, turned_out, mixing, readout,
    energy, back, kept, code, sep,
    hot, xt, angular, dist, env, inv, second, second_xt, second_msg, second_radial,
    second_value, second_slope, ang_grad, dist_grad, env_grad, sep_grad, acc, acc_pos,
):
    ch, n = sz.channels, sz.slots
    run = 3 * n
    owned = len(sz.own)
    mask = atom_mask(n, sz.edges, sz.neigh)
    mask_bf = mask.astype(bf16)
    gather_columns(sz, table, mask, mask_bf, code, sep, hot, xt)
    shifted_seps(code, sep)
    geometry(live_rows(code[...]), (sep[0], sep[1], sep[2]), angular, dist, env)
    in_one, out_one = wide_in[0], wide_out[0]

    def one(cols):
        inputs = [xt[col] for col in cols]
        return layer_forward(sz, cols, angular, dist, env, mask_bf, in_one, out_one, inputs)

    def one_store(col, got):
        _, _, parts = got
        kept[col] = jnp.concatenate(parts, axis=0)
        inv[sz.inner_row(*sz.order[col]) : sz.inner_row(*sz.order[col]) + n, :] = invariants(
            sz, parts
        )

    loop(sz.inner, 4, one, one_store)
    own_rows = [
        table[(a * sz.outer_y + 1) * n : (a * sz.outer_y + 1 + sz.inner_y) * n, :ch]
        for a in range(1, 1 + sz.inner_x)
    ]
    first_out = three(mm, inv[...], mixing[0]) + jnp.concatenate(own_rows, axis=0).astype(f32)
    second[...] = first_out.astype(bf16)

    in_two, out_two = wide_in[1], wide_out[1]
    back_in, back_out = turned_in[1], turned_out[1]

    def second_input(k):
        a, b = sz.own[k]
        window = jnp.concatenate(
            [second[pl.ds(sz.inner_row(a - 1 + d, b - 1), run), :] for d in range(3)], axis=0
        )
        return mm(window.astype(f32).T.astype(bf16), hot[k])

    def two(items):
        inputs = [second_input(k) for k in items]
        got = layer_forward(sz, items, angular, dist, env, mask_bf, in_two, out_two, inputs)
        return list(zip(inputs, got))

    def two_store(k, got):
        second_xt[k], (second_radial[k], hidden, parts) = got
        _, second_value[k], second_slope[k] = hidden
        second_msg[k] = jnp.concatenate(parts, axis=0)
        inv[k * n : (k + 1) * n, :] = invariants(sz, parts)

    loop(owned, 4, two, two_store)
    own_rows = [
        second[(a * sz.inner_y + 1) * n : (a * sz.inner_y + 1 + sz.cols_y) * n, :]
        for a in range(1, 1 + sz.cols_x)
    ]
    out = three(mm, inv[: owned * n], mixing[1]) + jnp.concatenate(own_rows, axis=0).astype(f32)
    gate = sigmoid(out)
    weights = readout[...]
    total = three(nt, jnp.ones((8, ch), f32), out * gate * weights)
    for k, (a, b) in enumerate(sz.own):
        energy[a - 1, b - 1 : b, :] = total[0:1, k * n : (k + 1) * n]
    out_grad = gate * (1.0 + out * (1.0 - gate)) * weights
    inv[: owned * n] = three(nt, out_grad, mixing[1])
    acc[...] = jnp.zeros_like(acc)
    acc_pos[...] = jnp.zeros_like(acc_pos)
    for a in range(sz.cols_x):
        first = ((a + 1) * sz.inner_y + 1) * n
        acc[first : first + sz.cols_y * n] = out_grad[a * sz.cols_y * n : (a + 1) * sz.cols_y * n]

    def two_back(k):
        return layer_backward(
            sz, k, angular, dist, back_in, back_out,
            second_radial[k], second_value[k], second_slope[k], second_xt[k], hot[k],
            second_msg[k], inv[k * n : (k + 1) * n, :],
        )

    def two_back_store(k, value):
        a, b = sz.own[k]
        got = store_grads(sz, k, value, ang_grad, dist_grad, env_grad)
        for d in range(3):
            acc[pl.ds(sz.inner_row(a - 1 + d, b - 1), run), :] += got[d * run : (d + 1) * run]

    loop(owned, 4, each(two_back), two_back_store)
    own_positions(
        sz, mask_bf, code, sep, dist, hot, ang_grad, dist_grad, env_grad, sep_grad, acc_pos
    )
    back[:, :ch] = acc[...].astype(bf16)
    high = acc_pos[...].astype(bf16)
    low = (acc_pos[...] - high.astype(f32)).astype(f32)
    filler = jnp.zeros((acc_pos.shape[0], ch - 16), f32)
    back[:, ch:] = jnp.concatenate([high.astype(f32), low, filler], axis=1).astype(bf16)


def packed_halo(sz, code):
    rows = len(sz.halo)
    first = len(sz.own)
    codes = code[first:]
    row = lax.broadcasted_iota(jnp.int32, (rows, sz.edges), 0)
    at_x, at_y = jnp.zeros_like(row), jnp.zeros_like(row)
    for h, (a, b) in enumerate(sz.halo):
        at_x, at_y = jnp.where(row == h, a, at_x), jnp.where(row == h, b, at_y)
    offset = codes >> 4
    step_x = (offset * 11) >> 5
    to_x = at_x + step_x - 2
    to_y = at_y + offset - 3 * step_x - 2
    inside = (to_x >= 0) & (to_x < sz.cols_x) & (to_y >= 0) & (to_y < sz.cols_y)
    inside = inside & (codes != dead_code)
    target = (to_x * sz.cols_y + to_y) * sz.slots + (codes & 15)
    target = jnp.where(inside, target, 0).astype(f32)
    lower = lax.broadcasted_iota(jnp.int32, (sz.edges, sz.edges), 0)
    upper = lax.broadcasted_iota(jnp.int32, (sz.edges, sz.edges), 1)
    running = mm(inside.astype(f32).astype(bf16), (lower <= upper).astype(f32).astype(bf16))
    place = jnp.where(inside, running - 1.0, -1.0)
    most = jnp.max(running).astype(jnp.int32)
    return target, place, (most + halo_lanes - 1) // halo_lanes


def halo_back(
    sz, part, table, cotangent, kept, sep, inv, weights,
    target, place, held, feature_acc, pos_acc,
):
    in_one, out_one, back_in, back_out = weights
    csep, ctarget, catom, cvalid, angular, dist, env, ang_grad, dist_grad, env_grad = held
    ch, n, lanes = sz.channels, sz.slots, halo_lanes
    first = len(sz.own)
    slot = lax.broadcasted_iota(jnp.int32, (lanes, sz.edges), 0).astype(f32)
    atom = (lax.broadcasted_iota(jnp.int32, (1, sz.edges), 1) // sz.neigh).astype(f32)
    ones = jnp.ones((1, sz.edges), f32)
    zeros = jnp.zeros((2, sz.edges), f32)
    wanted = slot + (part * lanes).astype(f32)
    for h in range(len(sz.halo)):
        pick = (place[h : h + 1] == wanted).astype(f32).astype(bf16)
        rows = jnp.concatenate(
            [sep[d, pl.ds(first + h, 1), :] for d in range(3)]
            + [target[h : h + 1], atom, ones, zeros],
            axis=0,
        )
        high = rows.astype(bf16).astype(f32)
        middle = (rows - high).astype(bf16).astype(f32)
        three_parts = jnp.concatenate([high, middle, rows - high - middle], axis=0).astype(bf16)
        got = nt(three_parts, pick)
        got = got[0:8] + got[8:16] + got[16:24]
        for d in range(3):
            csep[d, pl.ds(h, 1), :] = got[d : d + 1]
        ctarget[pl.ds(h, 1), :] = got[3:4]
        catom[pl.ds(h, 1), :] = got[4:5]
        cvalid[pl.ds(h, 1), :] = got[5:6]
    sep_x, sep_y, sep_z = csep[0], csep[1], csep[2]
    geometry(cvalid[...], (sep_x, sep_y, sep_z), angular, dist, env)
    own_rows = [
        table[sz.outer_row(a + 2, 2) : sz.outer_row(a + 2, 2) + sz.cols_y * n, :ch]
        for a in range(sz.cols_x)
    ]
    own_turned = jnp.concatenate(own_rows, axis=0).astype(f32).T.astype(bf16)
    own_index = lax.broadcasted_iota(jnp.int32, (len(sz.own) * n, 4 * lanes), 0).astype(f32)
    atom_index = lax.broadcasted_iota(jnp.int32, (n, lanes), 0).astype(f32)
    half = n // 2
    groups = [range(g, min(g + 4, len(sz.halo))) for g in range(0, len(sz.halo), 4)]

    def wide(ref, group):
        return jnp.concatenate([ref[pl.ds(h, 1), :] for h in group], axis=1)

    def one_hot_of(group):
        width = len(group) * lanes
        chosen = own_index[:, :width] == wide(ctarget, group)
        return jnp.where(chosen, wide(cvalid, group), 0.0).astype(bf16)

    results = []
    for group in groups:
        dist_row = wide(dist, group)
        weighted, value, slope = hidden_rows(sz, dist_row, wide(env, group), in_one)
        radial = mm(out_one, weighted)
        one_hot = one_hot_of(group)
        xt = mm(own_turned, one_hot)
        atoms, grads_of, product_grads = [], [], []
        for h in group:
            a, b = sz.halo[h]
            at = jnp.where(atom_index == catom[pl.ds(h, 1), :], cvalid[pl.ds(h, 1), :], 0.0)
            atoms.append(at)
            blocks = [at]
            rows = inv[sz.inner_row(a, b) : sz.inner_row(a, b) + n]
            message = kept[first + h]
            grads = []
            for side in range(2):
                mine = at[side * half : (side + 1) * half]
                cot = 2.0 * rows[side * half : (side + 1) * half, ch:]
                msgs = half_messages(sz, message, side)
                for m in range(8):
                    blocks.append(angular[m + 1, pl.ds(h, 1), :] * mine)
                    grads.append(msgs[m] * (cot[:, :ch] if m < 3 else cot[:, ch:]))
            blocks = jnp.concatenate(blocks, axis=0).astype(bf16)
            grads_of.append(grads)
            turned = jnp.concatenate([rows[:, :ch]] + grads, axis=0).T
            lane = lax.broadcasted_iota(jnp.int32, turned.shape, 1)
            vector = lax.rem(lane - n, 8 * half) < 3 * half
            lhs = jnp.concatenate(
                [
                    jnp.where(lane < n, turned, 0.0),
                    jnp.where((lane >= n) & vector, turned, 0.0),
                    jnp.where((lane >= n) & ~vector, turned, 0.0),
                ],
                axis=0,
            ).astype(bf16)
            product_grads.append(mm(lhs, blocks))
        product_grad = jnp.concatenate(product_grads, axis=1)
        products, mine, input_grad = radial_products(sz, product_grad, radial, xt)
        for k, h in enumerate(group):
            empty = jnp.zeros((half, ch), f32)
            rows = [
                jnp.concatenate([g, empty] if m % 8 < 3 else [empty, g], axis=1)
                for m, g in enumerate(grads_of[k])
            ]
            span = slice(k * lanes, (k + 1) * lanes)
            got = mm(
                jnp.concatenate(rows, axis=0).astype(bf16),
                jnp.concatenate([p[:, span] for p in products], axis=0),
            )
            for m in range(8):
                low = got[m * half : (m + 1) * half] * atoms[k][:half]
                high = got[(8 + m) * half : (9 + m) * half] * atoms[k][half:]
                ang_grad[m + 1, pl.ds(h, 1), :] = jnp.sum(low + high, axis=0, keepdims=True)
        dist_row_grad, env_row_grad = radial_backward(
            sz, dist_row, mine, value, slope, back_in, back_out
        )
        for k, h in enumerate(group):
            span = slice(k * lanes, (k + 1) * lanes)
            dist_grad[pl.ds(h, 1), :] = dist_row_grad[:, span]
            env_grad[pl.ds(h, 1), :] = env_row_grad[:, span]
        results.append(nt(one_hot, input_grad))
    for got in results:
        feature_acc[...] += got
    grads = separation_grads(
        cvalid[...], (sep_x, sep_y, sep_z), dist[...], ang_grad, dist_grad[...], env_grad[...]
    )
    for group in groups:
        rows = [
            jnp.concatenate([grad[h : h + 1] for h in group], axis=1) for grad in grads
        ]
        got = nt(one_hot_of(group), stacked_seps(rows))
        pos_acc[...] += got[:, :8] + got[:, 8:]


def second_kernel(
    sz, cotangent, table, kept, code, sep, wide_in, wide_out, turned_in, turned_out, mixing,
    feature_grad, forces,
    hot, xt, angular, dist, env, inv, ang_grad, dist_grad, env_grad, sep_grad,
    acc, acc_pos, halo_acc, halo_pos, *held,
):
    ch, n = sz.channels, sz.slots
    run = 3 * n
    mask_bf = atom_mask(n, sz.edges, sz.neigh).astype(bf16)
    inv[...] = three(nt, cotangent[:, :ch], mixing[0])
    target, place, parts = packed_halo(sz, code)
    in_one, out_one = wide_in[0], wide_out[0]
    back_in, back_out = turned_in[0], turned_out[0]
    owned = len(sz.own)
    seps = [sep[d, :owned] for d in range(3)]
    geometry(live_rows(code[:owned]), seps, angular, dist, env)
    index = lax.broadcasted_iota(jnp.int32, (sz.window, sz.edges), 0)

    def one_gather(k):
        window = window_of(sz, table, *sz.own[k])
        one_hot = (index == code[pl.ds(k, 1), :]).astype(f32).astype(bf16)
        return one_hot, mm(window[:, :ch].astype(f32).T.astype(bf16), one_hot)

    def one_gather_store(k, value):
        hot[k], xt[k] = value

    loop(owned, 4, each(one_gather), one_gather_store)
    acc[...] = jnp.zeros_like(acc)
    acc_pos[...] = jnp.zeros_like(acc_pos)
    halo_acc[...] = jnp.zeros_like(halo_acc)
    halo_pos[...] = jnp.zeros_like(halo_pos)

    def one_back(items):
        rows = [jnp.concatenate([ref[pl.ds(k, 1), :] for k in items], axis=1) for ref in (dist, env)]
        weighted, value, slope = hidden_rows(sz, *rows, in_one)
        out = []
        for k in items:
            span = slice((k - items[0]) * sz.edges, (k - items[0] + 1) * sz.edges)
            row = sz.inner_row(*sz.own[k])
            out.append(
                layer_backward(
                    sz, k, angular, dist, back_in, back_out,
                    mm(out_one, weighted[:, span]), value[:, span], slope[:, span],
                    xt[k], hot[k], kept[k], inv[row : row + n, :],
                )
            )
        return out

    def one_back_store(k, value):
        a, b = sz.own[k]
        got = store_grads(sz, k, value, ang_grad, dist_grad, env_grad)
        for d in range(3):
            acc[pl.ds(sz.inner_row(a - 1 + d, b - 1), run), :] += got[d * run : (d + 1) * run]

    loop(owned, 4, one_back, one_back_store)
    own_positions(
        sz, mask_bf, code, sep, dist, hot, ang_grad, dist_grad, env_grad, sep_grad, acc_pos
    )
    weights = (in_one, out_one, back_in, back_out)

    def halo_part(part, carry):
        halo_back(
            sz, part, table, cotangent, kept, sep, inv, weights,
            target, place, held, halo_acc, halo_pos,
        )
        return carry

    lax.fori_loop(0, parts, halo_part, 0)
    for a in range(sz.cols_x):
        inner = sz.inner_row(a + 1, 1)
        rows = sz.cols_y * n
        mine = slice(a * rows, (a + 1) * rows)
        feature_grad[mine] = (
            acc[inner : inner + rows] + cotangent[inner : inner + rows, :ch] + halo_acc[mine]
        )
        extra = cotangent[inner : inner + rows, ch : ch + 16]
        total = acc_pos[inner : inner + rows] + extra[:, :8] + extra[:, 8:] + halo_pos[mine]
        for b in range(sz.cols_y):
            forces[a, :, b, :] = -(total[b * n : (b + 1) * n].T)[:3]


def ring(axis):
    devices = lax.axis_size(axis)
    up = [(i, (i + 1) % devices) for i in range(devices)]
    return up, [(j, i) for i, j in up]


def extended(x, sides):
    for axis, dim in sides:
        up, down = ring(axis)
        length = x.shape[dim]
        last = lax.slice_in_dim(x, length - 2, length, axis=dim)
        initial = lax.slice_in_dim(x, 0, 2, axis=dim)
        before = lax.ppermute(last, axis, up)
        after = lax.ppermute(initial, axis, down)
        x = jnp.concatenate([before, x, after], axis=dim)
    return x


def summed(x, sides):
    total = x.astype(f32)
    for axis, dim in sides:
        up, down = ring(axis)
        length = x.shape[dim]
        sent = total.astype(bf16)
        last = lax.slice_in_dim(sent, length - 2, length, axis=dim)
        initial = lax.slice_in_dim(sent, 0, 2, axis=dim)
        before = lax.ppermute(last, axis, up).astype(f32)
        after = lax.ppermute(initial, axis, down).astype(f32)
        shape = list(x.shape)
        shape[dim] = length - 4
        parts = [before] + ([jnp.zeros(shape, f32)] if length > 4 else []) + [after]
        total = total + jnp.concatenate(parts, axis=dim)
    return total


def shards(
    features, positions, species, neighbours, counts, species_gain, radial_in, radial_out, mixing, readout
):
    cols_x, cols_y, slots, channels = features.shape
    neigh = neighbours.shape[-1]
    basis, hidden = radial_in.shape[1:]
    sz = Sizes(cols_x, cols_y, slots, neigh, channels, basis, hidden)
    vmem = pl.BlockSpec(memory_space=pltpu.VMEM)
    in_hbm = pl.BlockSpec(memory_space=pltpu.HBM)
    params = pltpu.CompilerParams(vmem_limit_bytes=40 * 1024 * 1024)
    given = (features, positions.transpose(0, 2, 1, 3), species, neighbours, counts, species_gain)
    block = pl.pallas_call(
        functools.partial(block_kernel, sz, species_gain.shape[0]),
        out_shape=jax.ShapeDtypeStruct((cols_x, cols_y, slots, 2 * channels), bf16),
        in_specs=[in_hbm] * 6,
        out_specs=vmem,
        scratch_shapes=[pltpu.VMEM(x.shape, x.dtype) for x in given]
        + [pltpu.SemaphoreType.DMA((6,))],
        compiler_params=pltpu.CompilerParams(vmem_limit_bytes=60 * 1024 * 1024),
        name="block_of_atoms",
    )(*given)
    sides = (("gx", 0), ("gy", 1))
    table = extended(block, sides).reshape(-1, 2 * channels)

    inner_atoms = sz.inner * slots
    owned = cols_x * cols_y
    edges = sz.edges
    columns, hidden_edges = sz.inner, (hidden, edges)
    grads = [
        pltpu.VMEM((9, owned, edges), f32),
        pltpu.VMEM((owned, edges), f32),
        pltpu.VMEM((owned, edges), f32),
        pltpu.VMEM((3, owned, edges), f32),
    ]
    weights = prepared(radial_in, radial_out, mixing)
    kept_shapes = [
        ((columns, sz.window, channels), f32),
        ((columns, edges), jnp.int32),
        ((3, columns, edges), f32),
    ]

    def edge_scratch(count):
        return [
            pltpu.VMEM((owned, sz.window, edges), bf16),
            pltpu.VMEM((count, channels, edges), f32),
            pltpu.VMEM((9, count, edges), f32),
            pltpu.VMEM((count, edges), f32),
            pltpu.VMEM((count, edges), f32),
            pltpu.VMEM((inner_atoms, 3 * channels), f32),
        ]

    energy, back, *kept = pl.pallas_call(
        functools.partial(first_kernel, sz),
        out_shape=[
            jax.ShapeDtypeStruct((cols_x, cols_y, slots), f32),
            jax.ShapeDtypeStruct((inner_atoms, 2 * channels), bf16),
        ]
        + [jax.ShapeDtypeStruct(*item) for item in kept_shapes],
        in_specs=[vmem] * 7,
        out_specs=[vmem] * 5,
        scratch_shapes=edge_scratch(columns)
        + [
            pltpu.VMEM((inner_atoms, channels), bf16),
            pltpu.VMEM((owned, channels, edges), f32),
            pltpu.VMEM((owned, sz.window, channels), f32),
            pltpu.VMEM((owned, 3 * channels, edges), f32),
            pltpu.VMEM((owned,) + hidden_edges, f32),
            pltpu.VMEM((owned,) + hidden_edges, f32),
        ]
        + grads
        + [pltpu.VMEM((inner_atoms, channels), f32), pltpu.VMEM((inner_atoms, 8), f32)],
        compiler_params=params,
        name="forward_and_second_back",
    )(table, *weights, readout.reshape(1, -1))

    back = back.reshape(sz.inner_x, sz.inner_y, slots, 2 * channels)
    cotangent = summed(back, sides).reshape(inner_atoms, 2 * channels)
    feature_grad, forces = pl.pallas_call(
        functools.partial(second_kernel, sz),
        out_shape=(
            jax.ShapeDtypeStruct((owned * slots, channels), f32),
            jax.ShapeDtypeStruct((cols_x, 3, cols_y, slots), f32),
        ),
        in_specs=[vmem] * 10,
        out_specs=(vmem,) * 2,
        scratch_shapes=edge_scratch(owned)
        + grads
        + [
            pltpu.VMEM((rows, width), f32)
            for rows in (inner_atoms, owned * slots)
            for width in (channels, 8)
        ]
        + [
            pltpu.VMEM(shape + (len(sz.halo), halo_lanes), f32)
            for shape in ((3,), (), (), (), (9,), (), (), (9,), (), ())
        ],
        compiler_params=params,
        name="first_back",
    )(cotangent, table, *kept, *weights)
    return (
        energy,
        forces.transpose(0, 2, 1, 3),
        feature_grad.reshape(cols_x, cols_y, slots, channels),
    )


def solution(mesh):
    placed = (
        P("gx", "gy", None, None),
        P("gx", "gy", None, None),
        P("gx", "gy", None),
        P("gx", "gy", None, None),
        P("gx", "gy", None),
        P(),
        P(),
        P(),
        P(),
        P(),
    )
    return jax.shard_map(
        shards,
        mesh=mesh,
        in_specs=placed,
        out_specs=(P("gx", "gy", None), P("gx", "gy", None, None), P("gx", "gy", None, None)),
        check_vma=False,
    )
```

```python
import functools

import jax
import jax.numpy as jnp
from jax import lax
from jax.experimental import pallas as pl
from jax.experimental.pallas import tpu as pltpu
from jax.sharding import PartitionSpec as P

column = 6.0
cutoff = 6.0
softening = 0.01
root_three = 3.0**0.5
f32 = jnp.float32
bf16 = jnp.bfloat16
code_lane = 32
part_lanes = 256


def mm(a, b):
    return lax.dot_general(a, b, (((1,), (0,)), ((), ())), preferred_element_type=f32)


def nt(a, b):
    return lax.dot_general(a, b, (((1,), (1,)), ((), ())), preferred_element_type=f32)


def split(x):
    high = x.astype(bf16)
    return high, (x - high.astype(f32)).astype(bf16)


def three(product, a, b):
    a_high, a_low = split(a)
    b_high, b_low = split(b) if b.dtype == f32 else (b[0], b[1])
    return product(a_high, b_high) + product(a_low, b_high) + product(a_high, b_low)


def parted(x):
    high = lax.reduce_precision(x, 8, 7)
    return high, x - high


def prepared(radial_in, radial_out, mixing):
    high, low = parted(radial_in)
    turned = jnp.concatenate([high, high, low, jnp.zeros_like(high)], axis=1).swapaxes(1, 2)
    back_in = jnp.concatenate([high, low], axis=1)
    high, low = parted(radial_out)
    wide = jnp.concatenate([high, high, low], axis=1).swapaxes(1, 2)
    high_mix, low_mix = parted(mixing)
    mix = jnp.stack([high_mix, low_mix], axis=1)
    return [x.astype(bf16) for x in (turned, wide, back_in, high, mix)]


def harmonic_rows(ux, uy, uz):
    square = ux * ux + uy * uy + uz * uz
    return [
        jnp.ones_like(ux),
        ux,
        uy,
        uz,
        root_three * ux * uy,
        root_three * uy * uz,
        0.5 * (3.0 * uz * uz - square),
        root_three * ux * uz,
        0.5 * root_three * (ux * ux - uy * uy),
    ]


class Sizes:
    def __init__(self, cols_x, cols_y, slots, neigh, channels, basis, hidden):
        self.cols_x, self.cols_y = cols_x, cols_y
        self.slots, self.neigh, self.channels = slots, neigh, channels
        self.basis, self.hidden = basis, hidden
        self.inner_x, self.inner_y = cols_x + 2, cols_y + 2
        self.outer_y = cols_y + 4
        self.inner = self.inner_x * self.inner_y
        self.edges = part_lanes
        self.window = 9 * slots

        cells = [(a, b) for a in range(self.inner_x) for b in range(self.inner_y)]
        self.own = [c for c in cells if self.is_own(*c)]
        self.halo = [c for c in cells if not self.is_own(*c)]
        self.order = self.own + self.halo

    def is_own(self, a, b):
        return 1 <= a <= self.cols_x and 1 <= b <= self.cols_y

    def outer_row(self, a, b):
        return (a * self.outer_y + b) * self.slots

    def inner_row(self, a, b):
        return (a * self.inner_y + b) * self.slots


def each(compute):
    return lambda items: [compute(item) for item in items]


def loop(count, group, compute, store):
    for first in range(0, count, group):
        items = list(range(first, min(first + group, count)))
        for item, value in zip(items, compute(items)):
            store(item, value)


def window_of(sz, table, a, b):
    run = 3 * sz.slots
    return jnp.concatenate(
        [table[pl.ds(sz.outer_row(a + d, b), run), :] for d in range(3)], axis=0
    )


def iota(shape, dim):
    return lax.broadcasted_iota(jnp.int32, shape, dim).astype(f32)


def bounds_of(sz, table):
    n, ch = sz.slots, sz.channels
    rows = [sz.outer_row(a + 1, b + 1) for a, b in sz.order]
    metas = jnp.concatenate([table[row : row + n, ch:] for row in rows], axis=0)
    shape = (sz.inner * n, sz.inner * n)
    left = lax.broadcasted_iota(jnp.int32, shape, 0)
    right = lax.broadcasted_iota(jnp.int32, shape, 1)
    earlier = (left // n == right // n) & (right < left)
    sums = mm(earlier.astype(f32).astype(bf16), metas)
    lane = code_lane + sz.neigh
    low = sums[:, lane : lane + 1]
    return low, low + metas[:, lane : lane + 1].astype(f32)


def gather_columns(sz, part, table, low, high, code, atom, sep, hot, xt):
    ch, n = sz.channels, sz.slots
    lane = iota((n, sz.edges), 1) + (part * sz.edges).astype(f32)
    row = iota((n, sz.edges), 0)
    slot = iota((sz.neigh, sz.edges), 0)
    target = iota((sz.window, sz.edges), 0)

    def one(col):
        a, b = sz.order[col]
        meta = table[pl.ds(sz.outer_row(a + 1, b + 1), n), ch : 2 * ch]
        mine = slice(col * n, (col + 1) * n)
        at = ((lane >= low[mine]) & (lane < high[mine])).astype(f32)
        valid = jnp.sum(at, axis=0, keepdims=True) - 1.0
        which = lane[:1] - jnp.sum(at * low[mine], axis=0, keepdims=True)
        spread = mm(meta.astype(f32).T[: 2 * code_lane].astype(bf16), at.astype(bf16))
        picked = jnp.where(slot == which, spread[code_lane:], 0.0)
        codes = jnp.sum(picked, axis=0, keepdims=True) + valid
        atoms = jnp.sum(at * row, axis=0, keepdims=True) + valid
        one_hot = (target == codes).astype(f32).astype(bf16)
        turned = window_of(sz, table, a, b).astype(f32).T.astype(bf16)[: ch + 32]
        found = mm(turned, one_hot)
        diff = found[ch : ch + 24] - spread[:24]
        return codes, atoms, one_hot, found[:ch], diff[0:8] + diff[8:16] + diff[16:24]

    def store(col, value):
        code[part, pl.ds(col, 1), :], atom[part, pl.ds(col, 1), :], one_hot, found, total = value
        if col < len(sz.own):
            hot[part, col] = one_hot
        xt[col] = found
        for d in range(3):
            sep[part, d, pl.ds(col, 1), :] = total[d : d + 1]

    loop(sz.inner, 4, each(one), store)


def shifted_seps(part, code, sep):
    offset = code[part].astype(jnp.int32) >> 4
    step_x = (offset * 11) >> 5
    step_y = offset - 3 * step_x
    sep[part, 0] = sep[part, 0] + column * (step_x - 1).astype(f32)
    sep[part, 1] = sep[part, 1] + column * (step_y - 1).astype(f32)


def geometry(live, seps):
    sep_x, sep_y, sep_z = seps
    dist_sq = sep_x * sep_x + sep_y * sep_y + sep_z * sep_z
    env = jnp.square(jnp.maximum(1.0 - dist_sq / (cutoff * cutoff), 0.0)) * live
    rows = harmonic_rows(sep_x / cutoff, sep_y / cutoff, sep_z / cutoff)
    return jnp.sqrt(dist_sq + softening), env, rows


def store_geometry(part, live, seps, dist, env, angular):
    dist[part], env[part], rows = geometry(live, seps)
    for m, row in enumerate(rows):
        angular[part, m] = row


def live_rows(code):
    return (code >= 0.0).astype(f32)


def basis_rows(sz, dist_row):
    width = dist_row.shape[1]
    spacing = cutoff / (sz.basis - 1)
    centre = lax.broadcasted_iota(jnp.int32, (sz.basis, width), 0).astype(f32) * spacing
    shifted = (dist_row - centre) * (1.0 / spacing)
    return jnp.exp(-shifted * shifted), shifted


def sigmoid(x):
    return 0.5 * jnp.tanh(0.5 * x) + 0.5


def hidden_rows(sz, dist_row, env_row, weight_in):
    basis, _ = basis_rows(sz, dist_row)
    high = basis.astype(bf16).astype(f32)
    stacked = jnp.concatenate([high, basis - high, high, jnp.zeros_like(high)], axis=0)
    pre = mm(weight_in, stacked.astype(bf16))
    gate = sigmoid(pre)
    value = pre * gate
    weighted = value * env_row
    high, low = split(weighted)
    slope = gate * (1.0 + pre * (1.0 - gate)) * env_row
    return jnp.concatenate([high, low, high], axis=0), value, slope


def atoms_at(sz, atom, part, col):
    return (iota((sz.slots, sz.edges), 0) == atom[part, pl.ds(col, 1), :]).astype(f32)


def block_rows(angular, part, col, at):
    return [angular[part, m, pl.ds(col, 1), :] * at for m in range(1, 9)]


def layer_forward(sz, part, cols, angular, dist, env, atom, weight_in, weight_out, inputs):
    rows = [jnp.concatenate([ref[part, pl.ds(c, 1), :] for c in cols], axis=1) for ref in (dist, env)]
    weighted, value, slope = hidden_rows(sz, *rows, weight_in)
    out = []
    for k, (col, xt) in enumerate(zip(cols, inputs)):
        span = slice(k * sz.edges, (k + 1) * sz.edges)
        radial = mm(weight_out, weighted[:, span])
        message = column_messages(sz, part, col, angular, atom, radial, xt)
        out.append((radial, value[:, span], slope[:, span], message))
    return out


def column_messages(sz, part, col, angular, atom, radial, xt):
    ch, n = sz.channels, sz.slots
    product = [(radial[l * ch : (l + 1) * ch] * xt).astype(bf16) for l in range(3)]
    at = atoms_at(sz, atom, part, col)
    scalar = nt(product[0], at.astype(bf16)).T
    blocks = jnp.concatenate(block_rows(angular, part, col, at), axis=0)
    high = blocks.astype(bf16).astype(f32)
    both = jnp.concatenate([high, blocks - high], axis=0).astype(bf16)
    count = 8 * n
    vector, tensor = nt(product[1], both), nt(product[2], both)
    vector = vector[:, :count] + vector[:, count:]
    tensor = tensor[:, :count] + tensor[:, count:]
    lane = lax.broadcasted_iota(jnp.int32, (ch, count), 1)
    return jnp.concatenate([scalar, jnp.where(lane < 3 * n, vector, tensor).T], axis=0)


def invariants(sz, message):
    n = sz.slots
    squares = message * message
    got = [squares[m * n : (m + 1) * n] for m in range(9)]
    return jnp.concatenate(
        [message[:n], got[1] + got[2] + got[3], got[4] + got[5] + got[6] + got[7] + got[8]],
        axis=1,
    )


def message_grads(sz, message, cotangent):
    ch, n = sz.channels, sz.slots
    twice = 2.0 * cotangent[:, ch:]
    parts = [
        message[m * n : (m + 1) * n] * (twice[:, :ch] if m < 4 else twice[:, ch:])
        for m in range(1, 9)
    ]
    return [cotangent[:, :ch]] + parts


def radial_products(sz, product_grad, radial, xt):
    ch = sz.channels
    products, mine, input_grad = [], [], None
    for l in range(3):
        grad, part = product_grad[l * ch : (l + 1) * ch], radial[l * ch : (l + 1) * ch]
        if l:
            products.append((part * xt).astype(bf16))
        mine.append((grad * xt).astype(bf16))
        term = grad * part
        input_grad = term if input_grad is None else input_grad + term
    return products, jnp.concatenate(mine, axis=0), input_grad.astype(bf16)


def radial_backward(sz, dist_row, radial_grad, value, slope, back_in, back_out):
    weighted_grad = mm(back_out, radial_grad)
    env_row_grad = jnp.sum(weighted_grad * value, axis=0, keepdims=True)
    both = mm(back_in, (weighted_grad * slope).astype(bf16))
    basis_grad = both[: sz.basis] + both[sz.basis : 2 * sz.basis]
    basis, shifted = basis_rows(sz, dist_row)
    spacing = cutoff / (sz.basis - 1)
    dist_row_grad = jnp.sum(
        basis_grad * basis * shifted * (-2.0 / spacing), axis=0, keepdims=True
    )
    return dist_row_grad, env_row_grad


def layer_backward(
    sz, part, cols, angular, dist, atom, back_in, back_out, radials, value, slope, inputs, hots,
    messages, cotangents,
):
    ch, n = sz.channels, sz.slots
    mine, windows, ang_grads = [], [], []
    for k, col in enumerate(cols):
        at = atoms_at(sz, atom, part, col)
        blocks = jnp.concatenate([at] + block_rows(angular, part, col, at), axis=0).astype(bf16)
        grads = message_grads(sz, messages[k], cotangents[k])
        turned = jnp.concatenate(grads, axis=0).T
        lane = lax.broadcasted_iota(jnp.int32, turned.shape, 1)
        lhs = jnp.concatenate(
            [
                jnp.where(lane < n, turned, 0.0),
                jnp.where((lane >= n) & (lane < 4 * n), turned, 0.0),
                jnp.where(lane >= 4 * n, turned, 0.0),
            ],
            axis=0,
        ).astype(bf16)
        products, radial_grad, input_grad = radial_products(
            sz, mm(lhs, blocks), radials[k], inputs[k]
        )
        mine.append(radial_grad)
        windows.append(nt(hots[k], input_grad))
        empty = jnp.zeros((n, ch), f32)
        wide = [
            jnp.concatenate([g, empty] if m < 3 else [empty, g], axis=1)
            for m, g in enumerate(grads[1:])
        ]
        got = mm(jnp.concatenate(wide, axis=0).astype(bf16), jnp.concatenate(products, axis=0))
        ang_grads.append(
            [jnp.sum(got[m * n : (m + 1) * n] * at, axis=0, keepdims=True) for m in range(8)]
        )
    dist_row = jnp.concatenate([dist[part, pl.ds(col, 1), :] for col in cols], axis=1)
    dist_row_grad, env_row_grad = radial_backward(
        sz, dist_row, jnp.concatenate(mine, axis=1), value, slope, back_in, back_out
    )
    out = []
    for k in range(len(cols)):
        span = slice(k * sz.edges, (k + 1) * sz.edges)
        out.append((windows[k], ang_grads[k], dist_row_grad[:, span], env_row_grad[:, span]))
    return out


def store_grads(sz, col, value, ang_grad, dist_grad, env_grad, acc):
    window, ang_grads, dist_row_grad, env_row_grad = value
    for m in range(8):
        ang_grad[m + 1, pl.ds(col, 1), :] = ang_grads[m]
    dist_grad[pl.ds(col, 1), :] = dist_row_grad
    env_grad[pl.ds(col, 1), :] = env_row_grad
    add_window(sz, sz.own[col], window, acc)


def add_window(sz, place, window, acc):
    a, b = place
    run = 3 * sz.slots
    for d in range(3):
        acc[pl.ds(sz.inner_row(a - 1 + d, b - 1), run), :] += window[d * run : (d + 1) * run]


def separation_grads(live, sep, dist, ang_grad, dist_grad, env_grad):
    sep_x, sep_y, sep_z = sep
    ux, uy, uz = sep_x / cutoff, sep_y / cutoff, sep_z / cutoff
    dist_sq = sep_x * sep_x + sep_y * sep_y + sep_z * sep_z
    inside = jnp.maximum(1.0 - dist_sq / (cutoff * cutoff), 0.0)
    sq_grad = dist_grad * (0.5 / dist) - env_grad * live * inside * (2.0 / (cutoff * cutoff))
    g = ang_grad
    r3 = root_three
    grad_x = g[1] + r3 * (uy * g[4] + uz * g[7] + ux * g[8]) - ux * g[6]
    grad_y = g[2] + r3 * (ux * g[4] + uz * g[5] - uy * g[8]) - uy * g[6]
    grad_z = g[3] + r3 * (uy * g[5] + ux * g[7]) + 2.0 * uz * g[6]
    return (
        2.0 * sep_x * sq_grad + grad_x / cutoff,
        2.0 * sep_y * sq_grad + grad_y / cutoff,
        2.0 * sep_z * sq_grad + grad_z / cutoff,
    )


def stacked_seps(rows):
    full = jnp.concatenate(rows + [jnp.zeros((5, rows[0].shape[1]), f32)], axis=0)
    high = full.astype(bf16).astype(f32)
    return jnp.concatenate([high, full - high], axis=0).astype(bf16)


def own_positions(
    sz, part, code, atom, sep, dist, hot, ang_grad, dist_grad, env_grad, sep_grad, acc_pos
):
    owned = len(sz.own)
    grads = separation_grads(
        live_rows(code[part, :owned]),
        [sep[part, d, :owned] for d in range(3)],
        dist[part, :owned],
        ang_grad,
        dist_grad[...],
        env_grad[...],
    )
    for d in range(3):
        sep_grad[d] = grads[d]
    for k, place in enumerate(sz.own):
        rows = [sep_grad[d, pl.ds(k, 1), :] for d in range(3)]
        signed = signed_hot(sz, hot[part, k], atoms_at(sz, atom, part, k).astype(bf16))
        got = nt(signed, stacked_seps(rows))
        add_window(sz, place, got[:, :8] + got[:, 8:], acc_pos)


def signed_hot(sz, one_hot, mask_bf):
    first = 4 * sz.slots
    return jnp.concatenate(
        [one_hot[:first], one_hot[first : first + sz.slots] - mask_bf, one_hot[first + sz.slots :]],
        axis=0,
    )


def fetch(sources, targets, sems):
    copies = [
        pltpu.make_async_copy(source, target, sems.at[k])
        for k, (source, target) in enumerate(zip(sources, targets))
    ]
    for copy in copies:
        copy.start()
    return copies


def block_kernel(sz, kinds, *refs):
    sources, block, held, sems = refs[:6], refs[6], refs[7:13], refs[13]
    for copy in fetch(sources, held, sems):
        copy.wait()
    features, positions, species, neighbours, counts, species_gain = held
    ch, n = sz.channels, sz.slots
    gains = species_gain[...]
    gain_high = gains.astype(bf16).astype(f32)
    rest = gains - gain_high
    gain_middle = rest.astype(bf16).astype(f32)
    parts = [gain_high, gain_middle, rest - gain_middle]
    above, below = jnp.zeros((24, ch), f32), jnp.zeros((8 - kinds, ch), f32)
    parts = [jnp.concatenate([above, part, below], axis=0).astype(bf16) for part in parts]
    kind = lax.broadcasted_iota(jnp.int32, (8, n), 0)
    tail_lane = lax.broadcasted_iota(jnp.int32, (n, ch - code_lane - sz.neigh), 1)
    lane = lax.broadcasted_iota(jnp.int32, (n, code_lane), 1)
    gap = jnp.zeros((5, n), f32)
    for a in range(sz.cols_x):
        for b in range(sz.cols_y):
            atoms = positions[a, :, b, :]
            high = atoms.astype(bf16).astype(f32)
            rest = atoms - high
            middle = rest.astype(bf16).astype(f32)
            chosen = (kind == species[a, pl.ds(b, 1), :]).astype(f32)
            last = jnp.where(kind == 7, counts[a, pl.ds(b, 1), :].astype(f32), chosen)
            rows = [high, gap, middle, gap, rest - middle, gap, last]
            turned = jnp.concatenate(rows, axis=0).T
            picked = jnp.where((lane >= 24) & (lane < 24 + kinds), turned, 0.0).astype(bf16)
            gain = mm(picked, parts[0]) + mm(picked, parts[1]) + mm(picked, parts[2])
            place = jnp.where(lane < 24, turned, 0.0)
            count = jnp.where(tail_lane == 0, turned[:, 31:32], 0.0)
            block[a, b, :, :ch] = (features[a, b].astype(f32) * gain).astype(bf16)
            block[a, b, :, ch:] = jnp.concatenate(
                [place, neighbours[a, b].astype(f32), count], axis=1
            ).astype(bf16)


def first_kernel(
    sz, table, wide_in, wide_out, turned_in, turned_out, mixing, readout,
    energy, back, kept, code, atom, sep,
    hot, xt, angular, dist, env, second, second_xt, second_msg, second_radial,
    second_value, second_slope, ang_grad, dist_grad, env_grad, sep_grad, acc, acc_pos,
):
    ch, n = sz.channels, sz.slots
    owned = len(sz.own)
    low, high = bounds_of(sz, table)
    most = jnp.maximum(jnp.max(high).astype(jnp.int32), 1)
    parts = (most + sz.edges - 1) // sz.edges
    in_one, out_one = wide_in[0], wide_out[0]
    code[...] = jnp.full_like(code, -1.0)
    kept[...] = jnp.zeros_like(kept)

    def first_part(part, carry):
        gather_columns(sz, part, table, low, high, code, atom, sep, hot, xt)
        shifted_seps(part, code, sep)
        seps = [sep[part, d] for d in range(3)]
        store_geometry(part, live_rows(code[part]), seps, dist, env, angular)

        def one(cols):
            inputs = [xt[col] for col in cols]
            return layer_forward(
                sz, part, cols, angular, dist, env, atom, in_one, out_one, inputs
            )

        def one_store(col, got):
            kept[col] += got[3]

        loop(sz.inner, 4, one, one_store)
        return carry

    lax.fori_loop(0, parts, first_part, 0)
    rows = [None] * sz.inner
    for col, (a, b) in enumerate(sz.order):
        rows[a * sz.inner_y + b] = invariants(sz, kept[col])
    own_rows = [
        table[(a * sz.outer_y + 1) * n : (a * sz.outer_y + 1 + sz.inner_y) * n, :ch]
        for a in range(1, 1 + sz.inner_x)
    ]
    first_out = three(mm, jnp.concatenate(rows, axis=0), mixing[0])
    first_out = first_out + jnp.concatenate(own_rows, axis=0).astype(f32)
    second[...] = first_out.astype(bf16)

    in_two, out_two = wide_in[1], wide_out[1]
    back_in, back_out = turned_in[1], turned_out[1]
    second_msg[...] = jnp.zeros_like(second_msg)
    every = list(range(owned))

    def second_part(part, carry):
        def second_input(k):
            a, b = sz.own[k]
            window = jnp.concatenate(
                [second[pl.ds(sz.inner_row(a - 1 + d, b - 1), 3 * n), :] for d in range(3)],
                axis=0,
            )
            return mm(window.astype(f32).T.astype(bf16), hot[part, k])

        inputs = [second_input(k) for k in every]
        got = layer_forward(sz, part, every, angular, dist, env, atom, in_two, out_two, inputs)
        for k, (radial, value, slope, message) in zip(every, got):
            second_xt[part, k], second_radial[part, k] = inputs[k], radial
            second_value[part, k], second_slope[part, k] = value, slope
            second_msg[k] += message
        return carry

    lax.fori_loop(0, parts, second_part, 0)
    inv = jnp.concatenate([invariants(sz, second_msg[k]) for k in every], axis=0)
    own_rows = [
        second[(a * sz.inner_y + 1) * n : (a * sz.inner_y + 1 + sz.cols_y) * n, :]
        for a in range(1, 1 + sz.cols_x)
    ]
    out = three(mm, inv, mixing[1]) + jnp.concatenate(own_rows, axis=0).astype(f32)
    gate = sigmoid(out)
    weights = readout[...]
    total = three(nt, jnp.ones((8, ch), f32), out * gate * weights)
    for k, (a, b) in enumerate(sz.own):
        energy[a - 1, b - 1 : b, :] = total[0:1, k * n : (k + 1) * n]
    out_grad = gate * (1.0 + out * (1.0 - gate)) * weights
    cotangents = three(nt, out_grad, mixing[1])
    acc[...] = jnp.zeros_like(acc)
    acc_pos[...] = jnp.zeros_like(acc_pos)
    for a in range(sz.cols_x):
        first = ((a + 1) * sz.inner_y + 1) * n
        acc[first : first + sz.cols_y * n] = out_grad[a * sz.cols_y * n : (a + 1) * sz.cols_y * n]

    def back_part(part, carry):
        got = layer_backward(
            sz, part, every, angular, dist, atom, back_in, back_out,
            [second_radial[part, k] for k in every],
            jnp.concatenate([second_value[part, k] for k in every], axis=1),
            jnp.concatenate([second_slope[part, k] for k in every], axis=1),
            [second_xt[part, k] for k in every],
            [hot[part, k] for k in every],
            [second_msg[k] for k in every],
            [cotangents[k * n : (k + 1) * n] for k in every],
        )
        for k, value in zip(every, got):
            store_grads(sz, k, value, ang_grad, dist_grad, env_grad, acc)
        own_positions(
            sz, part, code, atom, sep, dist, hot, ang_grad, dist_grad, env_grad, sep_grad, acc_pos
        )
        return carry

    lax.fori_loop(0, parts, back_part, 0)
    back[:, :ch] = acc[...].astype(bf16)
    high = acc_pos[...].astype(bf16)
    low = (acc_pos[...] - high.astype(f32)).astype(f32)
    filler = jnp.zeros((acc_pos.shape[0], ch - 16), f32)
    back[:, ch:] = jnp.concatenate([high.astype(f32), low, filler], axis=1).astype(bf16)


def packed_halo(sz, code, target, place):
    rows = len(sz.halo)
    first = len(sz.own)
    row = lax.broadcasted_iota(jnp.int32, (rows, sz.edges), 0)
    at_x, at_y = jnp.zeros_like(row), jnp.zeros_like(row)
    for h, (a, b) in enumerate(sz.halo):
        at_x, at_y = jnp.where(row == h, a, at_x), jnp.where(row == h, b, at_y)
    shape = (sz.edges, sz.edges)
    before = iota(shape, 0) <= iota(shape, 1)
    above = iota((rows, rows), 1) < iota((rows, rows), 0)
    count = jnp.zeros((1, 1), f32)
    for part in range(2):
        codes = code[part, first:].astype(jnp.int32)
        offset = codes >> 4
        step_x = (offset * 11) >> 5
        to_x = at_x + step_x - 2
        to_y = at_y + offset - 3 * step_x - 2
        inside = (to_x >= 0) & (to_x < sz.cols_x) & (to_y >= 0) & (to_y < sz.cols_y)
        flags = (inside & (codes >= 0)).astype(f32)
        wanted = (to_x * sz.cols_y + to_y) * sz.slots + (codes & 15)
        target[part] = flags * wanted.astype(f32)
        flags_bf = flags.astype(bf16)
        running = mm(flags_bf, before.astype(f32).astype(bf16)) - 1.0
        earlier = jnp.sum(mm(above.astype(f32).astype(bf16), flags_bf), axis=1, keepdims=True)
        place[part] = jnp.where(flags > 0.0, running + earlier + count, -1.0)
        count = count + jnp.sum(jnp.sum(flags, axis=1, keepdims=True), axis=0, keepdims=True)
    return (jnp.max(count).astype(jnp.int32) + sz.edges - 1) // sz.edges


def halo_back(
    sz, part, edge_parts, own_turned, atom, sep, gathered, weights, target, place,
    feature_acc, pos_acc,
):
    in_one, out_one, back_in, back_out = weights
    ch, n, lanes = sz.channels, sz.slots, sz.edges
    first = len(sz.own)
    count = len(sz.halo) * n
    wanted = iota((lanes, lanes), 0) + (part * lanes).astype(f32)
    ones, zeros = jnp.ones((1, lanes), f32), jnp.zeros((2, lanes), f32)

    def packed(edge_part, total):
        picks, sides = [], []
        for h in range(len(sz.halo)):
            pick = place[edge_part, pl.ds(h, 1), :] == wanted
            picks.append(pick.astype(f32).astype(bf16))
            rows = jnp.concatenate(
                [sep[edge_part, d, pl.ds(first + h, 1), :] for d in range(3)]
                + [
                    target[edge_part, pl.ds(h, 1), :],
                    atom[edge_part, pl.ds(first + h, 1), :] + float(h * n),
                    ones,
                    zeros,
                ],
                axis=0,
            )
            high = rows.astype(bf16).astype(f32)
            middle = (rows - high).astype(bf16).astype(f32)
            sides.append(
                jnp.concatenate([high, middle, rows - high - middle], axis=0).astype(bf16)
            )
        return total + nt(jnp.concatenate(sides, axis=1), jnp.concatenate(picks, axis=1))

    got = lax.fori_loop(0, edge_parts, packed, jnp.zeros((24, lanes), f32))
    got = got[0:8] + got[8:16] + got[16:24]
    seps = [got[d : d + 1] for d in range(3)]
    target_row, atom_row, valid = got[3:4], got[4:5], got[5:6]
    dist_row, env_row, angular = geometry(valid, seps)
    weighted, value, slope = hidden_rows(sz, dist_row, env_row, in_one)
    radial = mm(out_one, weighted)
    chosen = iota((first * n, lanes), 0) == target_row
    one_hot = jnp.where(chosen, valid, 0.0).astype(bf16)
    xt = mm(own_turned, one_hot)
    sources = jnp.where(iota((count, lanes), 0) == atom_row, valid, 0.0).astype(bf16)
    spread = mm(gathered[...], sources)
    parts = [spread[m * ch : (m + 1) * ch] for m in range(9)]
    vector = angular[1] * parts[1] + angular[2] * parts[2] + angular[3] * parts[3]
    tensor = angular[4] * parts[4]
    for m in range(5, 9):
        tensor = tensor + angular[m] * parts[m]
    product_grad = jnp.concatenate([parts[0], vector, tensor], axis=0)
    _, radial_grad, input_grad = radial_products(sz, product_grad, radial, xt)
    products = [radial[l * ch : (l + 1) * ch] * xt for l in range(3)]
    ang_grad = [None] + [
        jnp.sum(parts[m] * products[1 if m < 4 else 2], axis=0, keepdims=True)
        for m in range(1, 9)
    ]
    dist_grad, env_grad = radial_backward(
        sz, dist_row, radial_grad, value, slope, back_in, back_out
    )
    grads = separation_grads(valid, seps, dist_row, ang_grad, dist_grad, env_grad)
    feature_acc[...] += nt(one_hot, input_grad)
    got = nt(one_hot, stacked_seps(list(grads)))
    pos_acc[...] += got[:, :8] + got[:, 8:]


def second_kernel(
    sz, cotangent, table, kept, code, atom, sep,
    wide_in, wide_out, turned_in, turned_out, mixing,
    feature_grad, forces,
    hot, xt, angular, dist, env, ang_grad, dist_grad, env_grad, sep_grad,
    acc, acc_pos, halo_acc, halo_pos, target, place, gathered,
):
    ch, n = sz.channels, sz.slots
    inv = three(nt, cotangent[:, :ch], mixing[0])
    halo_parts = packed_halo(sz, code, target, place)
    second_used = (jnp.max(code[1]) >= 0.0).astype(jnp.int32)
    edge_parts = 1 + second_used
    in_one, out_one = wide_in[0], wide_out[0]
    back_in, back_out = turned_in[0], turned_out[0]
    owned = len(sz.own)
    every = list(range(owned))
    index = iota((sz.window, sz.edges), 0)
    acc[...] = jnp.zeros_like(acc)
    acc_pos[...] = jnp.zeros_like(acc_pos)
    halo_acc[...] = jnp.zeros_like(halo_acc)
    halo_pos[...] = jnp.zeros_like(halo_pos)

    def inv_rows(a, b):
        row = sz.inner_row(a, b)
        return inv[row : row + n]

    turned = [window_of(sz, table, *place_)[:, :ch].astype(f32).T.astype(bf16) for place_ in sz.own]

    def back_part(part, carry):
        seps = [sep[part, d, :owned] for d in range(3)]
        store_geometry(part, live_rows(code[part, :owned]), seps, dist, env, angular)
        hots = [
            (index == code[part, pl.ds(k, 1), :]).astype(f32).astype(bf16) for k in every
        ]
        for k in every:
            hot[part, k] = hots[k]
        rows = [
            jnp.concatenate([ref[part, pl.ds(k, 1), :] for k in every], axis=1)
            for ref in (dist, env)
        ]
        weighted, value, slope = hidden_rows(sz, *rows, in_one)
        got = layer_backward(
            sz, part, every, angular, dist, atom, back_in, back_out,
            [mm(out_one, weighted[:, k * sz.edges : (k + 1) * sz.edges]) for k in every],
            value, slope,
            [mm(turned[k], hots[k]) for k in every],
            hots,
            [kept[k] for k in every],
            [inv_rows(*sz.own[k]) for k in every],
        )
        for k, value in zip(every, got):
            store_grads(sz, k, value, ang_grad, dist_grad, env_grad, acc)
        own_positions(
            sz, part, code, atom, sep, dist, hot, ang_grad, dist_grad, env_grad, sep_grad, acc_pos
        )
        return carry

    lax.fori_loop(0, edge_parts, back_part, 0)
    halo_grads = [
        message_grads(sz, kept[owned + h], inv_rows(a, b)) for h, (a, b) in enumerate(sz.halo)
    ]
    for m in range(9):
        rows = jnp.concatenate([grads[m] for grads in halo_grads], axis=0)
        gathered[m * ch : (m + 1) * ch, :] = rows.T.astype(bf16)
    own_rows = [
        table[sz.outer_row(a + 2, 2) : sz.outer_row(a + 2, 2) + sz.cols_y * n, :ch]
        for a in range(sz.cols_x)
    ]
    own_turned = jnp.concatenate(own_rows, axis=0).astype(f32).T.astype(bf16)
    weights = (in_one, out_one, back_in, back_out)

    def halo_part(part, carry):
        halo_back(
            sz, part, edge_parts, own_turned, atom, sep, gathered, weights, target, place,
            halo_acc, halo_pos,
        )
        return carry

    lax.fori_loop(0, halo_parts, halo_part, 0)
    for a in range(sz.cols_x):
        inner = sz.inner_row(a + 1, 1)
        rows = sz.cols_y * n
        mine = slice(a * rows, (a + 1) * rows)
        feature_grad[mine] = (
            acc[inner : inner + rows] + cotangent[inner : inner + rows, :ch] + halo_acc[mine]
        )
        extra = cotangent[inner : inner + rows, ch : ch + 16]
        total = acc_pos[inner : inner + rows] + extra[:, :8] + extra[:, 8:] + halo_pos[mine]
        for b in range(sz.cols_y):
            forces[a, :, b, :] = -(total[b * n : (b + 1) * n].T)[:3]


def ring(axis):
    devices = lax.axis_size(axis)
    up = [(i, (i + 1) % devices) for i in range(devices)]
    return up, [(j, i) for i, j in up]


def extended(x, sides):
    for axis, dim in sides:
        up, down = ring(axis)
        length = x.shape[dim]
        last = lax.slice_in_dim(x, length - 2, length, axis=dim)
        initial = lax.slice_in_dim(x, 0, 2, axis=dim)
        before = lax.ppermute(last, axis, up)
        after = lax.ppermute(initial, axis, down)
        x = jnp.concatenate([before, x, after], axis=dim)
    return x


def summed(x, sides):
    total = x.astype(f32)
    for axis, dim in sides:
        up, down = ring(axis)
        length = x.shape[dim]
        sent = total.astype(bf16)
        last = lax.slice_in_dim(sent, length - 2, length, axis=dim)
        initial = lax.slice_in_dim(sent, 0, 2, axis=dim)
        before = lax.ppermute(last, axis, up).astype(f32)
        after = lax.ppermute(initial, axis, down).astype(f32)
        shape = list(x.shape)
        shape[dim] = length - 4
        parts = [before] + ([jnp.zeros(shape, f32)] if length > 4 else []) + [after]
        total = total + jnp.concatenate(parts, axis=dim)
    return total


def shards(
    features, positions, species, neighbours, counts, species_gain, radial_in, radial_out, mixing, readout
):
    cols_x, cols_y, slots, channels = features.shape
    neigh = neighbours.shape[-1]
    basis, hidden = radial_in.shape[1:]
    sz = Sizes(cols_x, cols_y, slots, neigh, channels, basis, hidden)
    vmem = pl.BlockSpec(memory_space=pltpu.VMEM)
    in_hbm = pl.BlockSpec(memory_space=pltpu.HBM)
    params = pltpu.CompilerParams(vmem_limit_bytes=40 * 1024 * 1024)
    given = (features, positions.transpose(0, 2, 1, 3), species, neighbours, counts, species_gain)
    block = pl.pallas_call(
        functools.partial(block_kernel, sz, species_gain.shape[0]),
        out_shape=jax.ShapeDtypeStruct((cols_x, cols_y, slots, 2 * channels), bf16),
        in_specs=[in_hbm] * 6,
        out_specs=vmem,
        scratch_shapes=[pltpu.VMEM(x.shape, x.dtype) for x in given]
        + [pltpu.SemaphoreType.DMA((6,))],
        compiler_params=pltpu.CompilerParams(vmem_limit_bytes=60 * 1024 * 1024),
        name="block_of_atoms",
    )(*given)
    sides = (("gx", 0), ("gy", 1))
    table = extended(block, sides).reshape(-1, 2 * channels)

    inner_atoms = sz.inner * slots
    owned = cols_x * cols_y
    edges = sz.edges
    columns = sz.inner
    grads = [
        pltpu.VMEM((9, owned, edges), f32),
        pltpu.VMEM((owned, edges), f32),
        pltpu.VMEM((owned, edges), f32),
        pltpu.VMEM((3, owned, edges), f32),
    ]
    weights = prepared(radial_in, radial_out, mixing)
    assert slots * neigh <= 2 * edges
    kept_shapes = [
        (columns, sz.window, channels),
        (2, columns, edges),
        (2, columns, edges),
        (2, 3, columns, edges),
    ]

    def edge_scratch(count):
        return [
            pltpu.VMEM((2, owned, sz.window, edges), bf16),
            pltpu.VMEM((count, channels, edges), f32),
            pltpu.VMEM((2, 9, count, edges), f32),
            pltpu.VMEM((2, count, edges), f32),
            pltpu.VMEM((2, count, edges), f32),
        ]

    energy, back, *kept = pl.pallas_call(
        functools.partial(first_kernel, sz),
        out_shape=[
            jax.ShapeDtypeStruct((cols_x, cols_y, slots), f32),
            jax.ShapeDtypeStruct((inner_atoms, 2 * channels), bf16),
        ]
        + [jax.ShapeDtypeStruct(shape, f32) for shape in kept_shapes],
        in_specs=[vmem] * 7,
        out_specs=[vmem] * 6,
        scratch_shapes=edge_scratch(columns)
        + [
            pltpu.VMEM((inner_atoms, channels), bf16),
            pltpu.VMEM((2, owned, channels, edges), f32),
            pltpu.VMEM((owned, sz.window, channels), f32),
            pltpu.VMEM((2, owned, 3 * channels, edges), f32),
            pltpu.VMEM((2, owned, hidden, edges), f32),
            pltpu.VMEM((2, owned, hidden, edges), f32),
        ]
        + grads
        + [pltpu.VMEM((inner_atoms, channels), f32), pltpu.VMEM((inner_atoms, 8), f32)],
        compiler_params=params,
        name="forward_and_second_back",
    )(table, *weights, readout.reshape(1, -1))

    back = back.reshape(sz.inner_x, sz.inner_y, slots, 2 * channels)
    cotangent = summed(back, sides).reshape(inner_atoms, 2 * channels)
    feature_grad, forces = pl.pallas_call(
        functools.partial(second_kernel, sz),
        out_shape=(
            jax.ShapeDtypeStruct((owned * slots, channels), f32),
            jax.ShapeDtypeStruct((cols_x, 3, cols_y, slots), f32),
        ),
        in_specs=[vmem] * 11,
        out_specs=(vmem,) * 2,
        scratch_shapes=edge_scratch(owned)
        + grads
        + [
            pltpu.VMEM((rows, width), f32)
            for rows in (inner_atoms, owned * slots)
            for width in (channels, 8)
        ]
        + [
            pltpu.VMEM((2, len(sz.halo), edges), f32),
            pltpu.VMEM((2, len(sz.halo), edges), f32),
            pltpu.VMEM((9 * channels, len(sz.halo) * slots), bf16),
        ],
        compiler_params=params,
        name="first_back",
    )(cotangent, table, *kept, *weights)
    return (
        energy,
        forces.transpose(0, 2, 1, 3),
        feature_grad.reshape(cols_x, cols_y, slots, channels),
    )


def solution(mesh):
    placed = (
        P("gx", "gy", None, None),
        P("gx", "gy", None, None),
        P("gx", "gy", None),
        P("gx", "gy", None, None),
        P("gx", "gy", None),
        P(),
        P(),
        P(),
        P(),
        P(),
    )
    return jax.shard_map(
        shards,
        mesh=mesh,
        in_specs=placed,
        out_specs=(P("gx", "gy", None), P("gx", "gy", None, None), P("gx", "gy", None, None)),
        check_vma=False,
    )
```

```python
import functools

import jax
import jax.numpy as jnp
from jax import lax
from jax.experimental import pallas as pl
from jax.experimental.pallas import tpu as pltpu
from jax.sharding import PartitionSpec as P

column = 6.0
cutoff = 6.0
softening = 0.01
root_three = 3.0**0.5
f32 = jnp.float32
bf16 = jnp.bfloat16
code_lane = 32
count_lane = 31
part_lanes = 256


def mm(a, b):
    return lax.dot_general(a, b, (((1,), (0,)), ((), ())), preferred_element_type=f32)


def nt(a, b):
    return lax.dot_general(a, b, (((1,), (1,)), ((), ())), preferred_element_type=f32)


def split(x):
    high = x.astype(bf16)
    return high, (x - high.astype(f32)).astype(bf16)


def three(product, a, b):
    a_high, a_low = split(a)
    b_high, b_low = split(b) if b.dtype == f32 else (b[0], b[1])
    return product(a_high, b_high) + product(a_low, b_high) + product(a_high, b_low)


def parted(x):
    high = lax.reduce_precision(x, 8, 7)
    return high, x - high


def prepared(radial_in, radial_out, mixing):
    high, low = parted(radial_in)
    turned = jnp.concatenate([high, high, low, jnp.zeros_like(high)], axis=1).swapaxes(1, 2)
    back_in = jnp.concatenate([high, low], axis=1)
    high, low = parted(radial_out)
    wide = jnp.concatenate([high, high, low], axis=1).swapaxes(1, 2)
    high_mix, low_mix = parted(mixing)
    mix = jnp.stack([high_mix, low_mix], axis=1)
    return [x.astype(bf16) for x in (turned, wide, back_in, high, mix)]


def harmonic_rows(ux, uy, uz):
    square = ux * ux + uy * uy + uz * uz
    return [
        jnp.ones_like(ux),
        ux,
        uy,
        uz,
        root_three * ux * uy,
        root_three * uy * uz,
        0.5 * (3.0 * uz * uz - square),
        root_three * ux * uz,
        0.5 * root_three * (ux * ux - uy * uy),
    ]


class Sizes:
    def __init__(self, cols_x, cols_y, slots, neigh, channels, basis, hidden):
        self.cols_x, self.cols_y = cols_x, cols_y
        self.slots, self.neigh, self.channels = slots, neigh, channels
        self.basis, self.hidden = basis, hidden
        self.inner_x, self.inner_y = cols_x + 2, cols_y + 2
        self.outer_y = cols_y + 4
        self.inner = self.inner_x * self.inner_y
        self.edges = part_lanes
        self.window = 9 * slots

        cells = [(a, b) for a in range(self.inner_x) for b in range(self.inner_y)]
        self.own = [c for c in cells if self.is_own(*c)]
        self.halo = [c for c in cells if not self.is_own(*c)]
        self.order = self.own + self.halo

    def is_own(self, a, b):
        return 1 <= a <= self.cols_x and 1 <= b <= self.cols_y

    def outer_row(self, a, b):
        return (a * self.outer_y + b) * self.slots

    def inner_row(self, a, b):
        return (a * self.inner_y + b) * self.slots


def each(compute):
    return lambda items: [compute(item) for item in items]


def loop(count, group, compute, store):
    for first in range(0, count, group):
        items = list(range(first, min(first + group, count)))
        for item, value in zip(items, compute(items)):
            store(item, value)


def window_of(sz, table, a, b):
    run = 3 * sz.slots
    return jnp.concatenate(
        [table[pl.ds(sz.outer_row(a + d, b), run), :] for d in range(3)], axis=0
    )


def inner_window(sz, table, a, b):
    rows = [sz.inner_row(a - 1 + d, b - 1) for d in range(3)]
    return jnp.concatenate([table[row : row + 3 * sz.slots, :] for row in rows], axis=0)


def iota(shape, dim):
    return lax.broadcasted_iota(jnp.int32, shape, dim).astype(f32)


def bounds_of(sz, table):
    n, ch = sz.slots, sz.channels
    rows = [sz.outer_row(a + 1, b + 1) for a, b in sz.order]
    metas = jnp.concatenate([table[row : row + n, ch:] for row in rows], axis=0)
    shape = (sz.inner * n, sz.inner * n)
    left = lax.broadcasted_iota(jnp.int32, shape, 0)
    right = lax.broadcasted_iota(jnp.int32, shape, 1)
    earlier = (left // n == right // n) & (right < left)
    sums = mm(earlier.astype(f32).astype(bf16), metas)
    low = sums[:, count_lane : count_lane + 1]
    return low, low + metas[:, count_lane : count_lane + 1].astype(f32)


def gather_columns(sz, part, table, low, high, code, atom, sep, hot, xt):
    ch, n = sz.channels, sz.slots
    lane = iota((n, sz.edges), 1) + (part * sz.edges).astype(f32)
    row = iota((n, sz.edges), 0)
    slot = iota((sz.neigh, sz.edges), 0)
    target = iota((sz.window, sz.edges), 0)

    def one(col):
        a, b = sz.order[col]
        meta = table[pl.ds(sz.outer_row(a + 1, b + 1), n), ch : 2 * ch]
        mine = slice(col * n, (col + 1) * n)
        at = ((lane >= low[mine]) & (lane < high[mine])).astype(f32)
        valid = jnp.sum(at, axis=0, keepdims=True) - 1.0
        which = lane[:1] - jnp.sum(at * low[mine], axis=0, keepdims=True)
        spread = mm(meta.astype(f32).T[: 2 * code_lane].astype(bf16), at.astype(bf16))
        picked = jnp.where(slot == which, spread[code_lane:], 0.0)
        codes = jnp.sum(picked, axis=0, keepdims=True) + valid
        atoms = jnp.sum(at * row, axis=0, keepdims=True) + valid
        one_hot = (target == codes).astype(f32).astype(bf16)
        turned = window_of(sz, table, a, b).astype(f32).T.astype(bf16)[: ch + 32]
        found = mm(turned, one_hot)
        diff = found[ch : ch + 24] - spread[:24]
        return codes, atoms, one_hot, found[:ch], diff[0:8] + diff[8:16] + diff[16:24]

    def store(col, value):
        code[part, pl.ds(col, 1), :], atom[part, pl.ds(col, 1), :], one_hot, found, total = value
        if col < len(sz.own):
            hot[part, col] = one_hot
        xt[col] = found
        for d in range(3):
            sep[part, d, pl.ds(col, 1), :] = total[d : d + 1]

    loop(sz.inner, 4, each(one), store)


def shifted_seps(part, code, sep):
    offset = code[part].astype(jnp.int32) >> 4
    step_x = (offset * 11) >> 5
    step_y = offset - 3 * step_x
    sep[part, 0] = sep[part, 0] + column * (step_x - 1).astype(f32)
    sep[part, 1] = sep[part, 1] + column * (step_y - 1).astype(f32)


def geometry(live, seps):
    sep_x, sep_y, sep_z = seps
    dist_sq = sep_x * sep_x + sep_y * sep_y + sep_z * sep_z
    env = jnp.square(jnp.maximum(1.0 - dist_sq / (cutoff * cutoff), 0.0)) * live
    rows = harmonic_rows(sep_x / cutoff, sep_y / cutoff, sep_z / cutoff)
    return jnp.sqrt(dist_sq + softening), env, rows


def store_geometry(part, live, seps, dist, env, angular):
    dist[part], env[part], rows = geometry(live, seps)
    for m, row in enumerate(rows):
        angular[part, m] = row


def live_rows(code):
    return (code >= 0.0).astype(f32)


def basis_rows(sz, dist_row):
    width = dist_row.shape[1]
    spacing = cutoff / (sz.basis - 1)
    centre = lax.broadcasted_iota(jnp.int32, (sz.basis, width), 0).astype(f32) * spacing
    shifted = (dist_row - centre) * (1.0 / spacing)
    return jnp.exp(-shifted * shifted), shifted


def sigmoid(x):
    return 0.5 * jnp.tanh(0.5 * x) + 0.5


def hidden_rows(sz, dist_row, env_row, weight_in):
    basis, _ = basis_rows(sz, dist_row)
    high = basis.astype(bf16).astype(f32)
    stacked = jnp.concatenate([high, basis - high, high, jnp.zeros_like(high)], axis=0)
    pre = mm(weight_in, stacked.astype(bf16))
    gate = sigmoid(pre)
    value = pre * gate
    weighted = value * env_row
    high, low = split(weighted)
    slope = gate * (1.0 + pre * (1.0 - gate)) * env_row
    return jnp.concatenate([high, low, high], axis=0), value, slope


def atoms_at(sz, atom, part, col):
    return (iota((sz.slots, sz.edges), 0) == atom[part, pl.ds(col, 1), :]).astype(f32)


def block_rows(angular, part, col, at):
    return [angular[part, m, pl.ds(col, 1), :] * at for m in range(1, 9)]


def layer_forward(sz, part, cols, angular, dist, env, atom, weight_in, weight_out, inputs):
    rows = [jnp.concatenate([ref[part, pl.ds(c, 1), :] for c in cols], axis=1) for ref in (dist, env)]
    weighted, value, slope = hidden_rows(sz, *rows, weight_in)
    radials = mm(weight_out, weighted)
    out = []
    for k, (col, xt) in enumerate(zip(cols, inputs)):
        span = slice(k * sz.edges, (k + 1) * sz.edges)
        radial = radials[:, span]
        message = column_messages(sz, part, col, angular, atom, radial, xt)
        out.append((radial, value[:, span], slope[:, span], message))
    return out


def column_messages(sz, part, col, angular, atom, radial, xt):
    ch, n = sz.channels, sz.slots
    product = (radial * jnp.concatenate([xt] * 3, axis=0)).astype(bf16)
    at = atoms_at(sz, atom, part, col)
    blocks = jnp.concatenate(block_rows(angular, part, col, at), axis=0)
    high = blocks.astype(bf16).astype(f32)
    low = blocks - high
    out = [nt(at.astype(bf16), product[:ch])]
    for l, rows in ((1, slice(0, 3 * n)), (2, slice(3 * n, 8 * n))):
        both = jnp.concatenate([high[rows], low[rows]], axis=0).astype(bf16)
        got = nt(both, product[l * ch : (l + 1) * ch])
        count = got.shape[0] // 2
        out.append(got[:count] + got[count:])
    return jnp.concatenate(out, axis=0)


def invariants(sz, message):
    n = sz.slots
    squares = message * message
    got = [squares[m * n : (m + 1) * n] for m in range(9)]
    return jnp.concatenate(
        [message[:n], got[1] + got[2] + got[3], got[4] + got[5] + got[6] + got[7] + got[8]],
        axis=1,
    )


def message_grads(sz, message, cotangent):
    ch, n = sz.channels, sz.slots
    twice = 2.0 * cotangent[:, ch:]
    parts = [
        message[m * n : (m + 1) * n] * (twice[:, :ch] if m < 4 else twice[:, ch:])
        for m in range(1, 9)
    ]
    return [cotangent[:, :ch]] + parts


def radial_products(sz, product_grad, radial, xt):
    ch = sz.channels
    products, mine, input_grad = [], [], None
    for l in range(3):
        grad, part = product_grad[l * ch : (l + 1) * ch], radial[l * ch : (l + 1) * ch]
        if l:
            products.append((part * xt).astype(bf16))
        mine.append((grad * xt).astype(bf16))
        term = grad * part
        input_grad = term if input_grad is None else input_grad + term
    return products, jnp.concatenate(mine, axis=0), input_grad.astype(bf16)


def radial_backward(sz, dist_row, radial_grad, value, slope, back_in, back_out):
    weighted_grad = mm(back_out, radial_grad)
    env_row_grad = jnp.sum(weighted_grad * value, axis=0, keepdims=True)
    both = mm(back_in, (weighted_grad * slope).astype(bf16))
    basis_grad = both[: sz.basis] + both[sz.basis : 2 * sz.basis]
    basis, shifted = basis_rows(sz, dist_row)
    spacing = cutoff / (sz.basis - 1)
    dist_row_grad = jnp.sum(
        basis_grad * basis * shifted * (-2.0 / spacing), axis=0, keepdims=True
    )
    return dist_row_grad, env_row_grad


def layer_backward(
    sz, part, cols, angular, dist, atom, back_in, back_out, radials, value, slope, inputs, hots,
    messages, cotangents,
):
    ch, n = sz.channels, sz.slots
    mine, windows, ang_grads = [], [], []
    for k, col in enumerate(cols):
        at = atoms_at(sz, atom, part, col)
        blocks = jnp.concatenate([at] + block_rows(angular, part, col, at), axis=0).astype(bf16)
        grads = message_grads(sz, messages[k], cotangents[k])
        turned = jnp.concatenate(grads, axis=0).T
        lane = lax.broadcasted_iota(jnp.int32, turned.shape, 1)
        lhs = jnp.concatenate(
            [
                jnp.where(lane < n, turned, 0.0),
                jnp.where((lane >= n) & (lane < 4 * n), turned, 0.0),
                jnp.where(lane >= 4 * n, turned, 0.0),
            ],
            axis=0,
        ).astype(bf16)
        products, radial_grad, input_grad = radial_products(
            sz, mm(lhs, blocks), radials[k], inputs[k]
        )
        mine.append(radial_grad)
        windows.append(nt(hots[k], input_grad))
        empty = jnp.zeros((n, ch), f32)
        wide = [
            jnp.concatenate([g, empty] if m < 3 else [empty, g], axis=1)
            for m, g in enumerate(grads[1:])
        ]
        got = mm(jnp.concatenate(wide, axis=0).astype(bf16), jnp.concatenate(products, axis=0))
        ang_grads.append(
            [jnp.sum(got[m * n : (m + 1) * n] * at, axis=0, keepdims=True) for m in range(8)]
        )
    dist_row = jnp.concatenate([dist[part, pl.ds(col, 1), :] for col in cols], axis=1)
    dist_row_grad, env_row_grad = radial_backward(
        sz, dist_row, jnp.concatenate(mine, axis=1), value, slope, back_in, back_out
    )
    out = []
    for k in range(len(cols)):
        span = slice(k * sz.edges, (k + 1) * sz.edges)
        out.append((windows[k], ang_grads[k], dist_row_grad[:, span], env_row_grad[:, span]))
    return out


def store_grads(sz, col, value, ang_grad, dist_grad, env_grad, acc):
    window, ang_grads, dist_row_grad, env_row_grad = value
    for m in range(8):
        ang_grad[m + 1, pl.ds(col, 1), :] = ang_grads[m]
    dist_grad[pl.ds(col, 1), :] = dist_row_grad
    env_grad[pl.ds(col, 1), :] = env_row_grad
    add_window(sz, sz.own[col], window, acc)


def add_window(sz, place, window, acc):
    a, b = place
    run = 3 * sz.slots
    for d in range(3):
        acc[pl.ds(sz.inner_row(a - 1 + d, b - 1), run), :] += window[d * run : (d + 1) * run]


def separation_grads(live, sep, dist, ang_grad, dist_grad, env_grad):
    sep_x, sep_y, sep_z = sep
    ux, uy, uz = sep_x / cutoff, sep_y / cutoff, sep_z / cutoff
    dist_sq = sep_x * sep_x + sep_y * sep_y + sep_z * sep_z
    inside = jnp.maximum(1.0 - dist_sq / (cutoff * cutoff), 0.0)
    sq_grad = dist_grad * (0.5 / dist) - env_grad * live * inside * (2.0 / (cutoff * cutoff))
    g = ang_grad
    r3 = root_three
    grad_x = g[1] + r3 * (uy * g[4] + uz * g[7] + ux * g[8]) - ux * g[6]
    grad_y = g[2] + r3 * (ux * g[4] + uz * g[5] - uy * g[8]) - uy * g[6]
    grad_z = g[3] + r3 * (uy * g[5] + ux * g[7]) + 2.0 * uz * g[6]
    return (
        2.0 * sep_x * sq_grad + grad_x / cutoff,
        2.0 * sep_y * sq_grad + grad_y / cutoff,
        2.0 * sep_z * sq_grad + grad_z / cutoff,
    )


def stacked_seps(rows):
    full = jnp.concatenate(rows + [jnp.zeros((5, rows[0].shape[1]), f32)], axis=0)
    high = full.astype(bf16).astype(f32)
    return jnp.concatenate([high, full - high], axis=0).astype(bf16)


def own_positions(
    sz, part, code, atom, sep, dist, hot, ang_grad, dist_grad, env_grad, sep_grad, acc_pos
):
    owned = len(sz.own)
    grads = separation_grads(
        live_rows(code[part, :owned]),
        [sep[part, d, :owned] for d in range(3)],
        dist[part, :owned],
        ang_grad,
        dist_grad[...],
        env_grad[...],
    )
    for d in range(3):
        sep_grad[d] = grads[d]
    for k, place in enumerate(sz.own):
        rows = [sep_grad[d, pl.ds(k, 1), :] for d in range(3)]
        signed = signed_hot(sz, hot[part, k], atoms_at(sz, atom, part, k).astype(bf16))
        got = nt(signed, stacked_seps(rows))
        add_window(sz, place, got[:, :8] + got[:, 8:], acc_pos)


def signed_hot(sz, one_hot, mask_bf):
    first = 4 * sz.slots
    return jnp.concatenate(
        [one_hot[:first], one_hot[first : first + sz.slots] - mask_bf, one_hot[first + sz.slots :]],
        axis=0,
    )


def fetch(sources, targets, sems):
    copies = [
        pltpu.make_async_copy(source, target, sems.at[k])
        for k, (source, target) in enumerate(zip(sources, targets))
    ]
    for copy in copies:
        copy.start()
    return copies


def block_kernel(sz, kinds, *refs):
    sources, block, held, sems = refs[:6], refs[6], refs[7:13], refs[13]
    for copy in fetch(sources, held, sems):
        copy.wait()
    features, positions, species, neighbours, counts, species_gain = held
    ch, n = sz.channels, sz.slots
    gains = species_gain[...]
    gain_high = gains.astype(bf16).astype(f32)
    rest = gains - gain_high
    gain_middle = rest.astype(bf16).astype(f32)
    parts = [gain_high, gain_middle, rest - gain_middle]
    above, below = jnp.zeros((24, ch), f32), jnp.zeros((8 - kinds, ch), f32)
    parts = [jnp.concatenate([above, part, below], axis=0).astype(bf16) for part in parts]
    kind = lax.broadcasted_iota(jnp.int32, (8, n), 0)
    lane = lax.broadcasted_iota(jnp.int32, (n, code_lane), 1)
    gap = jnp.zeros((5, n), f32)
    for a in range(sz.cols_x):
        sides = []
        for b in range(sz.cols_y):
            atoms = positions[a, :, b, :]
            high = atoms.astype(bf16).astype(f32)
            rest = atoms - high
            middle = rest.astype(bf16).astype(f32)
            chosen = (kind == species[a, pl.ds(b, 1), :]).astype(f32)
            last = jnp.where(kind == 7, counts[a, pl.ds(b, 1), :].astype(f32), chosen)
            rows = [high, gap, middle, gap, rest - middle, gap, last]
            turned = jnp.concatenate(rows, axis=0).T
            picked = jnp.where((lane >= 24) & (lane < 24 + kinds), turned, 0.0).astype(bf16)
            gain = mm(picked, parts[0]) + mm(picked, parts[1]) + mm(picked, parts[2])
            place = jnp.where((lane < 24) | (lane == count_lane), turned, 0.0)
            sides.append(jnp.concatenate([place, neighbours[a, b].astype(f32)], axis=1))
            block[a, b] = (features[a, b].astype(f32) * gain).astype(bf16)
        block[a, sz.cols_y] = jnp.concatenate(sides, axis=1).astype(bf16)


def fill_table(sz, strips, table):
    ch, n = sz.channels, sz.slots
    for a in range(sz.cols_x + 4):
        for k, strip in enumerate(strips):
            meta = strip[a, sz.cols_y].astype(f32)
            for b in range(sz.cols_y):
                row = sz.outer_row(a, k * sz.cols_y + b)
                mine = meta if b == 0 else pltpu.roll(meta, ch - b * 2 * code_lane, 1)
                table[row : row + n, :ch] = strip[a, b]
                table[row : row + n, ch:] = mine.astype(bf16)


def first_kernel(
    sz, before, middle, after, wide_in, wide_out, turned_in, turned_out, mixing, readout,
    energy, back, kept, code, atom, sep, inputs_kept, table,
    hot, xt, angular, dist, env, second, second_xt, second_msg, second_radial,
    second_value, second_slope, ang_grad, dist_grad, env_grad, sep_grad, acc, acc_pos,
):
    ch, n = sz.channels, sz.slots
    owned = len(sz.own)
    fill_table(sz, (before, middle, after), table)
    low, high = bounds_of(sz, table)
    most = jnp.maximum(jnp.max(high).astype(jnp.int32), 1)
    parts = (most + sz.edges - 1) // sz.edges
    in_one, out_one = wide_in[0], wide_out[0]
    code[...] = jnp.full_like(code, -1.0)
    kept[...] = jnp.zeros_like(kept)

    def first_part(part, carry):
        gather_columns(sz, part, table, low, high, code, atom, sep, hot, xt)
        shifted_seps(part, code, sep)
        seps = [sep[part, d] for d in range(3)]
        store_geometry(part, live_rows(code[part]), seps, dist, env, angular)

        def one(cols):
            inputs = [xt[col] for col in cols]
            return layer_forward(
                sz, part, cols, angular, dist, env, atom, in_one, out_one, inputs
            )

        def one_store(col, got):
            kept[col] += got[3]

        loop(sz.inner, 8, one, one_store)
        return carry

    lax.fori_loop(0, parts, first_part, 0)
    rows = [None] * sz.inner
    for col, (a, b) in enumerate(sz.order):
        rows[a * sz.inner_y + b] = invariants(sz, kept[col])
    own_rows = [
        table[(a * sz.outer_y + 1) * n : (a * sz.outer_y + 1 + sz.inner_y) * n, :ch]
        for a in range(1, 1 + sz.inner_x)
    ]
    first_out = three(mm, jnp.concatenate(rows, axis=0), mixing[0])
    inputs_kept[...] = jnp.concatenate(own_rows, axis=0)
    first_out = first_out + inputs_kept[...].astype(f32)
    second[...] = first_out.astype(bf16)

    in_two, out_two = wide_in[1], wide_out[1]
    back_in, back_out = turned_in[1], turned_out[1]
    second_msg[...] = jnp.zeros_like(second_msg)
    every = list(range(owned))

    def second_part(part, carry):
        def second_input(k):
            window = inner_window(sz, second, *sz.own[k])
            return mm(window.astype(f32).T.astype(bf16), hot[part, k])

        inputs = [second_input(k) for k in every]
        got = layer_forward(sz, part, every, angular, dist, env, atom, in_two, out_two, inputs)
        for k, (radial, value, slope, message) in zip(every, got):
            second_xt[part, k], second_radial[part, k] = inputs[k], radial
            second_value[part, k], second_slope[part, k] = value, slope
            second_msg[k] += message
        return carry

    lax.fori_loop(0, parts, second_part, 0)
    inv = jnp.concatenate([invariants(sz, second_msg[k]) for k in every], axis=0)
    own_rows = [
        second[(a * sz.inner_y + 1) * n : (a * sz.inner_y + 1 + sz.cols_y) * n, :]
        for a in range(1, 1 + sz.cols_x)
    ]
    out = three(mm, inv, mixing[1]) + jnp.concatenate(own_rows, axis=0).astype(f32)
    gate = sigmoid(out)
    weights = readout[...]
    total = three(nt, jnp.ones((8, ch), f32), out * gate * weights)
    for k, (a, b) in enumerate(sz.own):
        energy[a - 1, b - 1 : b, :] = total[0:1, k * n : (k + 1) * n]
    out_grad = gate * (1.0 + out * (1.0 - gate)) * weights
    cotangents = three(nt, out_grad, mixing[1])
    acc[...] = jnp.zeros_like(acc)
    acc_pos[...] = jnp.zeros_like(acc_pos)
    for a in range(sz.cols_x):
        first = ((a + 1) * sz.inner_y + 1) * n
        acc[first : first + sz.cols_y * n] = out_grad[a * sz.cols_y * n : (a + 1) * sz.cols_y * n]

    def back_part(part, carry):
        got = layer_backward(
            sz, part, every, angular, dist, atom, back_in, back_out,
            [second_radial[part, k] for k in every],
            jnp.concatenate([second_value[part, k] for k in every], axis=1),
            jnp.concatenate([second_slope[part, k] for k in every], axis=1),
            [second_xt[part, k] for k in every],
            [hot[part, k] for k in every],
            [second_msg[k] for k in every],
            [cotangents[k * n : (k + 1) * n] for k in every],
        )
        for k, value in zip(every, got):
            store_grads(sz, k, value, ang_grad, dist_grad, env_grad, acc)
        own_positions(
            sz, part, code, atom, sep, dist, hot, ang_grad, dist_grad, env_grad, sep_grad, acc_pos
        )
        return carry

    lax.fori_loop(0, parts, back_part, 0)
    for a in range(sz.inner_x):
        places = []
        for b in range(sz.inner_y):
            row = sz.inner_row(a, b)
            back[a, b + (b >= 2)] = acc[row : row + n].astype(bf16)
            full = acc_pos[row : row + n]
            high = full.astype(bf16).astype(f32)
            places += [high, full - high]
        filler = jnp.zeros((n, ch - 16 * sz.inner_y), f32)
        back[a, 2] = jnp.concatenate(places + [filler], axis=1).astype(bf16)


def packed_halo(sz, code, target, place):
    rows = len(sz.halo)
    first = len(sz.own)
    row = lax.broadcasted_iota(jnp.int32, (rows, sz.edges), 0)
    at_x, at_y = jnp.zeros_like(row), jnp.zeros_like(row)
    for h, (a, b) in enumerate(sz.halo):
        at_x, at_y = jnp.where(row == h, a, at_x), jnp.where(row == h, b, at_y)
    shape = (sz.edges, sz.edges)
    before = iota(shape, 0) <= iota(shape, 1)
    above = iota((rows, rows), 1) < iota((rows, rows), 0)
    count = jnp.zeros((1, 1), f32)
    for part in range(2):
        codes = code[part, first:].astype(jnp.int32)
        offset = codes >> 4
        step_x = (offset * 11) >> 5
        to_x = at_x + step_x - 2
        to_y = at_y + offset - 3 * step_x - 2
        inside = (to_x >= 0) & (to_x < sz.cols_x) & (to_y >= 0) & (to_y < sz.cols_y)
        flags = (inside & (codes >= 0)).astype(f32)
        wanted = (to_x * sz.cols_y + to_y) * sz.slots + (codes & 15)
        target[part] = flags * wanted.astype(f32)
        flags_bf = flags.astype(bf16)
        running = mm(flags_bf, before.astype(f32).astype(bf16)) - 1.0
        earlier = jnp.sum(mm(above.astype(f32).astype(bf16), flags_bf), axis=1, keepdims=True)
        place[part] = jnp.where(flags > 0.0, running + earlier + count, -1.0)
        count = count + jnp.sum(jnp.sum(flags, axis=1, keepdims=True), axis=0, keepdims=True)
    return (jnp.max(count).astype(jnp.int32) + sz.edges - 1) // sz.edges


def halo_back(
    sz, part, edge_parts, own_turned, atom, sep, gathered, weights, target, place,
    feature_acc, pos_acc,
):
    in_one, out_one, back_in, back_out = weights
    ch, n, lanes = sz.channels, sz.slots, sz.edges
    first = len(sz.own)
    count = len(sz.halo) * n
    wanted = iota((lanes, lanes), 0) + (part * lanes).astype(f32)
    ones, zeros = jnp.ones((1, lanes), f32), jnp.zeros((2, lanes), f32)

    def packed(edge_part, total):
        picks, sides = [], []
        for h in range(len(sz.halo)):
            pick = place[edge_part, pl.ds(h, 1), :] == wanted
            picks.append(pick.astype(f32).astype(bf16))
            rows = jnp.concatenate(
                [sep[edge_part, d, pl.ds(first + h, 1), :] for d in range(3)]
                + [
                    target[edge_part, pl.ds(h, 1), :],
                    atom[edge_part, pl.ds(first + h, 1), :] + float(h * n),
                    ones,
                    zeros,
                ],
                axis=0,
            )
            high = rows.astype(bf16).astype(f32)
            middle = (rows - high).astype(bf16).astype(f32)
            sides.append(
                jnp.concatenate([high, middle, rows - high - middle], axis=0).astype(bf16)
            )
        return total + nt(jnp.concatenate(sides, axis=1), jnp.concatenate(picks, axis=1))

    got = lax.fori_loop(0, edge_parts, packed, jnp.zeros((24, lanes), f32))
    got = got[0:8] + got[8:16] + got[16:24]
    seps = [got[d : d + 1] for d in range(3)]
    target_row, atom_row, valid = got[3:4], got[4:5], got[5:6]
    dist_row, env_row, angular = geometry(valid, seps)
    weighted, value, slope = hidden_rows(sz, dist_row, env_row, in_one)
    radial = mm(out_one, weighted)
    chosen = iota((first * n, lanes), 0) == target_row
    one_hot = jnp.where(chosen, valid, 0.0).astype(bf16)
    xt = mm(own_turned, one_hot)
    sources = jnp.where(iota((count, lanes), 0) == atom_row, valid, 0.0).astype(bf16)
    spread = mm(gathered[...], sources)
    parts = [spread[m * ch : (m + 1) * ch] for m in range(9)]
    vector = angular[1] * parts[1] + angular[2] * parts[2] + angular[3] * parts[3]
    tensor = angular[4] * parts[4]
    for m in range(5, 9):
        tensor = tensor + angular[m] * parts[m]
    product_grad = jnp.concatenate([parts[0], vector, tensor], axis=0)
    _, radial_grad, input_grad = radial_products(sz, product_grad, radial, xt)
    products = [radial[l * ch : (l + 1) * ch] * xt for l in range(3)]
    ang_grad = [None] + [
        jnp.sum(parts[m] * products[1 if m < 4 else 2], axis=0, keepdims=True)
        for m in range(1, 9)
    ]
    dist_grad, env_grad = radial_backward(
        sz, dist_row, radial_grad, value, slope, back_in, back_out
    )
    grads = separation_grads(valid, seps, dist_row, ang_grad, dist_grad, env_grad)
    feature_acc[...] += nt(one_hot, input_grad)
    got = nt(one_hot, stacked_seps(list(grads)))
    pos_acc[...] += got[:, :8] + got[:, 8:]


def second_kernel(
    sz, total, before, after, kept, code, atom, sep, table,
    wide_in, wide_out, turned_in, turned_out, mixing,
    feature_grad, forces,
    hot, xt, angular, dist, env, ang_grad, dist_grad, env_grad, sep_grad,
    acc, acc_pos, halo_acc, halo_pos, target, place, gathered,
):
    ch, n = sz.channels, sz.slots
    cells = []
    for a in range(sz.inner_x):
        for b in range(sz.inner_y):
            far = before[a, b + 1] if b < 2 else after[a, b - 2]
            cells.append(total[a, b + (b >= 2)] + far.astype(f32))
    cotangent = jnp.concatenate(cells, axis=0)
    inv = three(nt, cotangent, mixing[0])
    halo_parts = packed_halo(sz, code, target, place)
    second_used = (jnp.max(code[1]) >= 0.0).astype(jnp.int32)
    edge_parts = 1 + second_used
    in_one, out_one = wide_in[0], wide_out[0]
    back_in, back_out = turned_in[0], turned_out[0]
    owned = len(sz.own)
    every = list(range(owned))
    index = iota((sz.window, sz.edges), 0)
    acc[...] = jnp.zeros_like(acc)
    acc_pos[...] = jnp.zeros_like(acc_pos)
    halo_acc[...] = jnp.zeros_like(halo_acc)
    halo_pos[...] = jnp.zeros_like(halo_pos)

    def inv_rows(a, b):
        row = sz.inner_row(a, b)
        return inv[row : row + n]

    turned = [inner_window(sz, table, a, b).astype(f32).T.astype(bf16) for a, b in sz.own]

    def back_part(part, carry):
        seps = [sep[part, d, :owned] for d in range(3)]
        store_geometry(part, live_rows(code[part, :owned]), seps, dist, env, angular)
        hots = [
            (index == code[part, pl.ds(k, 1), :]).astype(f32).astype(bf16) for k in every
        ]
        for k in every:
            hot[part, k] = hots[k]
        rows = [
            jnp.concatenate([ref[part, pl.ds(k, 1), :] for k in every], axis=1)
            for ref in (dist, env)
        ]
        weighted, value, slope = hidden_rows(sz, *rows, in_one)
        radials = mm(out_one, weighted)
        got = layer_backward(
            sz, part, every, angular, dist, atom, back_in, back_out,
            [radials[:, k * sz.edges : (k + 1) * sz.edges] for k in every],
            value, slope,
            [mm(turned[k], hots[k]) for k in every],
            hots,
            [kept[k] for k in every],
            [inv_rows(*sz.own[k]) for k in every],
        )
        for k, value in zip(every, got):
            store_grads(sz, k, value, ang_grad, dist_grad, env_grad, acc)
        own_positions(
            sz, part, code, atom, sep, dist, hot, ang_grad, dist_grad, env_grad, sep_grad, acc_pos
        )
        return carry

    lax.fori_loop(0, edge_parts, back_part, 0)
    halo_grads = [
        message_grads(sz, kept[owned + h], inv_rows(a, b)) for h, (a, b) in enumerate(sz.halo)
    ]
    for m in range(9):
        rows = jnp.concatenate([grads[m] for grads in halo_grads], axis=0)
        gathered[m * ch : (m + 1) * ch, :] = rows.T.astype(bf16)
    own_rows = [
        table[sz.inner_row(a + 1, 1) : sz.inner_row(a + 1, 1) + sz.cols_y * n, :]
        for a in range(sz.cols_x)
    ]
    own_turned = jnp.concatenate(own_rows, axis=0).astype(f32).T.astype(bf16)
    weights = (in_one, out_one, back_in, back_out)

    def halo_part(part, carry):
        halo_back(
            sz, part, edge_parts, own_turned, atom, sep, gathered, weights, target, place,
            halo_acc, halo_pos,
        )
        return carry

    lax.fori_loop(0, halo_parts, halo_part, 0)
    for a in range(sz.cols_x):
        inner = sz.inner_row(a + 1, 1)
        rows = sz.cols_y * n
        mine = slice(a * rows, (a + 1) * rows)
        feature_grad[mine] = (
            acc[inner : inner + rows] + cotangent[inner : inner + rows] + halo_acc[mine]
        )
        moved = acc_pos[inner : inner + rows] + halo_pos[mine]
        for b in range(sz.cols_y):
            lane = 16 * (b + 1)
            far, start = (before[a + 1, 0], 16 * (b + 3)) if b < 1 else (after[a + 1, 2], 16 * (b - 1))
            both = total[a + 1, 2][:, lane : lane + 16]
            both = both + far.astype(f32)[:, start : start + 16]
            place_grad = moved[b * n : (b + 1) * n] + both[:, :8] + both[:, 8:]
            forces[a, :, b, :] = -(place_grad.T)[:3]


def ring(axis):
    devices = lax.axis_size(axis)
    up = [(i, (i + 1) % devices) for i in range(devices)]
    return up, [(j, i) for i, j in up]


def both_ways(first, last, axis):
    up, down = ring(axis)
    return lax.ppermute(last, axis, up), lax.ppermute(first, axis, down)


def shards(
    features, positions, species, neighbours, counts, species_gain, radial_in, radial_out, mixing, readout
):
    cols_x, cols_y, slots, channels = features.shape
    neigh = neighbours.shape[-1]
    basis, hidden = radial_in.shape[1:]
    sz = Sizes(cols_x, cols_y, slots, neigh, channels, basis, hidden)
    vmem = pl.BlockSpec(memory_space=pltpu.VMEM)
    in_hbm = pl.BlockSpec(memory_space=pltpu.HBM)
    params = pltpu.CompilerParams(vmem_limit_bytes=40 * 1024 * 1024)
    given = (features, positions.transpose(0, 2, 1, 3), species, neighbours, counts, species_gain)
    block = pl.pallas_call(
        functools.partial(block_kernel, sz, species_gain.shape[0]),
        out_shape=jax.ShapeDtypeStruct((cols_x, cols_y + 1, slots, channels), bf16),
        in_specs=[in_hbm] * 6,
        out_specs=vmem,
        scratch_shapes=[pltpu.VMEM(x.shape, x.dtype) for x in given]
        + [pltpu.SemaphoreType.DMA((6,))],
        compiler_params=pltpu.CompilerParams(vmem_limit_bytes=60 * 1024 * 1024),
        name="block_of_atoms",
    )(*given)
    assert cols_x == 2 and cols_y == 2
    before, after = both_ways(block, block, "gx")
    middle = jnp.concatenate([before, block, after], axis=0)
    before, after = both_ways(middle, middle, "gy")

    inner_atoms = sz.inner * slots
    owned = cols_x * cols_y
    edges = sz.edges
    columns = sz.inner
    grads = [
        pltpu.VMEM((9, owned, edges), f32),
        pltpu.VMEM((owned, edges), f32),
        pltpu.VMEM((owned, edges), f32),
        pltpu.VMEM((3, owned, edges), f32),
    ]
    weights = prepared(radial_in, radial_out, mixing)
    assert slots * neigh <= 2 * edges
    kept_shapes = [
        (columns, sz.window, channels),
        (2, columns, edges),
        (2, columns, edges),
        (2, 3, columns, edges),
    ]

    def edge_scratch(count):
        return [
            pltpu.VMEM((2, owned, sz.window, edges), bf16),
            pltpu.VMEM((count, channels, edges), f32),
            pltpu.VMEM((2, 9, count, edges), f32),
            pltpu.VMEM((2, count, edges), f32),
            pltpu.VMEM((2, count, edges), f32),
        ]

    energy, back, *kept = pl.pallas_call(
        functools.partial(first_kernel, sz),
        out_shape=[
            jax.ShapeDtypeStruct((cols_x, cols_y, slots), f32),
            jax.ShapeDtypeStruct((sz.inner_x, sz.inner_y + 1, slots, channels), bf16),
        ]
        + [jax.ShapeDtypeStruct(shape, f32) for shape in kept_shapes]
        + [jax.ShapeDtypeStruct((inner_atoms, channels), bf16)],
        in_specs=[vmem] * 9,
        out_specs=[vmem] * 7,
        scratch_shapes=[pltpu.VMEM(((cols_x + 4) * (cols_y + 4) * slots, 2 * channels), bf16)]
        + edge_scratch(columns)
        + [
            pltpu.VMEM((inner_atoms, channels), bf16),
            pltpu.VMEM((2, owned, channels, edges), f32),
            pltpu.VMEM((owned, sz.window, channels), f32),
            pltpu.VMEM((2, owned, 3 * channels, edges), f32),
            pltpu.VMEM((2, owned, hidden, edges), f32),
            pltpu.VMEM((2, owned, hidden, edges), f32),
        ]
        + grads
        + [pltpu.VMEM((inner_atoms, channels), f32), pltpu.VMEM((inner_atoms, 8), f32)],
        compiler_params=params,
        name="forward_and_second_back",
    )(before, middle, after, *weights, readout.reshape(1, -1))

    far = both_ways(back[:2], back[2:], "gx")
    total = back.astype(f32) + jnp.concatenate(far, axis=0).astype(f32)
    sent = total.astype(bf16)
    far = both_ways(sent[:, :3], sent[:, 2:], "gy")
    feature_grad, forces = pl.pallas_call(
        functools.partial(second_kernel, sz),
        out_shape=(
            jax.ShapeDtypeStruct((owned * slots, channels), f32),
            jax.ShapeDtypeStruct((cols_x, 3, cols_y, slots), f32),
        ),
        in_specs=[vmem] * 13,
        out_specs=(vmem,) * 2,
        scratch_shapes=edge_scratch(owned)
        + grads
        + [
            pltpu.VMEM((rows, width), f32)
            for rows in (inner_atoms, owned * slots)
            for width in (channels, 8)
        ]
        + [
            pltpu.VMEM((2, len(sz.halo), edges), f32),
            pltpu.VMEM((2, len(sz.halo), edges), f32),
            pltpu.VMEM((9 * channels, len(sz.halo) * slots), bf16),
        ],
        compiler_params=params,
        name="first_back",
    )(total, *far, *kept, *weights)
    return (
        energy,
        forces.transpose(0, 2, 1, 3),
        feature_grad.reshape(cols_x, cols_y, slots, channels),
    )


def solution(mesh):
    placed = (
        P("gx", "gy", None, None),
        P("gx", "gy", None, None),
        P("gx", "gy", None),
        P("gx", "gy", None, None),
        P("gx", "gy", None),
        P(),
        P(),
        P(),
        P(),
        P(),
    )
    return jax.shard_map(
        shards,
        mesh=mesh,
        in_specs=placed,
        out_specs=(P("gx", "gy", None), P("gx", "gy", None, None), P("gx", "gy", None, None)),
        check_vma=False,
    )
```

```python
import functools

import jax
import jax.numpy as jnp
from jax import lax
from jax.experimental import pallas as pl
from jax.experimental.pallas import tpu as pltpu
from jax.sharding import PartitionSpec as P

column = 6.0
cutoff = 6.0
softening = 0.01
root_three = 3.0**0.5
f32 = jnp.float32
bf16 = jnp.bfloat16
code_lane = 32
count_lane = 31
part_lanes = 256


def mm(a, b):
    return lax.dot_general(a, b, (((1,), (0,)), ((), ())), preferred_element_type=f32)


def nt(a, b):
    return lax.dot_general(a, b, (((1,), (1,)), ((), ())), preferred_element_type=f32)


def split(x):
    high = x.astype(bf16)
    return high, (x - high.astype(f32)).astype(bf16)


def three(product, a, b):
    a_high, a_low = split(a)
    b_high, b_low = split(b) if b.dtype == f32 else (b[0], b[1])
    return product(a_high, b_high) + product(a_low, b_high) + product(a_high, b_low)


def parted(x):
    high = lax.reduce_precision(x, 8, 7)
    return high, x - high


def prepared(radial_in, radial_out, mixing):
    high, low = parted(radial_in)
    turned = jnp.concatenate([high, high, low, jnp.zeros_like(high)], axis=1).swapaxes(1, 2)
    back_in = jnp.concatenate([high, low], axis=1)
    high, low = parted(radial_out)
    wide = jnp.concatenate([high, high, low], axis=1).swapaxes(1, 2)
    high_mix, low_mix = parted(mixing)
    mix = jnp.stack([high_mix, low_mix], axis=1)
    return [x.astype(bf16) for x in (turned, wide, back_in, high, mix)]


def harmonic_rows(ux, uy, uz):
    square = ux * ux + uy * uy + uz * uz
    return [
        jnp.ones_like(ux),
        ux,
        uy,
        uz,
        root_three * ux * uy,
        root_three * uy * uz,
        0.5 * (3.0 * uz * uz - square),
        root_three * ux * uz,
        0.5 * root_three * (ux * ux - uy * uy),
    ]


class Sizes:
    def __init__(self, cols_x, cols_y, slots, neigh, channels, basis, hidden):
        self.cols_x, self.cols_y = cols_x, cols_y
        self.slots, self.neigh, self.channels = slots, neigh, channels
        self.basis, self.hidden = basis, hidden
        self.inner_x, self.inner_y = cols_x + 2, cols_y + 2
        self.outer_y = cols_y + 4
        self.inner = self.inner_x * self.inner_y
        self.edges = part_lanes
        self.window = 9 * slots

        cells = [(a, b) for a in range(self.inner_x) for b in range(self.inner_y)]
        self.own = [c for c in cells if self.is_own(*c)]
        last = self.inner_x - 1
        self.halo = [c for c in cells if c[0] in (0, last)]
        self.halo += [(a, b) for b in (0, self.inner_y - 1) for a in range(1, last)]
        self.order = self.own + self.halo

    def is_own(self, a, b):
        return 1 <= a <= self.cols_x and 1 <= b <= self.cols_y

    def outer_row(self, a, b):
        return (a * self.outer_y + b) * self.slots

    def inner_row(self, a, b):
        return (a * self.inner_y + b) * self.slots


def each(compute):
    return lambda items: [compute(item) for item in items]


def run_steps(*steps):
    steps = list(steps)
    while steps:
        for step in list(steps):
            try:
                next(step)
            except StopIteration:
                steps.remove(step)


def loop(count, group, compute, store):
    for first in range(0, count, group):
        items = list(range(first, min(first + group, count)))
        for item, value in zip(items, compute(items)):
            store(item, value)


def iota(shape, dim):
    return lax.broadcasted_iota(jnp.int32, shape, dim).astype(f32)


def bounds_of(sz, table):
    n, ch = sz.slots, sz.channels
    rows = [sz.outer_row(a + 1, b + 1) for a, b in sz.order]
    metas = jnp.concatenate([table[row : row + n, ch:] for row in rows], axis=0)
    shape = (sz.inner * n, sz.inner * n)
    left = lax.broadcasted_iota(jnp.int32, shape, 0)
    right = lax.broadcasted_iota(jnp.int32, shape, 1)
    earlier = (left // n == right // n) & (right < left)
    sums = mm(earlier.astype(f32).astype(bf16), metas)
    low = sums[:, count_lane : count_lane + 1]
    return low, low + metas[:, count_lane : count_lane + 1].astype(f32)


def gather_columns(sz, part, table, low, high, code, atom, sep, xt):
    ch, n, edges = sz.channels, sz.slots, sz.edges
    lane = iota((n, edges), 1) + (part * edges).astype(f32)
    row = iota((n, edges), 0)
    slot = iota((sz.neigh, 2 * edges), 0)
    second = (lax.broadcasted_iota(jnp.int32, (1, 2 * edges), 1) >= edges).astype(f32)
    target = iota((12 * n, 2 * edges), 0)
    empty = jnp.zeros((n, edges), f32)

    firsts = list(range(0, sz.inner, 2))
    ats, valids, which, atoms, spreads = [], [], [], [], []
    for col, (a, b) in enumerate(sz.order):
        mine = slice(col * n, (col + 1) * n)
        at = ((lane >= low[mine]) & (lane < high[mine])).astype(f32)
        ats.append(at)
        valids.append(jnp.sum(at, axis=0, keepdims=True) - 1.0)
        which.append(lane[:1] - jnp.sum(at * low[mine], axis=0, keepdims=True))
        atoms.append(jnp.sum(at * row, axis=0, keepdims=True) + valids[-1])
    for first in firsts:
        places = [sz.outer_row(a + 1, b + 1) for a, b in sz.order[first : first + 2]]
        metas = [table[place : place + n, ch : 2 * ch] for place in places]
        turned = jnp.concatenate(metas, axis=0).astype(f32).T[: 2 * code_lane].astype(bf16)
        apart = jnp.concatenate(
            [
                jnp.concatenate([ats[first], empty], axis=1),
                jnp.concatenate([empty, ats[first + 1]], axis=1),
            ],
            axis=0,
        )
        spreads.append(mm(turned, apart.astype(bf16)))
    hots, windows, codes_of = [], [], []
    for first, spread in zip(firsts, spreads):
        (a, b), (_, other_b) = sz.order[first : first + 2]
        both = jnp.concatenate(which[first : first + 2], axis=1)
        picked = jnp.where(slot == both, spread[code_lane:], 0.0)
        codes = jnp.sum(picked, axis=0, keepdims=True)
        codes = codes + jnp.concatenate(valids[first : first + 2], axis=1)
        if other_b != b:
            width, height = 4, 3
            ahead = (codes >= 3.0 * n).astype(f32) + (codes >= 6.0 * n).astype(f32)
            rows = codes + n * (ahead + second)
        else:
            width, height = 3, 4
            rows = codes + 3.0 * n * second
        rows = jnp.where(codes < 0.0, -1.0, rows)
        hots.append((target == rows).astype(f32).astype(bf16))
        window = jnp.concatenate(
            [table[pl.ds(sz.outer_row(a + d, b), width * n), :] for d in range(height)], axis=0
        )
        windows.append(window.astype(f32).T.astype(bf16)[: ch + 32])
        codes_of.append(codes)
    founds = [mm(window, one_hot) for window, one_hot in zip(windows, hots)]
    for first, spread, codes, found in zip(firsts, spreads, codes_of, founds):
        diff = found[ch : ch + 24] - spread[:24]
        total = diff[0:8] + diff[8:16] + diff[16:24]
        for col, span in ((first, slice(0, edges)), (first + 1, slice(edges, 2 * edges))):
            code[part, pl.ds(col, 1), :] = codes[:, span]
            atom[part, pl.ds(col, 1), :] = atoms[col]
            xt[col] = found[:ch, span]
            for d in range(3):
                sep[part, d, pl.ds(col, 1), :] = total[d : d + 1, span]


def wide_rows(rows):
    return jnp.concatenate([rows[k : k + 1] for k in range(rows.shape[0])], axis=1)


def own_hot(sz, codes):
    row = lax.broadcasted_iota(jnp.int32, codes.shape, 0)
    place = jnp.zeros_like(row)
    for k, (a, b) in enumerate(sz.own):
        place = jnp.where(row == k, sz.inner_row(a - 1, b - 1), place)
    whole = codes.astype(jnp.int32)
    ahead = (((whole >> 4) * 11) >> 5) * (sz.slots * (sz.inner_y - 3))
    rows = jnp.where(codes < 0.0, -1.0, (place + whole + ahead).astype(f32))
    wide = wide_rows(rows)
    return (iota((sz.inner * sz.slots, wide.shape[1]), 0) == wide).astype(f32).astype(bf16)


def own_atoms(sz, atoms):
    row = iota(atoms.shape, 0)
    wide = wide_rows(jnp.where(atoms < 0.0, -1.0, atoms + row * float(sz.slots)))
    return (iota((len(sz.own) * sz.slots, wide.shape[1]), 0) == wide).astype(f32).astype(bf16)


def shifted_seps(part, code, sep):
    offset = code[part].astype(jnp.int32) >> 4
    step_x = (offset * 11) >> 5
    step_y = offset - 3 * step_x
    sep[part, 0] = sep[part, 0] + column * (step_x - 1).astype(f32)
    sep[part, 1] = sep[part, 1] + column * (step_y - 1).astype(f32)


def geometry(live, seps):
    sep_x, sep_y, sep_z = seps
    dist_sq = sep_x * sep_x + sep_y * sep_y + sep_z * sep_z
    env = jnp.square(jnp.maximum(1.0 - dist_sq / (cutoff * cutoff), 0.0)) * live
    rows = harmonic_rows(sep_x / cutoff, sep_y / cutoff, sep_z / cutoff)
    return jnp.sqrt(dist_sq + softening), env, rows


def store_geometry(part, live, seps, dist, env, angular):
    dist[part], env[part], rows = geometry(live, seps)
    for m, row in enumerate(rows):
        angular[part, m] = row


def live_rows(code):
    return (code >= 0.0).astype(f32)


def basis_rows(sz, dist_row):
    width = dist_row.shape[1]
    spacing = cutoff / (sz.basis - 1)
    centre = lax.broadcasted_iota(jnp.int32, (sz.basis, width), 0).astype(f32) * spacing
    shifted = (dist_row - centre) * (1.0 / spacing)
    return jnp.exp(-shifted * shifted), shifted


def sigmoid(x):
    return 0.5 * jnp.tanh(0.5 * x) + 0.5


def hidden_rows(sz, dist_row, env_row, weight_in):
    basis, _ = basis_rows(sz, dist_row)
    high = basis.astype(bf16).astype(f32)
    stacked = jnp.concatenate([high, basis - high, high, jnp.zeros_like(high)], axis=0)
    pre = mm(weight_in, stacked.astype(bf16))
    gate = sigmoid(pre)
    value = pre * gate
    weighted = value * env_row
    high, low = split(weighted)
    slope = gate * (1.0 + pre * (1.0 - gate)) * env_row
    return jnp.concatenate([high, low, high], axis=0), value, slope


def atoms_at(sz, atom, part, col):
    return (iota((sz.slots, sz.edges), 0) == atom[part, pl.ds(col, 1), :]).astype(f32)


def block_rows(angular, part, col, at):
    return [angular[part, m, pl.ds(col, 1), :] * at for m in range(1, 9)]


def layer_forward(sz, part, cols, angular, dist, env, atom, weight_in, weight_out, inputs):
    rows = [jnp.concatenate([ref[part, pl.ds(c, 1), :] for c in cols], axis=1) for ref in (dist, env)]
    weighted, value, slope = hidden_rows(sz, *rows, weight_in)
    radials = mm(weight_out, weighted)
    spans = [slice(k * sz.edges, (k + 1) * sz.edges) for k in range(len(cols))]
    sides = [message_sides(sz, part, col, angular, atom) for col in cols]
    products = [
        (radials[:, span] * jnp.concatenate([xt] * 3, axis=0)).astype(bf16)
        for span, xt in zip(spans, inputs)
    ]
    ch = sz.channels
    got = [
        [nt(both, product[l * ch : (l + 1) * ch]) for l, both in enumerate(side)]
        for side, product in zip(sides, products)
    ]
    out = []
    for span, parts in zip(spans, got):
        halves = [len(x) // 2 for x in parts]
        rows = [parts[0]] + [x[:h] + x[h:] for x, h in zip(parts[1:], halves[1:])]
        message = jnp.concatenate(rows, axis=0)
        out.append((radials[:, span], value[:, span], slope[:, span], message))
    return out


def message_sides(sz, part, col, angular, atom):
    n = sz.slots
    at = atoms_at(sz, atom, part, col)
    blocks = jnp.concatenate(block_rows(angular, part, col, at), axis=0)
    high = blocks.astype(bf16).astype(f32)
    low = blocks - high
    sides = [at.astype(bf16)]
    for rows in (slice(0, 3 * n), slice(3 * n, 8 * n)):
        sides.append(jnp.concatenate([high[rows], low[rows]], axis=0).astype(bf16))
    return sides


def invariants(sz, message):
    n = sz.slots
    squares = message * message
    got = [squares[m * n : (m + 1) * n] for m in range(9)]
    return jnp.concatenate(
        [message[:n], got[1] + got[2] + got[3], got[4] + got[5] + got[6] + got[7] + got[8]],
        axis=1,
    )


def message_grads(sz, message, cotangent):
    ch, n = sz.channels, sz.slots
    twice = 2.0 * cotangent[:, ch:]
    parts = [
        message[m * n : (m + 1) * n] * (twice[:, :ch] if m < 4 else twice[:, ch:])
        for m in range(1, 9)
    ]
    return [cotangent[:, :ch]] + parts


def radial_products(sz, product_grad, radial, xt):
    ch = sz.channels
    products, mine, input_grad = [], [], None
    for l in range(3):
        grad, part = product_grad[l * ch : (l + 1) * ch], radial[l * ch : (l + 1) * ch]
        if l:
            products.append((part * xt).astype(bf16))
        mine.append((grad * xt).astype(bf16))
        term = grad * part
        input_grad = term if input_grad is None else input_grad + term
    return products, jnp.concatenate(mine, axis=0), input_grad.astype(bf16)


def radial_backward(sz, dist_row, radial_grad, value, slope, back_in, back_out):
    weighted_grad = mm(back_out, radial_grad)
    env_row_grad = jnp.sum(weighted_grad * value, axis=0, keepdims=True)
    both = mm(back_in, (weighted_grad * slope).astype(bf16))
    basis_grad = both[: sz.basis] + both[sz.basis : 2 * sz.basis]
    basis, shifted = basis_rows(sz, dist_row)
    spacing = cutoff / (sz.basis - 1)
    dist_row_grad = jnp.sum(
        basis_grad * basis * shifted * (-2.0 / spacing), axis=0, keepdims=True
    )
    return dist_row_grad, env_row_grad


def layer_backward(
    sz, part, cols, angular, dist, atom, back_in, back_out, radials, value, slope, inputs,
    messages, cotangents,
):
    ch, n = sz.channels, sz.slots
    ats = [atoms_at(sz, atom, part, col) for col in cols]
    grads_of = [message_grads(sz, *both) for both in zip(messages, cotangents)]
    lhs = []
    for grads in grads_of:
        turned = jnp.concatenate(grads, axis=0).T
        lane = lax.broadcasted_iota(jnp.int32, turned.shape, 1)
        lhs.append(
            jnp.concatenate(
                [
                    jnp.where(lane < n, turned, 0.0),
                    jnp.where((lane >= n) & (lane < 4 * n), turned, 0.0),
                    jnp.where(lane >= 4 * n, turned, 0.0),
                ],
                axis=0,
            ).astype(bf16)
        )
    blocks = [
        jnp.concatenate([at] + block_rows(angular, part, col, at), axis=0).astype(bf16)
        for col, at in zip(cols, ats)
    ]
    yield
    product_grads = [mm(left, right) for left, right in zip(lhs, blocks)]
    yield
    triples = [
        radial_products(sz, *three_of) for three_of in zip(product_grads, radials, inputs)
    ]
    mine = [triple[1] for triple in triples]
    input_grads = [triple[2] for triple in triples]
    yield
    empty = jnp.zeros((n, ch), f32)
    wides = []
    for grads in grads_of:
        wide = [
            jnp.concatenate([g, empty] if m < 3 else [empty, g], axis=1)
            for m, g in enumerate(grads[1:])
        ]
        wides.append(jnp.concatenate(wide, axis=0).astype(bf16))
    gots = [
        mm(wide, jnp.concatenate(triple[0], axis=0)) for wide, triple in zip(wides, triples)
    ]
    yield
    ang_grads = [
        [jnp.sum(got[m * n : (m + 1) * n] * at, axis=0, keepdims=True) for m in range(8)]
        for got, at in zip(gots, ats)
    ]
    dist_row = jnp.concatenate([dist[part, pl.ds(col, 1), :] for col in cols], axis=1)
    dist_row_grad, env_row_grad = radial_backward(
        sz, dist_row, jnp.concatenate(mine, axis=1), value, slope, back_in, back_out
    )
    out = []
    for k in range(len(cols)):
        span = slice(k * sz.edges, (k + 1) * sz.edges)
        out.append((ang_grads[k], dist_row_grad[:, span], env_row_grad[:, span]))
    yield
    return jnp.concatenate(input_grads, axis=1), out


def store_grads(sz, col, value, ang_grad, dist_grad, env_grad):
    ang_grads, dist_row_grad, env_row_grad = value
    for m in range(8):
        ang_grad[m + 1, pl.ds(col, 1), :] = ang_grads[m]
    dist_grad[pl.ds(col, 1), :] = dist_row_grad
    env_grad[pl.ds(col, 1), :] = env_row_grad


def separation_grads(live, sep, dist, ang_grad, dist_grad, env_grad):
    sep_x, sep_y, sep_z = sep
    ux, uy, uz = sep_x / cutoff, sep_y / cutoff, sep_z / cutoff
    dist_sq = sep_x * sep_x + sep_y * sep_y + sep_z * sep_z
    inside = jnp.maximum(1.0 - dist_sq / (cutoff * cutoff), 0.0)
    sq_grad = dist_grad * (0.5 / dist) - env_grad * live * inside * (2.0 / (cutoff * cutoff))
    g = ang_grad
    r3 = root_three
    grad_x = g[1] + r3 * (uy * g[4] + uz * g[7] + ux * g[8]) - ux * g[6]
    grad_y = g[2] + r3 * (ux * g[4] + uz * g[5] - uy * g[8]) - uy * g[6]
    grad_z = g[3] + r3 * (uy * g[5] + ux * g[7]) + 2.0 * uz * g[6]
    return (
        2.0 * sep_x * sq_grad + grad_x / cutoff,
        2.0 * sep_y * sq_grad + grad_y / cutoff,
        2.0 * sep_z * sq_grad + grad_z / cutoff,
    )


def stacked_seps(rows):
    full = jnp.concatenate(rows + [jnp.zeros((5, rows[0].shape[1]), f32)], axis=0)
    high = full.astype(bf16).astype(f32)
    return jnp.concatenate([high, full - high], axis=0).astype(bf16)


def own_positions(sz, part, code, atom, sep, dist, hot, ang_grad, dist_grad, env_grad, acc_pos):
    owned, n = len(sz.own), sz.slots
    grads = separation_grads(
        live_rows(code[part, :owned]),
        [sep[part, d, :owned] for d in range(3)],
        dist[part, :owned],
        ang_grad,
        dist_grad[...],
        env_grad[...],
    )
    ends = jnp.concatenate([hot, own_atoms(sz, atom[part, :owned])], axis=0)
    got = nt(ends, stacked_seps([wide_rows(grad) for grad in grads]))
    got = got[:, :8] + got[:, 8:]
    atoms = sz.inner * n
    acc_pos[...] += got[:atoms]
    for k, (a, b) in enumerate(sz.own):
        row = sz.inner_row(a, b)
        acc_pos[row : row + n] -= got[atoms + k * n : atoms + (k + 1) * n]


def fetch(sources, targets, sems):
    copies = [
        pltpu.make_async_copy(source, target, sems.at[k])
        for k, (source, target) in enumerate(zip(sources, targets))
    ]
    for copy in copies:
        copy.start()
    return copies


def block_kernel(sz, kinds, *refs):
    sources, block, held, sems = refs[:6], refs[6], refs[7:13], refs[13]
    for copy in fetch(sources, held, sems):
        copy.wait()
    features, positions, species, neighbours, counts, species_gain = held
    ch, n = sz.channels, sz.slots
    gains = species_gain[...]
    gain_high = gains.astype(bf16).astype(f32)
    rest = gains - gain_high
    gain_middle = rest.astype(bf16).astype(f32)
    parts = [gain_high, gain_middle, rest - gain_middle]
    above, below = jnp.zeros((24, ch), f32), jnp.zeros((8 - kinds, ch), f32)
    parts = [jnp.concatenate([above, part, below], axis=0).astype(bf16) for part in parts]
    kind = lax.broadcasted_iota(jnp.int32, (8, n), 0)
    lane = lax.broadcasted_iota(jnp.int32, (n, code_lane), 1)
    gap = jnp.zeros((5, n), f32)
    for a in range(sz.cols_x):
        sides = []
        for b in range(sz.cols_y):
            atoms = positions[a, :, b, :]
            high = atoms.astype(bf16).astype(f32)
            rest = atoms - high
            middle = rest.astype(bf16).astype(f32)
            chosen = (kind == species[a, pl.ds(b, 1), :]).astype(f32)
            last = jnp.where(kind == 7, counts[a, pl.ds(b, 1), :].astype(f32), chosen)
            rows = [high, gap, middle, gap, rest - middle, gap, last]
            turned = jnp.concatenate(rows, axis=0).T
            picked = jnp.where((lane >= 24) & (lane < 24 + kinds), turned, 0.0).astype(bf16)
            gain = mm(picked, parts[0]) + mm(picked, parts[1]) + mm(picked, parts[2])
            place = jnp.where((lane < 24) | (lane == count_lane), turned, 0.0)
            sides.append(jnp.concatenate([place, neighbours[a, b].astype(f32)], axis=1))
            block[a, b] = (features[a, b].astype(f32) * gain).astype(bf16)
        block[a, sz.cols_y] = jnp.concatenate(sides, axis=1).astype(bf16)


def fill_table(sz, strips, table):
    ch, n = sz.channels, sz.slots
    for a in range(sz.cols_x + 4):
        for k, strip in enumerate(strips):
            meta = strip[a, sz.cols_y].astype(f32)
            for b in range(sz.cols_y):
                row = sz.outer_row(a, k * sz.cols_y + b)
                mine = meta if b == 0 else pltpu.roll(meta, ch - b * 2 * code_lane, 1)
                table[row : row + n, :ch] = strip[a, b]
                table[row : row + n, ch:] = mine.astype(bf16)


def first_kernel(
    sz, before, middle, after, wide_in, wide_out, turned_in, turned_out, mixing, readout,
    energy, back, kept, code, atom, sep, inputs_kept, table,
    hot, xt, angular, dist, env, second, second_xt, second_msg, second_radial,
    second_value, second_slope, ang_grad, dist_grad, env_grad, acc, acc_pos,
):
    ch, n = sz.channels, sz.slots
    owned = len(sz.own)
    fill_table(sz, (before, middle, after), table)
    low, high = bounds_of(sz, table)
    most = jnp.maximum(jnp.max(high).astype(jnp.int32), 1)
    parts = (most + sz.edges - 1) // sz.edges
    in_one, out_one = wide_in[0], wide_out[0]
    code[...] = jnp.full_like(code, -1.0)
    kept[...] = jnp.zeros_like(kept)

    def first_part(part, carry):
        gather_columns(sz, part, table, low, high, code, atom, sep, xt)
        shifted_seps(part, code, sep)
        seps = [sep[part, d] for d in range(3)]
        store_geometry(part, live_rows(code[part]), seps, dist, env, angular)

        def one(cols):
            inputs = [xt[col] for col in cols]
            return layer_forward(
                sz, part, cols, angular, dist, env, atom, in_one, out_one, inputs
            )

        def one_store(col, got):
            kept[col] += got[3]

        loop(sz.inner, 8, one, one_store)
        return carry

    lax.fori_loop(0, parts, first_part, 0)
    rows = [None] * sz.inner
    for col, (a, b) in enumerate(sz.order):
        rows[a * sz.inner_y + b] = invariants(sz, kept[col])
    own_rows = [
        table[(a * sz.outer_y + 1) * n : (a * sz.outer_y + 1 + sz.inner_y) * n, :ch]
        for a in range(1, 1 + sz.inner_x)
    ]
    first_out = three(mm, jnp.concatenate(rows, axis=0), mixing[0])
    inputs_kept[...] = jnp.concatenate(own_rows, axis=0)
    first_out = first_out + inputs_kept[...].astype(f32)
    second[...] = first_out.astype(bf16)

    in_two, out_two = wide_in[1], wide_out[1]
    back_in, back_out = turned_in[1], turned_out[1]
    second_msg[...] = jnp.zeros_like(second_msg)
    second_turned = second[...].astype(f32).T.astype(bf16)
    every = list(range(owned))

    def second_part(part, carry):
        one_hot = own_hot(sz, code[part, :owned])
        hot[part] = one_hot
        found = mm(second_turned, one_hot)
        inputs = [found[:, k * sz.edges : (k + 1) * sz.edges] for k in every]
        got = layer_forward(sz, part, every, angular, dist, env, atom, in_two, out_two, inputs)
        for k, (radial, value, slope, message) in zip(every, got):
            second_xt[part, k], second_radial[part, k] = inputs[k], radial
            second_value[part, k], second_slope[part, k] = value, slope
            second_msg[k] += message
        return carry

    lax.fori_loop(0, parts, second_part, 0)
    inv = jnp.concatenate([invariants(sz, second_msg[k]) for k in every], axis=0)
    own_rows = [
        second[(a * sz.inner_y + 1) * n : (a * sz.inner_y + 1 + sz.cols_y) * n, :]
        for a in range(1, 1 + sz.cols_x)
    ]
    out = three(mm, inv, mixing[1]) + jnp.concatenate(own_rows, axis=0).astype(f32)
    gate = sigmoid(out)
    weights = readout[...]
    total = three(nt, jnp.ones((8, ch), f32), out * gate * weights)
    for k, (a, b) in enumerate(sz.own):
        energy[a - 1, b - 1 : b, :] = total[0:1, k * n : (k + 1) * n]
    out_grad = gate * (1.0 + out * (1.0 - gate)) * weights
    cotangents = three(nt, out_grad, mixing[1])
    acc[...] = jnp.zeros_like(acc)
    acc_pos[...] = jnp.zeros_like(acc_pos)
    for a in range(sz.cols_x):
        first = ((a + 1) * sz.inner_y + 1) * n
        acc[first : first + sz.cols_y * n] = out_grad[a * sz.cols_y * n : (a + 1) * sz.cols_y * n]

    def back_steps(part):
        input_grad, got = yield from layer_backward(
            sz, part, every, angular, dist, atom, back_in, back_out,
            [second_radial[part, k] for k in every],
            jnp.concatenate([second_value[part, k] for k in every], axis=1),
            jnp.concatenate([second_slope[part, k] for k in every], axis=1),
            [second_xt[part, k] for k in every],
            [second_msg[k] for k in every],
            [cotangents[k * n : (k + 1) * n] for k in every],
        )
        for k, value in zip(every, got):
            store_grads(sz, k, value, ang_grad, dist_grad, env_grad)
        acc[...] += nt(hot[part], input_grad)
        own_positions(
            sz, part, code, atom, sep, dist, hot[part], ang_grad, dist_grad, env_grad, acc_pos
        )

    def back_part(part, carry):
        run_steps(back_steps(part))
        return carry

    lax.fori_loop(0, parts, back_part, 0)
    for a in range(sz.inner_x):
        places = []
        for b in range(sz.inner_y):
            row = sz.inner_row(a, b)
            back[a, b + (b >= 2)] = acc[row : row + n].astype(bf16)
            full = acc_pos[row : row + n]
            high = full.astype(bf16).astype(f32)
            places += [high, full - high]
        filler = jnp.zeros((n, ch - 16 * sz.inner_y), f32)
        back[a, 2] = jnp.concatenate(places + [filler], axis=1).astype(bf16)


def packed_halo(sz, code, target, place):
    rows = len(sz.halo)
    first = len(sz.own)
    row = lax.broadcasted_iota(jnp.int32, (rows, sz.edges), 0)
    at_x, at_y = jnp.zeros_like(row), jnp.zeros_like(row)
    for h, (a, b) in enumerate(sz.halo):
        at_x, at_y = jnp.where(row == h, a, at_x), jnp.where(row == h, b, at_y)
    shape = (sz.edges, sz.edges)
    before = iota(shape, 0) <= iota(shape, 1)
    above = iota((rows, rows), 1) < iota((rows, rows), 0)
    count = jnp.zeros((1, 1), f32)
    for part in range(2):
        codes = code[part, first:].astype(jnp.int32)
        offset = codes >> 4
        step_x = (offset * 11) >> 5
        to_x = at_x + step_x - 2
        to_y = at_y + offset - 3 * step_x - 2
        inside = (to_x >= 0) & (to_x < sz.cols_x) & (to_y >= 0) & (to_y < sz.cols_y)
        flags = (inside & (codes >= 0)).astype(f32)
        wanted = (to_x * sz.cols_y + to_y) * sz.slots + (codes & 15)
        target[part] = flags * wanted.astype(f32)
        flags_bf = flags.astype(bf16)
        running = mm(flags_bf, before.astype(f32).astype(bf16)) - 1.0
        earlier = jnp.sum(mm(above.astype(f32).astype(bf16), flags_bf), axis=1, keepdims=True)
        place[part] = jnp.where(flags > 0.0, running + earlier + count, -1.0)
        count = count + jnp.sum(jnp.sum(flags, axis=1, keepdims=True), axis=0, keepdims=True)
    return (jnp.max(count).astype(jnp.int32) + sz.edges - 1) // sz.edges


def halo_back(
    sz, part, edge_parts, own_turned, atom, sep, gathered, weights, target, place,
    feature_acc, pos_acc,
):
    in_one, out_one, back_in, back_out = weights
    ch, n, lanes = sz.channels, sz.slots, sz.edges
    first = len(sz.own)
    count = len(sz.halo) * n
    wanted = iota((lanes, lanes), 0) + jnp.asarray(part * lanes).astype(f32)
    ones, zeros = jnp.ones((1, lanes), f32), jnp.zeros((2, lanes), f32)

    def packed(edge_part, total):
        picks, sides = [], []
        for h in range(len(sz.halo)):
            pick = place[edge_part, pl.ds(h, 1), :] == wanted
            picks.append(pick.astype(f32).astype(bf16))
            rows = jnp.concatenate(
                [sep[edge_part, d, pl.ds(first + h, 1), :] for d in range(3)]
                + [
                    target[edge_part, pl.ds(h, 1), :],
                    atom[edge_part, pl.ds(first + h, 1), :] + float(h * n),
                    ones,
                    zeros,
                ],
                axis=0,
            )
            high = rows.astype(bf16).astype(f32)
            middle = (rows - high).astype(bf16).astype(f32)
            sides.append(
                jnp.concatenate([high, middle, rows - high - middle], axis=0).astype(bf16)
            )
        return total + nt(jnp.concatenate(sides, axis=1), jnp.concatenate(picks, axis=1))

    got = packed(0, jnp.zeros((24, lanes), f32))
    yield
    got = lax.fori_loop(1, edge_parts, packed, got)
    got = got[0:8] + got[8:16] + got[16:24]
    seps = [got[d : d + 1] for d in range(3)]
    target_row, atom_row, valid = got[3:4], got[4:5], got[5:6]
    dist_row, env_row, angular = geometry(valid, seps)
    yield
    weighted, value, slope = hidden_rows(sz, dist_row, env_row, in_one)
    yield
    radial = mm(out_one, weighted)
    chosen = iota((first * n, lanes), 0) == target_row
    one_hot = jnp.where(chosen, valid, 0.0).astype(bf16)
    xt = mm(own_turned, one_hot)
    sources = jnp.where(iota((count, lanes), 0) == atom_row, valid, 0.0).astype(bf16)
    yield
    spread = mm(gathered[...], sources)
    yield
    parts = [spread[m * ch : (m + 1) * ch] for m in range(9)]
    vector = angular[1] * parts[1] + angular[2] * parts[2] + angular[3] * parts[3]
    tensor = angular[4] * parts[4]
    for m in range(5, 9):
        tensor = tensor + angular[m] * parts[m]
    product_grad = jnp.concatenate([parts[0], vector, tensor], axis=0)
    _, radial_grad, input_grad = radial_products(sz, product_grad, radial, xt)
    products = [radial[l * ch : (l + 1) * ch] * xt for l in range(3)]
    ang_grad = [None] + [
        jnp.sum(parts[m] * products[1 if m < 4 else 2], axis=0, keepdims=True)
        for m in range(1, 9)
    ]
    yield
    dist_grad, env_grad = radial_backward(
        sz, dist_row, radial_grad, value, slope, back_in, back_out
    )
    grads = separation_grads(valid, seps, dist_row, ang_grad, dist_grad, env_grad)
    yield
    feature_acc[...] += nt(one_hot, input_grad)
    got = nt(one_hot, stacked_seps(list(grads)))
    pos_acc[...] += got[:, :8] + got[:, 8:]


def second_kernel(
    sz, total, before, after, kept, code, atom, sep, table,
    wide_in, wide_out, turned_in, turned_out, mixing,
    feature_grad, forces,
    angular, dist, env, ang_grad, dist_grad, env_grad,
    acc, acc_pos, halo_acc, halo_pos, target, place, gathered,
):
    ch, n = sz.channels, sz.slots
    cells = []
    for a in range(sz.inner_x):
        for b in range(sz.inner_y):
            far = before[a, b + 1] if b < 2 else after[a, b - 2]
            cells.append(total[a, b + (b >= 2)] + far.astype(f32))
    cotangent = jnp.concatenate(cells, axis=0)
    inv = three(nt, cotangent, mixing[0])
    halo_parts = packed_halo(sz, code, target, place)
    second_used = (jnp.max(code[1]) >= 0.0).astype(jnp.int32)
    edge_parts = 1 + second_used
    in_one, out_one = wide_in[0], wide_out[0]
    back_in, back_out = turned_in[0], turned_out[0]
    owned = len(sz.own)
    every = list(range(owned))
    acc[...] = jnp.zeros_like(acc)
    acc_pos[...] = jnp.zeros_like(acc_pos)
    halo_acc[...] = jnp.zeros_like(halo_acc)
    halo_pos[...] = jnp.zeros_like(halo_pos)

    def inv_rows(a, b):
        row = sz.inner_row(a, b)
        return inv[row : row + n]

    turned = table[...].astype(f32).T.astype(bf16)

    def back_steps(part):
        seps = [sep[part, d, :owned] for d in range(3)]
        store_geometry(part, live_rows(code[part, :owned]), seps, dist, env, angular)
        one_hot = own_hot(sz, code[part, :owned])
        found = mm(turned, one_hot)
        rows = [
            jnp.concatenate([ref[part, pl.ds(k, 1), :] for k in every], axis=1)
            for ref in (dist, env)
        ]
        yield
        weighted, value, slope = hidden_rows(sz, *rows, in_one)
        yield
        radials = mm(out_one, weighted)
        yield
        input_grad, got = yield from layer_backward(
            sz, part, every, angular, dist, atom, back_in, back_out,
            [radials[:, k * sz.edges : (k + 1) * sz.edges] for k in every],
            value, slope,
            [found[:, k * sz.edges : (k + 1) * sz.edges] for k in every],
            [kept[k] for k in every],
            [inv_rows(*sz.own[k]) for k in every],
        )
        for k, value in zip(every, got):
            store_grads(sz, k, value, ang_grad, dist_grad, env_grad)
        acc[...] += nt(one_hot, input_grad)
        own_positions(
            sz, part, code, atom, sep, dist, one_hot, ang_grad, dist_grad, env_grad, acc_pos
        )

    def back_part(part, carry):
        run_steps(back_steps(part))
        return carry

    halo_grads = [
        message_grads(sz, kept[owned + h], inv_rows(a, b)) for h, (a, b) in enumerate(sz.halo)
    ]
    for m in range(9):
        rows = jnp.concatenate([grads[m] for grads in halo_grads], axis=0)
        gathered[m * ch : (m + 1) * ch, :] = rows.T.astype(bf16)
    own_rows = [
        table[sz.inner_row(a + 1, 1) : sz.inner_row(a + 1, 1) + sz.cols_y * n, :]
        for a in range(sz.cols_x)
    ]
    own_turned = jnp.concatenate(own_rows, axis=0).astype(f32).T.astype(bf16)
    weights = (in_one, out_one, back_in, back_out)

    def halo_steps(part):
        return halo_back(
            sz, part, edge_parts, own_turned, atom, sep, gathered, weights, target, place,
            halo_acc, halo_pos,
        )

    def halo_part(part, carry):
        run_steps(halo_steps(part))
        return carry

    run_steps(back_steps(0), halo_steps(0))
    lax.fori_loop(1, edge_parts, back_part, 0)
    lax.fori_loop(1, halo_parts, halo_part, 0)
    for a in range(sz.cols_x):
        inner = sz.inner_row(a + 1, 1)
        rows = sz.cols_y * n
        mine = slice(a * rows, (a + 1) * rows)
        feature_grad[mine] = (
            acc[inner : inner + rows] + cotangent[inner : inner + rows] + halo_acc[mine]
        )
        moved = acc_pos[inner : inner + rows] + halo_pos[mine]
        for b in range(sz.cols_y):
            lane = 16 * (b + 1)
            far, start = (before[a + 1, 0], 16 * (b + 3)) if b < 1 else (after[a + 1, 2], 16 * (b - 1))
            both = total[a + 1, 2][:, lane : lane + 16]
            both = both + far.astype(f32)[:, start : start + 16]
            place_grad = moved[b * n : (b + 1) * n] + both[:, :8] + both[:, 8:]
            forces[a, :, b, :] = -(place_grad.T)[:3]


def ring(axis):
    devices = lax.axis_size(axis)
    up = [(i, (i + 1) % devices) for i in range(devices)]
    return up, [(j, i) for i, j in up]


def both_ways(first, last, axis):
    up, down = ring(axis)
    return lax.ppermute(last, axis, up), lax.ppermute(first, axis, down)


def shards(
    features, positions, species, neighbours, counts, species_gain, radial_in, radial_out, mixing, readout
):
    cols_x, cols_y, slots, channels = features.shape
    neigh = neighbours.shape[-1]
    basis, hidden = radial_in.shape[1:]
    sz = Sizes(cols_x, cols_y, slots, neigh, channels, basis, hidden)
    vmem = pl.BlockSpec(memory_space=pltpu.VMEM)
    in_hbm = pl.BlockSpec(memory_space=pltpu.HBM)
    params = pltpu.CompilerParams(vmem_limit_bytes=40 * 1024 * 1024)
    given = (features, positions.transpose(0, 2, 1, 3), species, neighbours, counts, species_gain)
    block = pl.pallas_call(
        functools.partial(block_kernel, sz, species_gain.shape[0]),
        out_shape=jax.ShapeDtypeStruct((cols_x, cols_y + 1, slots, channels), bf16),
        in_specs=[in_hbm] * 6,
        out_specs=vmem,
        scratch_shapes=[pltpu.VMEM(x.shape, x.dtype) for x in given]
        + [pltpu.SemaphoreType.DMA((6,))],
        compiler_params=pltpu.CompilerParams(vmem_limit_bytes=60 * 1024 * 1024),
        name="block_of_atoms",
    )(*given)
    assert cols_x == 2 and cols_y == 2
    before, after = both_ways(block, block, "gx")
    middle = jnp.concatenate([before, block, after], axis=0)
    before, after = both_ways(middle, middle, "gy")

    inner_atoms = sz.inner * slots
    owned = cols_x * cols_y
    edges = sz.edges
    columns = sz.inner
    grads = [
        pltpu.VMEM((9, owned, edges), f32),
        pltpu.VMEM((owned, edges), f32),
        pltpu.VMEM((owned, edges), f32),
    ]
    weights = prepared(radial_in, radial_out, mixing)
    assert slots * neigh <= 2 * edges
    kept_shapes = [
        (columns, sz.window, channels),
        (2, columns, edges),
        (2, columns, edges),
        (2, 3, columns, edges),
    ]

    def edge_scratch(count):
        return [
            pltpu.VMEM((2, 9, count, edges), f32),
            pltpu.VMEM((2, count, edges), f32),
            pltpu.VMEM((2, count, edges), f32),
        ]

    energy, back, *kept = pl.pallas_call(
        functools.partial(first_kernel, sz),
        out_shape=[
            jax.ShapeDtypeStruct((cols_x, cols_y, slots), f32),
            jax.ShapeDtypeStruct((sz.inner_x, sz.inner_y + 1, slots, channels), bf16),
        ]
        + [jax.ShapeDtypeStruct(shape, f32) for shape in kept_shapes]
        + [jax.ShapeDtypeStruct((inner_atoms, channels), bf16)],
        in_specs=[vmem] * 9,
        out_specs=[vmem] * 7,
        scratch_shapes=[pltpu.VMEM(((cols_x + 4) * (cols_y + 4) * slots, 2 * channels), bf16)]
        + [
            pltpu.VMEM((2, inner_atoms, owned * edges), bf16),
            pltpu.VMEM((columns, channels, edges), f32),
        ]
        + edge_scratch(columns)
        + [
            pltpu.VMEM((inner_atoms, channels), bf16),
            pltpu.VMEM((2, owned, channels, edges), f32),
            pltpu.VMEM((owned, sz.window, channels), f32),
            pltpu.VMEM((2, owned, 3 * channels, edges), f32),
            pltpu.VMEM((2, owned, hidden, edges), f32),
            pltpu.VMEM((2, owned, hidden, edges), f32),
        ]
        + grads
        + [pltpu.VMEM((inner_atoms, channels), f32), pltpu.VMEM((inner_atoms, 8), f32)],
        compiler_params=params,
        name="forward_and_second_back",
    )(before, middle, after, *weights, readout.reshape(1, -1))

    far = both_ways(back[:2], back[2:], "gx")
    total = back.astype(f32) + jnp.concatenate(far, axis=0).astype(f32)
    sent = total.astype(bf16)
    far = both_ways(sent[:, :3], sent[:, 2:], "gy")
    feature_grad, forces = pl.pallas_call(
        functools.partial(second_kernel, sz),
        out_shape=(
            jax.ShapeDtypeStruct((owned * slots, channels), f32),
            jax.ShapeDtypeStruct((cols_x, 3, cols_y, slots), f32),
        ),
        in_specs=[vmem] * 13,
        out_specs=(vmem,) * 2,
        scratch_shapes=edge_scratch(owned)
        + grads
        + [
            pltpu.VMEM((rows, width), f32)
            for rows in (inner_atoms, owned * slots)
            for width in (channels, 8)
        ]
        + [
            pltpu.VMEM((2, len(sz.halo), edges), f32),
            pltpu.VMEM((2, len(sz.halo), edges), f32),
            pltpu.VMEM((9 * channels, len(sz.halo) * slots), bf16),
        ],
        compiler_params=params,
        name="first_back",
    )(total, *far, *kept, *weights)
    return (
        energy,
        forces.transpose(0, 2, 1, 3),
        feature_grad.reshape(cols_x, cols_y, slots, channels),
    )


def solution(mesh):
    placed = (
        P("gx", "gy", None, None),
        P("gx", "gy", None, None),
        P("gx", "gy", None),
        P("gx", "gy", None, None),
        P("gx", "gy", None),
        P(),
        P(),
        P(),
        P(),
        P(),
    )
    return jax.shard_map(
        shards,
        mesh=mesh,
        in_specs=placed,
        out_specs=(P("gx", "gy", None), P("gx", "gy", None, None), P("gx", "gy", None, None)),
        check_vma=False,
    )
```

```python
import functools

import jax
import jax.numpy as jnp
from jax import lax
from jax.experimental import pallas as pl
from jax.experimental.pallas import tpu as pltpu
from jax.sharding import PartitionSpec as P

column = 6.0
cutoff = 6.0
softening = 0.01
root_three = 3.0**0.5
f32 = jnp.float32
bf16 = jnp.bfloat16
code_lane = 32
count_lane = 31
part_lanes = 256


def mm(a, b):
    return lax.dot_general(a, b, (((1,), (0,)), ((), ())), preferred_element_type=f32)


def nt(a, b):
    return lax.dot_general(a, b, (((1,), (1,)), ((), ())), preferred_element_type=f32)


def split(x):
    high = x.astype(bf16)
    return high, (x - high.astype(f32)).astype(bf16)


def three(product, a, b):
    a_high, a_low = split(a)
    b_high, b_low = split(b) if b.dtype == f32 else (b[0], b[1])
    return product(a_high, b_high) + product(a_low, b_high) + product(a_high, b_low)


def parted(x):
    high = lax.reduce_precision(x, 8, 7)
    return high, x - high


def prepared(radial_in, radial_out, mixing):
    high, low = parted(radial_in)
    turned = jnp.concatenate([high, high, low, jnp.zeros_like(high)], axis=1).swapaxes(1, 2)
    back_in = jnp.concatenate([high, low], axis=1)
    high, low = parted(radial_out)
    wide = jnp.concatenate([high, high, low], axis=1).swapaxes(1, 2)
    high_mix, low_mix = parted(mixing)
    mix = jnp.stack([high_mix, low_mix], axis=1)
    return [x.astype(bf16) for x in (turned, wide, back_in, high, mix)]


def harmonic_rows(ux, uy, uz):
    square = ux * ux + uy * uy + uz * uz
    return [
        jnp.ones_like(ux),
        ux,
        uy,
        uz,
        root_three * ux * uy,
        root_three * uy * uz,
        0.5 * (3.0 * uz * uz - square),
        root_three * ux * uz,
        0.5 * root_three * (ux * ux - uy * uy),
    ]


class Sizes:
    def __init__(self, cols_x, cols_y, slots, neigh, channels, basis, hidden):
        self.cols_x, self.cols_y = cols_x, cols_y
        self.slots, self.neigh, self.channels = slots, neigh, channels
        self.basis, self.hidden = basis, hidden
        self.inner_x, self.inner_y = cols_x + 2, cols_y + 2
        self.outer_y = cols_y + 4
        self.inner = self.inner_x * self.inner_y
        self.edges = part_lanes
        self.window = 9 * slots

        cells = [(a, b) for a in range(self.inner_x) for b in range(self.inner_y)]
        self.own = [c for c in cells if self.is_own(*c)]
        last = self.inner_x - 1
        self.halo = [c for c in cells if c[0] in (0, last)]
        self.halo += [(a, b) for b in (0, self.inner_y - 1) for a in range(1, last)]
        self.order = self.own + self.halo

    def is_own(self, a, b):
        return 1 <= a <= self.cols_x and 1 <= b <= self.cols_y

    def outer_row(self, a, b):
        return (a * self.outer_y + b) * self.slots

    def inner_row(self, a, b):
        return (a * self.inner_y + b) * self.slots


def each(compute):
    return lambda items: [compute(item) for item in items]


def run_steps(*steps):
    steps = list(steps)
    while steps:
        for step in list(steps):
            try:
                next(step)
            except StopIteration:
                steps.remove(step)


def loop(count, group, compute, store):
    for first in range(0, count, group):
        items = list(range(first, min(first + group, count)))
        for item, value in zip(items, compute(items)):
            store(item, value)


def iota(shape, dim):
    return lax.broadcasted_iota(jnp.int32, shape, dim).astype(f32)


def bounds_of(sz, table):
    n, ch = sz.slots, sz.channels
    rows = [sz.outer_row(a + 1, b + 1) for a, b in sz.order]
    metas = jnp.concatenate([table[row : row + n, ch:] for row in rows], axis=0)
    shape = (sz.inner * n, sz.inner * n)
    left = lax.broadcasted_iota(jnp.int32, shape, 0)
    right = lax.broadcasted_iota(jnp.int32, shape, 1)
    earlier = (left // n == right // n) & (right < left)
    sums = mm(earlier.astype(f32).astype(bf16), metas)
    low = sums[:, count_lane : count_lane + 1]
    return low, low + metas[:, count_lane : count_lane + 1].astype(f32)


def gather_columns(sz, part, table, low, high, code, atom, sep, xt):
    ch, n, edges = sz.channels, sz.slots, sz.edges
    lane = iota((n, edges), 1) + (part * edges).astype(f32)
    row = iota((n, edges), 0)
    slot = iota((sz.neigh, 2 * edges), 0)
    second = (lax.broadcasted_iota(jnp.int32, (1, 2 * edges), 1) >= edges).astype(f32)
    target = iota((12 * n, 2 * edges), 0)
    empty = jnp.zeros((n, edges), f32)

    firsts = list(range(0, sz.inner, 2))
    ats, valids, which, atoms, spreads = [], [], [], [], []
    for col, (a, b) in enumerate(sz.order):
        mine = slice(col * n, (col + 1) * n)
        at = ((lane >= low[mine]) & (lane < high[mine])).astype(f32)
        ats.append(at)
        valids.append(jnp.sum(at, axis=0, keepdims=True) - 1.0)
        which.append(lane[:1] - jnp.sum(at * low[mine], axis=0, keepdims=True))
        atoms.append(jnp.sum(at * row, axis=0, keepdims=True) + valids[-1])
    for first in firsts:
        places = [sz.outer_row(a + 1, b + 1) for a, b in sz.order[first : first + 2]]
        metas = [table[place : place + n, ch : 2 * ch] for place in places]
        turned = jnp.concatenate(metas, axis=0).astype(f32).T[: 2 * code_lane].astype(bf16)
        apart = jnp.concatenate(
            [
                jnp.concatenate([ats[first], empty], axis=1),
                jnp.concatenate([empty, ats[first + 1]], axis=1),
            ],
            axis=0,
        )
        spreads.append(mm(turned, apart.astype(bf16)))
    hots, windows, codes_of = [], [], []
    for first, spread in zip(firsts, spreads):
        (a, b), (_, other_b) = sz.order[first : first + 2]
        both = jnp.concatenate(which[first : first + 2], axis=1)
        picked = jnp.where(slot == both, spread[code_lane:], 0.0)
        codes = jnp.sum(picked, axis=0, keepdims=True)
        codes = codes + jnp.concatenate(valids[first : first + 2], axis=1)
        if other_b != b:
            width, height = 4, 3
            ahead = (codes >= 3.0 * n).astype(f32) + (codes >= 6.0 * n).astype(f32)
            rows = codes + n * (ahead + second)
        else:
            width, height = 3, 4
            rows = codes + 3.0 * n * second
        rows = jnp.where(codes < 0.0, -1.0, rows)
        hots.append((target == rows).astype(f32).astype(bf16))
        window = jnp.concatenate(
            [table[pl.ds(sz.outer_row(a + d, b), width * n), :] for d in range(height)], axis=0
        )
        windows.append(window.astype(f32).T.astype(bf16)[: ch + 32])
        codes_of.append(codes)
    founds = [mm(window, one_hot) for window, one_hot in zip(windows, hots)]
    for first, spread, codes, found in zip(firsts, spreads, codes_of, founds):
        diff = found[ch : ch + 24] - spread[:24]
        total = diff[0:8] + diff[8:16] + diff[16:24]
        for col, span in ((first, slice(0, edges)), (first + 1, slice(edges, 2 * edges))):
            code[part, pl.ds(col, 1), :] = codes[:, span]
            atom[part, pl.ds(col, 1), :] = atoms[col]
            xt[col] = found[:ch, span]
            for d in range(3):
                sep[part, d, pl.ds(col, 1), :] = total[d : d + 1, span]


def wide_rows(rows):
    return jnp.concatenate([rows[k : k + 1] for k in range(rows.shape[0])], axis=1)


def own_hot(sz, codes):
    row = lax.broadcasted_iota(jnp.int32, codes.shape, 0)
    place = jnp.zeros_like(row)
    for k, (a, b) in enumerate(sz.own):
        place = jnp.where(row == k, sz.inner_row(a - 1, b - 1), place)
    whole = codes.astype(jnp.int32)
    ahead = (((whole >> 4) * 11) >> 5) * (sz.slots * (sz.inner_y - 3))
    rows = jnp.where(codes < 0.0, -1.0, (place + whole + ahead).astype(f32))
    wide = wide_rows(rows)
    return (iota((sz.inner * sz.slots, wide.shape[1]), 0) == wide).astype(f32).astype(bf16)


def own_atoms(sz, atoms):
    row = iota(atoms.shape, 0)
    wide = wide_rows(jnp.where(atoms < 0.0, -1.0, atoms + row * float(sz.slots)))
    return (iota((len(sz.own) * sz.slots, wide.shape[1]), 0) == wide).astype(f32).astype(bf16)


def shifted_seps(part, code, sep):
    offset = code[part].astype(jnp.int32) >> 4
    step_x = (offset * 11) >> 5
    step_y = offset - 3 * step_x
    sep[part, 0] = sep[part, 0] + column * (step_x - 1).astype(f32)
    sep[part, 1] = sep[part, 1] + column * (step_y - 1).astype(f32)


def geometry(live, seps):
    sep_x, sep_y, sep_z = seps
    dist_sq = sep_x * sep_x + sep_y * sep_y + sep_z * sep_z
    env = jnp.square(jnp.maximum(1.0 - dist_sq / (cutoff * cutoff), 0.0)) * live
    rows = harmonic_rows(sep_x / cutoff, sep_y / cutoff, sep_z / cutoff)
    return jnp.sqrt(dist_sq + softening), env, rows


def store_geometry(part, live, seps, dist, env, angular):
    dist[part], env[part], rows = geometry(live, seps)
    for m, row in enumerate(rows):
        angular[part, m] = row


def live_rows(code):
    return (code >= 0.0).astype(f32)


def basis_rows(sz, dist_row):
    width = dist_row.shape[1]
    spacing = cutoff / (sz.basis - 1)
    centre = lax.broadcasted_iota(jnp.int32, (sz.basis, width), 0).astype(f32) * spacing
    shifted = (dist_row - centre) * (1.0 / spacing)
    return jnp.exp(-shifted * shifted), shifted


def sigmoid(x):
    return 0.5 * jnp.tanh(0.5 * x) + 0.5


def hidden_rows(sz, dist_row, env_row, weight_in):
    basis, _ = basis_rows(sz, dist_row)
    high = basis.astype(bf16).astype(f32)
    stacked = jnp.concatenate([high, basis - high, high, jnp.zeros_like(high)], axis=0)
    pre = mm(weight_in, stacked.astype(bf16))
    gate = sigmoid(pre)
    value = pre * gate
    weighted = value * env_row
    high, low = split(weighted)
    slope = gate * (1.0 + pre * (1.0 - gate)) * env_row
    return jnp.concatenate([high, low, high], axis=0), value, slope


def atoms_at(sz, atom, part, col):
    return (iota((sz.slots, sz.edges), 0) == atom[part, pl.ds(col, 1), :]).astype(f32)


def block_rows(angular, part, col, at):
    return [angular[part, m, pl.ds(col, 1), :] * at for m in range(1, 9)]


def layer_forward(sz, part, cols, angular, dist, env, atom, weight_in, weight_out, inputs):
    rows = [jnp.concatenate([ref[part, pl.ds(c, 1), :] for c in cols], axis=1) for ref in (dist, env)]
    weighted, value, slope = hidden_rows(sz, *rows, weight_in)
    radials = mm(weight_out, weighted)
    spans = [slice(k * sz.edges, (k + 1) * sz.edges) for k in range(len(cols))]
    sides = [message_sides(sz, part, col, angular, atom) for col in cols]
    products = [
        (radials[:, span] * jnp.concatenate([xt] * 3, axis=0)).astype(bf16)
        for span, xt in zip(spans, inputs)
    ]
    ch = sz.channels
    got = [
        [nt(both, product[l * ch : (l + 1) * ch]) for l, both in enumerate(side)]
        for side, product in zip(sides, products)
    ]
    out = []
    for span, parts in zip(spans, got):
        halves = [len(x) // 2 for x in parts]
        rows = [parts[0]] + [x[:h] + x[h:] for x, h in zip(parts[1:], halves[1:])]
        message = jnp.concatenate(rows, axis=0)
        out.append((radials[:, span], value[:, span], slope[:, span], message))
    return out


def message_sides(sz, part, col, angular, atom):
    n = sz.slots
    at = atoms_at(sz, atom, part, col)
    blocks = jnp.concatenate(block_rows(angular, part, col, at), axis=0)
    high = blocks.astype(bf16).astype(f32)
    low = blocks - high
    sides = [at.astype(bf16)]
    for rows in (slice(0, 3 * n), slice(3 * n, 8 * n)):
        sides.append(jnp.concatenate([high[rows], low[rows]], axis=0).astype(bf16))
    return sides


def invariants(sz, message):
    n = sz.slots
    squares = message * message
    got = [squares[m * n : (m + 1) * n] for m in range(9)]
    return jnp.concatenate(
        [message[:n], got[1] + got[2] + got[3], got[4] + got[5] + got[6] + got[7] + got[8]],
        axis=1,
    )


def message_grads(sz, message, cotangent):
    ch, n = sz.channels, sz.slots
    twice = 2.0 * cotangent[:, ch:]
    parts = [
        message[m * n : (m + 1) * n] * (twice[:, :ch] if m < 4 else twice[:, ch:])
        for m in range(1, 9)
    ]
    return [cotangent[:, :ch]] + parts


def radial_products(sz, product_grad, radial, xt):
    ch = sz.channels
    products, mine, input_grad = [], [], None
    for l in range(3):
        grad, part = product_grad[l * ch : (l + 1) * ch], radial[l * ch : (l + 1) * ch]
        if l:
            products.append((part * xt).astype(bf16))
        mine.append((grad * xt).astype(bf16))
        term = grad * part
        input_grad = term if input_grad is None else input_grad + term
    return products, jnp.concatenate(mine, axis=0), input_grad.astype(bf16)


def radial_backward(sz, dist_row, radial_grad, value, slope, back_in, back_out):
    weighted_grad = mm(back_out, radial_grad)
    env_row_grad = jnp.sum(weighted_grad * value, axis=0, keepdims=True)
    both = mm(back_in, (weighted_grad * slope).astype(bf16))
    basis_grad = both[: sz.basis] + both[sz.basis : 2 * sz.basis]
    basis, shifted = basis_rows(sz, dist_row)
    spacing = cutoff / (sz.basis - 1)
    dist_row_grad = jnp.sum(
        basis_grad * basis * shifted * (-2.0 / spacing), axis=0, keepdims=True
    )
    return dist_row_grad, env_row_grad


def layer_backward(
    sz, part, cols, angular, dist, atom, back_in, back_out, radials, value, slope, inputs,
    messages, cotangents,
):
    ch, n = sz.channels, sz.slots
    ats = [atoms_at(sz, atom, part, col) for col in cols]
    grads_of = [message_grads(sz, *both) for both in zip(messages, cotangents)]
    lhs = []
    for grads in grads_of:
        turned = jnp.concatenate(grads, axis=0).T
        lane = lax.broadcasted_iota(jnp.int32, turned.shape, 1)
        lhs.append(
            jnp.concatenate(
                [
                    jnp.where(lane < n, turned, 0.0),
                    jnp.where((lane >= n) & (lane < 4 * n), turned, 0.0),
                    jnp.where(lane >= 4 * n, turned, 0.0),
                ],
                axis=0,
            ).astype(bf16)
        )
    blocks = [
        jnp.concatenate([at] + block_rows(angular, part, col, at), axis=0).astype(bf16)
        for col, at in zip(cols, ats)
    ]
    yield
    product_grads = [mm(left, right) for left, right in zip(lhs, blocks)]
    yield
    triples = [
        radial_products(sz, *three_of) for three_of in zip(product_grads, radials, inputs)
    ]
    mine = [triple[1] for triple in triples]
    input_grads = [triple[2] for triple in triples]
    yield
    empty = jnp.zeros((n, ch), f32)
    wides = []
    for grads in grads_of:
        wide = [
            jnp.concatenate([g, empty] if m < 3 else [empty, g], axis=1)
            for m, g in enumerate(grads[1:])
        ]
        wides.append(jnp.concatenate(wide, axis=0).astype(bf16))
    gots = [
        mm(wide, jnp.concatenate(triple[0], axis=0)) for wide, triple in zip(wides, triples)
    ]
    yield
    ang_grads = [
        [jnp.sum(got[m * n : (m + 1) * n] * at, axis=0, keepdims=True) for m in range(8)]
        for got, at in zip(gots, ats)
    ]
    dist_row = jnp.concatenate([dist[part, pl.ds(col, 1), :] for col in cols], axis=1)
    dist_row_grad, env_row_grad = radial_backward(
        sz, dist_row, jnp.concatenate(mine, axis=1), value, slope, back_in, back_out
    )
    out = []
    for k in range(len(cols)):
        span = slice(k * sz.edges, (k + 1) * sz.edges)
        out.append((ang_grads[k], dist_row_grad[:, span], env_row_grad[:, span]))
    yield
    return jnp.concatenate(input_grads, axis=1), out


def store_grads(sz, col, value, ang_grad, dist_grad, env_grad):
    ang_grads, dist_row_grad, env_row_grad = value
    for m in range(8):
        ang_grad[m + 1, pl.ds(col, 1), :] = ang_grads[m]
    dist_grad[pl.ds(col, 1), :] = dist_row_grad
    env_grad[pl.ds(col, 1), :] = env_row_grad


def separation_grads(live, sep, dist, ang_grad, dist_grad, env_grad):
    sep_x, sep_y, sep_z = sep
    ux, uy, uz = sep_x / cutoff, sep_y / cutoff, sep_z / cutoff
    dist_sq = sep_x * sep_x + sep_y * sep_y + sep_z * sep_z
    inside = jnp.maximum(1.0 - dist_sq / (cutoff * cutoff), 0.0)
    sq_grad = dist_grad * (0.5 / dist) - env_grad * live * inside * (2.0 / (cutoff * cutoff))
    g = ang_grad
    r3 = root_three
    grad_x = g[1] + r3 * (uy * g[4] + uz * g[7] + ux * g[8]) - ux * g[6]
    grad_y = g[2] + r3 * (ux * g[4] + uz * g[5] - uy * g[8]) - uy * g[6]
    grad_z = g[3] + r3 * (uy * g[5] + ux * g[7]) + 2.0 * uz * g[6]
    return (
        2.0 * sep_x * sq_grad + grad_x / cutoff,
        2.0 * sep_y * sq_grad + grad_y / cutoff,
        2.0 * sep_z * sq_grad + grad_z / cutoff,
    )


def stacked_seps(rows):
    full = jnp.concatenate(rows + [jnp.zeros((5, rows[0].shape[1]), f32)], axis=0)
    high = full.astype(bf16).astype(f32)
    return jnp.concatenate([high, full - high], axis=0).astype(bf16)


def own_positions(sz, part, code, atom, sep, dist, hot, ang_grad, dist_grad, env_grad, acc_pos):
    owned, n = len(sz.own), sz.slots
    grads = separation_grads(
        live_rows(code[part, :owned]),
        [sep[part, d, :owned] for d in range(3)],
        dist[part, :owned],
        ang_grad,
        dist_grad[...],
        env_grad[...],
    )
    ends = jnp.concatenate([hot, own_atoms(sz, atom[part, :owned])], axis=0)
    got = nt(ends, stacked_seps([wide_rows(grad) for grad in grads]))
    got = got[:, :8] + got[:, 8:]
    atoms = sz.inner * n
    acc_pos[...] += got[:atoms]
    for k, (a, b) in enumerate(sz.own):
        row = sz.inner_row(a, b)
        acc_pos[row : row + n] -= got[atoms + k * n : atoms + (k + 1) * n]


def fetch(sources, targets, sems):
    copies = [
        pltpu.make_async_copy(source, target, sems.at[k])
        for k, (source, target) in enumerate(zip(sources, targets))
    ]
    for copy in copies:
        copy.start()
    return copies


def block_kernel(sz, kinds, *refs):
    sources, block, held, sems = refs[:6], refs[6], refs[7:13], refs[13]
    for copy in fetch(sources, held, sems):
        copy.wait()
    features, positions, species, neighbours, counts, species_gain = held
    ch, n = sz.channels, sz.slots
    gains = species_gain[...]
    gain_high = gains.astype(bf16).astype(f32)
    rest = gains - gain_high
    gain_middle = rest.astype(bf16).astype(f32)
    parts = [gain_high, gain_middle, rest - gain_middle]
    above, below = jnp.zeros((24, ch), f32), jnp.zeros((8 - kinds, ch), f32)
    parts = [jnp.concatenate([above, part, below], axis=0).astype(bf16) for part in parts]
    kind = lax.broadcasted_iota(jnp.int32, (8, n), 0)
    lane = lax.broadcasted_iota(jnp.int32, (n, code_lane), 1)
    gap = jnp.zeros((5, n), f32)
    for a in range(sz.cols_x):
        sides = []
        for b in range(sz.cols_y):
            atoms = positions[a, :, b, :]
            high = atoms.astype(bf16).astype(f32)
            rest = atoms - high
            middle = rest.astype(bf16).astype(f32)
            chosen = (kind == species[a, pl.ds(b, 1), :]).astype(f32)
            last = jnp.where(kind == 7, counts[a, pl.ds(b, 1), :].astype(f32), chosen)
            rows = [high, gap, middle, gap, rest - middle, gap, last]
            turned = jnp.concatenate(rows, axis=0).T
            picked = jnp.where((lane >= 24) & (lane < 24 + kinds), turned, 0.0).astype(bf16)
            gain = mm(picked, parts[0]) + mm(picked, parts[1]) + mm(picked, parts[2])
            place = jnp.where((lane < 24) | (lane == count_lane), turned, 0.0)
            sides.append(jnp.concatenate([place, neighbours[a, b].astype(f32)], axis=1))
            block[a, b] = (features[a, b].astype(f32) * gain).astype(bf16)
        block[a, sz.cols_y] = jnp.concatenate(sides, axis=1).astype(bf16)


def fill_table(sz, strips, table):
    ch, n = sz.channels, sz.slots
    for a in range(sz.cols_x + 4):
        for k, strip in enumerate(strips):
            meta = strip[a, sz.cols_y].astype(f32)
            for b in range(sz.cols_y):
                row = sz.outer_row(a, k * sz.cols_y + b)
                mine = meta if b == 0 else pltpu.roll(meta, ch - b * 2 * code_lane, 1)
                table[row : row + n, :ch] = strip[a, b]
                table[row : row + n, ch:] = mine.astype(bf16)


def first_kernel(
    sz, before, middle, after, wide_in, wide_out, turned_in, turned_out, mixing, readout,
    energy, back, kept, code, atom, sep, inputs_kept, table,
    hot, xt, angular, dist, env, second, second_xt, second_msg, second_radial,
    second_value, second_slope, ang_grad, dist_grad, env_grad, acc, acc_pos,
):
    ch, n = sz.channels, sz.slots
    owned = len(sz.own)
    fill_table(sz, (before, middle, after), table)
    low, high = bounds_of(sz, table)
    most = jnp.maximum(jnp.max(high).astype(jnp.int32), 1)
    parts = (most + sz.edges - 1) // sz.edges
    in_one, out_one = wide_in[0], wide_out[0]
    code[...] = jnp.full_like(code, -1.0)
    kept[...] = jnp.zeros_like(kept)

    def first_part(part, carry):
        gather_columns(sz, part, table, low, high, code, atom, sep, xt)
        shifted_seps(part, code, sep)
        seps = [sep[part, d] for d in range(3)]
        store_geometry(part, live_rows(code[part]), seps, dist, env, angular)

        def one(cols):
            inputs = [xt[col] for col in cols]
            return layer_forward(
                sz, part, cols, angular, dist, env, atom, in_one, out_one, inputs
            )

        def one_store(col, got):
            kept[col] += got[3]

        loop(sz.inner, 8, one, one_store)
        return carry

    lax.fori_loop(0, parts, first_part, 0)
    rows = [None] * sz.inner
    for col, (a, b) in enumerate(sz.order):
        rows[a * sz.inner_y + b] = invariants(sz, kept[col])
    own_rows = [
        table[(a * sz.outer_y + 1) * n : (a * sz.outer_y + 1 + sz.inner_y) * n, :ch]
        for a in range(1, 1 + sz.inner_x)
    ]
    first_out = three(mm, jnp.concatenate(rows, axis=0), mixing[0])
    inputs_kept[...] = jnp.concatenate(own_rows, axis=0)
    first_out = first_out + inputs_kept[...].astype(f32)
    second[...] = first_out.astype(bf16)

    in_two, out_two = wide_in[1], wide_out[1]
    back_in, back_out = turned_in[1], turned_out[1]
    second_msg[...] = jnp.zeros_like(second_msg)
    second_turned = second[...].astype(f32).T.astype(bf16)
    every = list(range(owned))

    def second_part(part, carry):
        one_hot = own_hot(sz, code[part, :owned])
        hot[part] = one_hot
        found = mm(second_turned, one_hot)
        inputs = [found[:, k * sz.edges : (k + 1) * sz.edges] for k in every]
        got = layer_forward(sz, part, every, angular, dist, env, atom, in_two, out_two, inputs)
        for k, (radial, value, slope, message) in zip(every, got):
            second_xt[part, k], second_radial[part, k] = inputs[k], radial
            second_value[part, k], second_slope[part, k] = value, slope
            second_msg[k] += message
        return carry

    lax.fori_loop(0, parts, second_part, 0)
    inv = jnp.concatenate([invariants(sz, second_msg[k]) for k in every], axis=0)
    own_rows = [
        second[(a * sz.inner_y + 1) * n : (a * sz.inner_y + 1 + sz.cols_y) * n, :]
        for a in range(1, 1 + sz.cols_x)
    ]
    out = three(mm, inv, mixing[1]) + jnp.concatenate(own_rows, axis=0).astype(f32)
    gate = sigmoid(out)
    weights = readout[...]
    total = three(nt, jnp.ones((8, ch), f32), out * gate * weights)
    for k, (a, b) in enumerate(sz.own):
        energy[a - 1, b - 1 : b, :] = total[0:1, k * n : (k + 1) * n]
    out_grad = gate * (1.0 + out * (1.0 - gate)) * weights
    cotangents = three(nt, out_grad, mixing[1])
    acc[...] = jnp.zeros_like(acc)
    acc_pos[...] = jnp.zeros_like(acc_pos)
    for a in range(sz.cols_x):
        first = ((a + 1) * sz.inner_y + 1) * n
        acc[first : first + sz.cols_y * n] = out_grad[a * sz.cols_y * n : (a + 1) * sz.cols_y * n]

    def back_steps(part):
        input_grad, got = yield from layer_backward(
            sz, part, every, angular, dist, atom, back_in, back_out,
            [second_radial[part, k] for k in every],
            jnp.concatenate([second_value[part, k] for k in every], axis=1),
            jnp.concatenate([second_slope[part, k] for k in every], axis=1),
            [second_xt[part, k] for k in every],
            [second_msg[k] for k in every],
            [cotangents[k * n : (k + 1) * n] for k in every],
        )
        for k, value in zip(every, got):
            store_grads(sz, k, value, ang_grad, dist_grad, env_grad)
        acc[...] += nt(hot[part], input_grad)
        own_positions(
            sz, part, code, atom, sep, dist, hot[part], ang_grad, dist_grad, env_grad, acc_pos
        )

    def back_part(part, carry):
        run_steps(back_steps(part))
        return carry

    lax.fori_loop(0, parts, back_part, 0)
    for a in range(sz.inner_x):
        places = []
        for b in range(sz.inner_y):
            row = sz.inner_row(a, b)
            back[a, b + (b >= 2)] = acc[row : row + n].astype(bf16)
            full = acc_pos[row : row + n]
            high = full.astype(bf16).astype(f32)
            places += [high, full - high]
        filler = jnp.zeros((n, ch - 16 * sz.inner_y), f32)
        back[a, 2] = jnp.concatenate(places + [filler], axis=1).astype(bf16)


def packed_halo(sz, code, target, place):
    rows = len(sz.halo)
    first = len(sz.own)
    row = lax.broadcasted_iota(jnp.int32, (rows, sz.edges), 0)
    at_x, at_y = jnp.zeros_like(row), jnp.zeros_like(row)
    for h, (a, b) in enumerate(sz.halo):
        at_x, at_y = jnp.where(row == h, a, at_x), jnp.where(row == h, b, at_y)
    shape = (sz.edges, sz.edges)
    before = iota(shape, 0) <= iota(shape, 1)
    above = iota((rows, rows), 1) < iota((rows, rows), 0)
    count = jnp.zeros((1, 1), f32)
    for part in range(2):
        codes = code[part, first:].astype(jnp.int32)
        offset = codes >> 4
        step_x = (offset * 11) >> 5
        to_x = at_x + step_x - 2
        to_y = at_y + offset - 3 * step_x - 2
        inside = (to_x >= 0) & (to_x < sz.cols_x) & (to_y >= 0) & (to_y < sz.cols_y)
        flags = (inside & (codes >= 0)).astype(f32)
        wanted = (to_x * sz.cols_y + to_y) * sz.slots + (codes & 15)
        target[part] = flags * wanted.astype(f32)
        flags_bf = flags.astype(bf16)
        running = mm(flags_bf, before.astype(f32).astype(bf16)) - 1.0
        earlier = jnp.sum(mm(above.astype(f32).astype(bf16), flags_bf), axis=1, keepdims=True)
        place[part] = jnp.where(flags > 0.0, running + earlier + count, -1.0)
        count = count + jnp.sum(jnp.sum(flags, axis=1, keepdims=True), axis=0, keepdims=True)
    return (jnp.max(count).astype(jnp.int32) + sz.edges - 1) // sz.edges


def halo_back(
    sz, part, edge_parts, own_turned, atom, sep, gathered, weights, target, place,
    feature_acc, pos_acc,
):
    in_one, out_one, back_in, back_out = weights
    ch, n, lanes = sz.channels, sz.slots, sz.edges
    first = len(sz.own)
    count = len(sz.halo) * n
    wanted = iota((lanes, lanes), 0) + jnp.asarray(part * lanes).astype(f32)
    ones, zeros = jnp.ones((1, lanes), f32), jnp.zeros((2, lanes), f32)

    def packed(edge_part, total):
        picks, sides = [], []
        for h in range(len(sz.halo)):
            pick = place[edge_part, pl.ds(h, 1), :] == wanted
            picks.append(pick.astype(f32).astype(bf16))
            rows = jnp.concatenate(
                [sep[edge_part, d, pl.ds(first + h, 1), :] for d in range(3)]
                + [
                    target[edge_part, pl.ds(h, 1), :],
                    atom[edge_part, pl.ds(first + h, 1), :] + float(h * n),
                    ones,
                    zeros,
                ],
                axis=0,
            )
            high = rows.astype(bf16).astype(f32)
            middle = (rows - high).astype(bf16).astype(f32)
            sides.append(
                jnp.concatenate([high, middle, rows - high - middle], axis=0).astype(bf16)
            )
        middle = len(picks) // 2
        for span in (slice(0, middle), slice(middle, None)):
            total = total + nt(
                jnp.concatenate(sides[span], axis=1), jnp.concatenate(picks[span], axis=1)
            )
        return total

    got = packed(0, jnp.zeros((24, lanes), f32))
    yield
    got = lax.fori_loop(1, edge_parts, packed, got)
    got = got[0:8] + got[8:16] + got[16:24]
    seps = [got[d : d + 1] for d in range(3)]
    target_row, atom_row, valid = got[3:4], got[4:5], got[5:6]
    dist_row, env_row, angular = geometry(valid, seps)
    yield
    weighted, value, slope = hidden_rows(sz, dist_row, env_row, in_one)
    yield
    radial = mm(out_one, weighted)
    chosen = iota((first * n, lanes), 0) == target_row
    one_hot = jnp.where(chosen, valid, 0.0).astype(bf16)
    xt = mm(own_turned, one_hot)
    sources = jnp.where(iota((count, lanes), 0) == atom_row, valid, 0.0).astype(bf16)
    yield
    rows = gathered.shape[0] // 2
    spread = jnp.concatenate([mm(gathered[:rows], sources), mm(gathered[rows:], sources)], axis=0)
    yield
    parts = [spread[m * ch : (m + 1) * ch] for m in range(9)]
    vector = angular[1] * parts[1] + angular[2] * parts[2] + angular[3] * parts[3]
    tensor = angular[4] * parts[4]
    for m in range(5, 9):
        tensor = tensor + angular[m] * parts[m]
    product_grad = jnp.concatenate([parts[0], vector, tensor], axis=0)
    _, radial_grad, input_grad = radial_products(sz, product_grad, radial, xt)
    products = [radial[l * ch : (l + 1) * ch] * xt for l in range(3)]
    ang_grad = [None] + [
        jnp.sum(parts[m] * products[1 if m < 4 else 2], axis=0, keepdims=True)
        for m in range(1, 9)
    ]
    yield
    dist_grad, env_grad = radial_backward(
        sz, dist_row, radial_grad, value, slope, back_in, back_out
    )
    grads = separation_grads(valid, seps, dist_row, ang_grad, dist_grad, env_grad)
    yield
    feature_acc[...] += nt(one_hot, input_grad)
    got = nt(one_hot, stacked_seps(list(grads)))
    pos_acc[...] += got[:, :8] + got[:, 8:]


def second_kernel(
    sz, total, before, after, kept, code, atom, sep, table,
    wide_in, wide_out, turned_in, turned_out, mixing,
    feature_grad, forces,
    angular, dist, env, ang_grad, dist_grad, env_grad,
    acc, acc_pos, halo_acc, halo_pos, target, place, gathered,
):
    ch, n = sz.channels, sz.slots
    cells = []
    for a in range(sz.inner_x):
        for b in range(sz.inner_y):
            far = before[a, b + 1] if b < 2 else after[a, b - 2]
            cells.append(total[a, b + (b >= 2)] + far.astype(f32))
    cotangent = jnp.concatenate(cells, axis=0)
    inv = three(nt, cotangent, mixing[0])
    halo_parts = packed_halo(sz, code, target, place)
    second_used = (jnp.max(code[1]) >= 0.0).astype(jnp.int32)
    edge_parts = 1 + second_used
    in_one, out_one = wide_in[0], wide_out[0]
    back_in, back_out = turned_in[0], turned_out[0]
    owned = len(sz.own)
    every = list(range(owned))
    acc[...] = jnp.zeros_like(acc)
    acc_pos[...] = jnp.zeros_like(acc_pos)
    halo_acc[...] = jnp.zeros_like(halo_acc)
    halo_pos[...] = jnp.zeros_like(halo_pos)

    def inv_rows(a, b):
        row = sz.inner_row(a, b)
        return inv[row : row + n]

    turned = table[...].astype(f32).T.astype(bf16)

    def back_steps(part):
        seps = [sep[part, d, :owned] for d in range(3)]
        store_geometry(part, live_rows(code[part, :owned]), seps, dist, env, angular)
        one_hot = own_hot(sz, code[part, :owned])
        found = mm(turned, one_hot)
        rows = [
            jnp.concatenate([ref[part, pl.ds(k, 1), :] for k in every], axis=1)
            for ref in (dist, env)
        ]
        yield
        weighted, value, slope = hidden_rows(sz, *rows, in_one)
        yield
        radials = mm(out_one, weighted)
        yield
        input_grad, got = yield from layer_backward(
            sz, part, every, angular, dist, atom, back_in, back_out,
            [radials[:, k * sz.edges : (k + 1) * sz.edges] for k in every],
            value, slope,
            [found[:, k * sz.edges : (k + 1) * sz.edges] for k in every],
            [kept[k] for k in every],
            [inv_rows(*sz.own[k]) for k in every],
        )
        for k, value in zip(every, got):
            store_grads(sz, k, value, ang_grad, dist_grad, env_grad)
        acc[...] += nt(one_hot, input_grad)
        own_positions(
            sz, part, code, atom, sep, dist, one_hot, ang_grad, dist_grad, env_grad, acc_pos
        )

    def back_part(part, carry):
        run_steps(back_steps(part))
        return carry

    halo_grads = [
        message_grads(sz, kept[owned + h], inv_rows(a, b)) for h, (a, b) in enumerate(sz.halo)
    ]
    for m in range(9):
        rows = jnp.concatenate([grads[m] for grads in halo_grads], axis=0)
        gathered[m * ch : (m + 1) * ch, :] = rows.T.astype(bf16)
    own_rows = [
        table[sz.inner_row(a + 1, 1) : sz.inner_row(a + 1, 1) + sz.cols_y * n, :]
        for a in range(sz.cols_x)
    ]
    own_turned = jnp.concatenate(own_rows, axis=0).astype(f32).T.astype(bf16)
    weights = (in_one, out_one, back_in, back_out)

    def halo_steps(part):
        return halo_back(
            sz, part, edge_parts, own_turned, atom, sep, gathered, weights, target, place,
            halo_acc, halo_pos,
        )

    def halo_part(part, carry):
        run_steps(halo_steps(part))
        return carry

    run_steps(back_steps(0), halo_steps(0))
    lax.fori_loop(1, edge_parts, back_part, 0)
    lax.fori_loop(1, halo_parts, halo_part, 0)
    for a in range(sz.cols_x):
        inner = sz.inner_row(a + 1, 1)
        rows = sz.cols_y * n
        mine = slice(a * rows, (a + 1) * rows)
        feature_grad[mine] = (
            acc[inner : inner + rows] + cotangent[inner : inner + rows] + halo_acc[mine]
        )
        moved = acc_pos[inner : inner + rows] + halo_pos[mine]
        for b in range(sz.cols_y):
            lane = 16 * (b + 1)
            far, start = (before[a + 1, 0], 16 * (b + 3)) if b < 1 else (after[a + 1, 2], 16 * (b - 1))
            both = total[a + 1, 2][:, lane : lane + 16]
            both = both + far.astype(f32)[:, start : start + 16]
            place_grad = moved[b * n : (b + 1) * n] + both[:, :8] + both[:, 8:]
            forces[a, :, b, :] = -(place_grad.T)[:3]


def both_ways(first, last, axis):
    devices = lax.axis_size(axis)
    near = [(i, i ^ 1) for i in range(devices)]
    far = [(i, (i + 1 if i % 2 else i - 1) % devices) for i in range(devices)]
    even = lax.axis_index(axis) % 2 == 0
    if first is last:
        to_near = to_far = first
    else:
        to_near, to_far = jnp.where(even, last, first), jnp.where(even, first, last)
    from_far = lax.ppermute(to_far, axis, far)
    from_near = lax.ppermute(to_near, axis, near)
    return jnp.where(even, from_far, from_near), jnp.where(even, from_near, from_far)


def shards(
    features, positions, species, neighbours, counts, species_gain, radial_in, radial_out, mixing, readout
):
    cols_x, cols_y, slots, channels = features.shape
    neigh = neighbours.shape[-1]
    basis, hidden = radial_in.shape[1:]
    sz = Sizes(cols_x, cols_y, slots, neigh, channels, basis, hidden)
    vmem = pl.BlockSpec(memory_space=pltpu.VMEM)
    in_hbm = pl.BlockSpec(memory_space=pltpu.HBM)
    params = pltpu.CompilerParams(vmem_limit_bytes=40 * 1024 * 1024)
    given = (features, positions.transpose(0, 2, 1, 3), species, neighbours, counts, species_gain)
    block = pl.pallas_call(
        functools.partial(block_kernel, sz, species_gain.shape[0]),
        out_shape=jax.ShapeDtypeStruct((cols_x, cols_y + 1, slots, channels), bf16),
        in_specs=[in_hbm] * 6,
        out_specs=vmem,
        scratch_shapes=[pltpu.VMEM(x.shape, x.dtype) for x in given]
        + [pltpu.SemaphoreType.DMA((6,))],
        compiler_params=pltpu.CompilerParams(vmem_limit_bytes=60 * 1024 * 1024),
        name="block_of_atoms",
    )(*given)
    assert cols_x == 2 and cols_y == 2
    before, after = both_ways(block, block, "gx")
    middle = jnp.concatenate([before, block, after], axis=0)
    before, after = both_ways(middle, middle, "gy")

    inner_atoms = sz.inner * slots
    owned = cols_x * cols_y
    edges = sz.edges
    columns = sz.inner
    grads = [
        pltpu.VMEM((9, owned, edges), f32),
        pltpu.VMEM((owned, edges), f32),
        pltpu.VMEM((owned, edges), f32),
    ]
    weights = prepared(radial_in, radial_out, mixing)
    assert slots * neigh <= 2 * edges
    kept_shapes = [
        (columns, sz.window, channels),
        (2, columns, edges),
        (2, columns, edges),
        (2, 3, columns, edges),
    ]

    def edge_scratch(count):
        return [
            pltpu.VMEM((2, 9, count, edges), f32),
            pltpu.VMEM((2, count, edges), f32),
            pltpu.VMEM((2, count, edges), f32),
        ]

    energy, back, *kept = pl.pallas_call(
        functools.partial(first_kernel, sz),
        out_shape=[
            jax.ShapeDtypeStruct((cols_x, cols_y, slots), f32),
            jax.ShapeDtypeStruct((sz.inner_x, sz.inner_y + 1, slots, channels), bf16),
        ]
        + [jax.ShapeDtypeStruct(shape, f32) for shape in kept_shapes]
        + [jax.ShapeDtypeStruct((inner_atoms, channels), bf16)],
        in_specs=[vmem] * 9,
        out_specs=[vmem] * 7,
        scratch_shapes=[pltpu.VMEM(((cols_x + 4) * (cols_y + 4) * slots, 2 * channels), bf16)]
        + [
            pltpu.VMEM((2, inner_atoms, owned * edges), bf16),
            pltpu.VMEM((columns, channels, edges), f32),
        ]
        + edge_scratch(columns)
        + [
            pltpu.VMEM((inner_atoms, channels), bf16),
            pltpu.VMEM((2, owned, channels, edges), f32),
            pltpu.VMEM((owned, sz.window, channels), f32),
            pltpu.VMEM((2, owned, 3 * channels, edges), f32),
            pltpu.VMEM((2, owned, hidden, edges), f32),
            pltpu.VMEM((2, owned, hidden, edges), f32),
        ]
        + grads
        + [pltpu.VMEM((inner_atoms, channels), f32), pltpu.VMEM((inner_atoms, 8), f32)],
        compiler_params=params,
        name="forward_and_second_back",
    )(before, middle, after, *weights, readout.reshape(1, -1))

    far = both_ways(back[:2], back[2:], "gx")
    total = back.astype(f32) + jnp.concatenate(far, axis=0).astype(f32)
    sent = total.astype(bf16)
    far = both_ways(sent[:, :3], sent[:, 2:], "gy")
    feature_grad, forces = pl.pallas_call(
        functools.partial(second_kernel, sz),
        out_shape=(
            jax.ShapeDtypeStruct((owned * slots, channels), f32),
            jax.ShapeDtypeStruct((cols_x, 3, cols_y, slots), f32),
        ),
        in_specs=[vmem] * 13,
        out_specs=(vmem,) * 2,
        scratch_shapes=edge_scratch(owned)
        + grads
        + [
            pltpu.VMEM((rows, width), f32)
            for rows in (inner_atoms, owned * slots)
            for width in (channels, 8)
        ]
        + [
            pltpu.VMEM((2, len(sz.halo), edges), f32),
            pltpu.VMEM((2, len(sz.halo), edges), f32),
            pltpu.VMEM((9 * channels, len(sz.halo) * slots), bf16),
        ],
        compiler_params=params,
        name="first_back",
    )(total, *far, *kept, *weights)
    return (
        energy,
        forces.transpose(0, 2, 1, 3),
        feature_grad.reshape(cols_x, cols_y, slots, channels),
    )


def solution(mesh):
    placed = (
        P("gx", "gy", None, None),
        P("gx", "gy", None, None),
        P("gx", "gy", None),
        P("gx", "gy", None, None),
        P("gx", "gy", None),
        P(),
        P(),
        P(),
        P(),
        P(),
    )
    return jax.shard_map(
        shards,
        mesh=mesh,
        in_specs=placed,
        out_specs=(P("gx", "gy", None), P("gx", "gy", None, None), P("gx", "gy", None, None)),
        check_vma=False,
    )
```

```python
import functools

import jax
import jax.numpy as jnp
from jax import lax
from jax.experimental import pallas as pl
from jax.experimental.pallas import tpu as pltpu
from jax.sharding import PartitionSpec as P

column = 6.0
cutoff = 6.0
softening = 0.01
root_three = 3.0**0.5
f32 = jnp.float32
bf16 = jnp.bfloat16
code_lane = 32
count_lane = 31
part_lanes = 256


def mm(a, b):
    return lax.dot_general(a, b, (((1,), (0,)), ((), ())), preferred_element_type=f32)


def nt(a, b):
    return lax.dot_general(a, b, (((1,), (1,)), ((), ())), preferred_element_type=f32)


def split(x):
    high = x.astype(bf16)
    return high, (x - high.astype(f32)).astype(bf16)


def three(product, a, b):
    a_high, a_low = split(a)
    b_high, b_low = split(b) if b.dtype == f32 else (b[0], b[1])
    return product(a_high, b_high) + product(a_low, b_high) + product(a_high, b_low)


def parted(x):
    high = lax.reduce_precision(x, 8, 7)
    return high, x - high


def prepared(radial_in, radial_out, mixing):
    high, low = parted(radial_in)
    turned = jnp.concatenate([high, high, low, jnp.zeros_like(high)], axis=1).swapaxes(1, 2)
    back_in = jnp.concatenate([high, low], axis=1)
    high, low = parted(radial_out)
    wide = jnp.concatenate([high, high, low], axis=1).swapaxes(1, 2)
    high_mix, low_mix = parted(mixing)
    mix = jnp.stack([high_mix, low_mix], axis=1)
    return [x.astype(bf16) for x in (turned, wide, back_in, high, mix)]


def harmonic_rows(ux, uy, uz):
    square = ux * ux + uy * uy + uz * uz
    return [
        jnp.ones_like(ux),
        ux,
        uy,
        uz,
        root_three * ux * uy,
        root_three * uy * uz,
        0.5 * (3.0 * uz * uz - square),
        root_three * ux * uz,
        0.5 * root_three * (ux * ux - uy * uy),
    ]


class Sizes:
    def __init__(self, cols_x, cols_y, slots, neigh, channels, basis, hidden):
        self.cols_x, self.cols_y = cols_x, cols_y
        self.slots, self.neigh, self.channels = slots, neigh, channels
        self.basis, self.hidden = basis, hidden
        self.inner_x, self.inner_y = cols_x + 2, cols_y + 2
        self.outer_y = cols_y + 4
        self.inner = self.inner_x * self.inner_y
        self.edges = part_lanes
        self.window = 9 * slots

        cells = [(a, b) for a in range(self.inner_x) for b in range(self.inner_y)]
        self.own = [c for c in cells if self.is_own(*c)]
        last = self.inner_x - 1
        self.halo = [c for c in cells if c[0] in (0, last)]
        self.halo += [(a, b) for b in (0, self.inner_y - 1) for a in range(1, last)]
        self.order = self.own + self.halo

    def is_own(self, a, b):
        return 1 <= a <= self.cols_x and 1 <= b <= self.cols_y

    def outer_row(self, a, b):
        return (a * self.outer_y + b) * self.slots

    def inner_row(self, a, b):
        return (a * self.inner_y + b) * self.slots


def each(compute):
    return lambda items: [compute(item) for item in items]


def run_steps(*steps):
    steps = list(steps)
    while steps:
        for step in list(steps):
            try:
                next(step)
            except StopIteration:
                steps.remove(step)


def loop(count, group, compute, store):
    for first in range(0, count, group):
        items = list(range(first, min(first + group, count)))
        for item, value in zip(items, compute(items)):
            store(item, value)


def iota(shape, dim):
    return lax.broadcasted_iota(jnp.int32, shape, dim).astype(f32)


def bounds_of(sz, table):
    n, ch = sz.slots, sz.channels
    rows = [sz.outer_row(a + 1, b + 1) for a, b in sz.order]
    metas = jnp.concatenate([table[row : row + n, ch:] for row in rows], axis=0)
    shape = (sz.inner * n, sz.inner * n)
    left = lax.broadcasted_iota(jnp.int32, shape, 0)
    right = lax.broadcasted_iota(jnp.int32, shape, 1)
    earlier = (left // n == right // n) & (right < left)
    sums = mm(earlier.astype(f32).astype(bf16), metas)
    low = sums[:, count_lane : count_lane + 1]
    return low, low + metas[:, count_lane : count_lane + 1].astype(f32)


def gather_columns(sz, part, table, low, high, code, atom, sep, xt):
    ch, n, edges = sz.channels, sz.slots, sz.edges
    lane = iota((n, edges), 1) + (part * edges).astype(f32)
    row = iota((n, edges), 0)
    slot = iota((sz.neigh, 2 * edges), 0)
    second = (lax.broadcasted_iota(jnp.int32, (1, 2 * edges), 1) >= edges).astype(f32)
    target = iota((12 * n, 2 * edges), 0)
    empty = jnp.zeros((n, edges), f32)

    firsts = list(range(0, sz.inner, 2))
    ats, valids, which, atoms, spreads = [], [], [], [], []
    for col, (a, b) in enumerate(sz.order):
        mine = slice(col * n, (col + 1) * n)
        at = ((lane >= low[mine]) & (lane < high[mine])).astype(f32)
        ats.append(at)
        valids.append(jnp.sum(at, axis=0, keepdims=True) - 1.0)
        which.append(lane[:1] - jnp.sum(at * low[mine], axis=0, keepdims=True))
        atoms.append(jnp.sum(at * row, axis=0, keepdims=True) + valids[-1])
    for first in firsts:
        places = [sz.outer_row(a + 1, b + 1) for a, b in sz.order[first : first + 2]]
        metas = [table[place : place + n, ch : 2 * ch] for place in places]
        turned = jnp.concatenate(metas, axis=0).astype(f32).T[: 2 * code_lane].astype(bf16)
        apart = jnp.concatenate(
            [
                jnp.concatenate([ats[first], empty], axis=1),
                jnp.concatenate([empty, ats[first + 1]], axis=1),
            ],
            axis=0,
        )
        spreads.append(mm(turned, apart.astype(bf16)))
    hots, windows, codes_of = [], [], []
    for first, spread in zip(firsts, spreads):
        (a, b), (_, other_b) = sz.order[first : first + 2]
        both = jnp.concatenate(which[first : first + 2], axis=1)
        picked = jnp.where(slot == both, spread[code_lane:], 0.0)
        codes = jnp.sum(picked, axis=0, keepdims=True)
        codes = codes + jnp.concatenate(valids[first : first + 2], axis=1)
        if other_b != b:
            width, height = 4, 3
            ahead = (codes >= 3.0 * n).astype(f32) + (codes >= 6.0 * n).astype(f32)
            rows = codes + n * (ahead + second)
        else:
            width, height = 3, 4
            rows = codes + 3.0 * n * second
        rows = jnp.where(codes < 0.0, -1.0, rows)
        hots.append((target == rows).astype(f32).astype(bf16))
        window = jnp.concatenate(
            [table[pl.ds(sz.outer_row(a + d, b), width * n), :] for d in range(height)], axis=0
        )
        windows.append(window.astype(f32).T.astype(bf16)[: ch + 32])
        codes_of.append(codes)
    founds = [mm(window, one_hot) for window, one_hot in zip(windows, hots)]
    for first, spread, codes, found in zip(firsts, spreads, codes_of, founds):
        diff = found[ch : ch + 24] - spread[:24]
        total = diff[0:8] + diff[8:16] + diff[16:24]
        for col, span in ((first, slice(0, edges)), (first + 1, slice(edges, 2 * edges))):
            code[part, pl.ds(col, 1), :] = codes[:, span]
            atom[part, pl.ds(col, 1), :] = atoms[col]
            xt[col] = found[:ch, span]
            for d in range(3):
                sep[part, d, pl.ds(col, 1), :] = total[d : d + 1, span]


def wide_rows(rows):
    return jnp.concatenate([rows[k : k + 1] for k in range(rows.shape[0])], axis=1)


def own_hot(sz, codes):
    row = lax.broadcasted_iota(jnp.int32, codes.shape, 0)
    place = jnp.zeros_like(row)
    for k, (a, b) in enumerate(sz.own):
        place = jnp.where(row == k, sz.inner_row(a - 1, b - 1), place)
    whole = codes.astype(jnp.int32)
    ahead = (((whole >> 4) * 11) >> 5) * (sz.slots * (sz.inner_y - 3))
    rows = jnp.where(codes < 0.0, -1.0, (place + whole + ahead).astype(f32))
    wide = wide_rows(rows)
    return (iota((sz.inner * sz.slots, wide.shape[1]), 0) == wide).astype(f32).astype(bf16)


def own_atoms(sz, atoms):
    row = iota(atoms.shape, 0)
    wide = wide_rows(jnp.where(atoms < 0.0, -1.0, atoms + row * float(sz.slots)))
    return (iota((len(sz.own) * sz.slots, wide.shape[1]), 0) == wide).astype(f32).astype(bf16)


def shifted_seps(part, code, sep):
    offset = code[part].astype(jnp.int32) >> 4
    step_x = (offset * 11) >> 5
    step_y = offset - 3 * step_x
    sep[part, 0] = sep[part, 0] + column * (step_x - 1).astype(f32)
    sep[part, 1] = sep[part, 1] + column * (step_y - 1).astype(f32)


def geometry(live, seps):
    sep_x, sep_y, sep_z = seps
    dist_sq = sep_x * sep_x + sep_y * sep_y + sep_z * sep_z
    env = jnp.square(jnp.maximum(1.0 - dist_sq / (cutoff * cutoff), 0.0)) * live
    rows = harmonic_rows(sep_x / cutoff, sep_y / cutoff, sep_z / cutoff)
    return jnp.sqrt(dist_sq + softening), env, rows


def store_geometry(part, live, seps, dist, env, angular):
    dist[part], env[part], rows = geometry(live, seps)
    for m, row in enumerate(rows):
        angular[part, m] = row


def live_rows(code):
    return (code >= 0.0).astype(f32)


def basis_rows(sz, dist_row):
    width = dist_row.shape[1]
    spacing = cutoff / (sz.basis - 1)
    centre = lax.broadcasted_iota(jnp.int32, (sz.basis, width), 0).astype(f32) * spacing
    shifted = (dist_row - centre) * (1.0 / spacing)
    return jnp.exp(-shifted * shifted), shifted


def sigmoid(x):
    return 0.5 * jnp.tanh(0.5 * x) + 0.5


def hidden_rows(sz, dist_row, env_row, weight_in):
    basis, _ = basis_rows(sz, dist_row)
    high = basis.astype(bf16).astype(f32)
    stacked = jnp.concatenate([high, basis - high, high, jnp.zeros_like(high)], axis=0)
    pre = mm(weight_in, stacked.astype(bf16))
    gate = sigmoid(pre)
    value = pre * gate
    weighted = value * env_row
    high, low = split(weighted)
    slope = gate * (1.0 + pre * (1.0 - gate)) * env_row
    return jnp.concatenate([high, low, high], axis=0), value, slope


def atoms_at(sz, atom, part, col):
    return (iota((sz.slots, sz.edges), 0) == atom[part, pl.ds(col, 1), :]).astype(f32)


def block_rows(angular, part, col, at):
    return [angular[part, m, pl.ds(col, 1), :] * at for m in range(1, 9)]


def layer_forward(sz, part, cols, angular, dist, env, atom, weight_in, weight_out, inputs):
    rows = [jnp.concatenate([ref[part, pl.ds(c, 1), :] for c in cols], axis=1) for ref in (dist, env)]
    weighted, value, slope = hidden_rows(sz, *rows, weight_in)
    radials = mm(weight_out, weighted)
    spans = [slice(k * sz.edges, (k + 1) * sz.edges) for k in range(len(cols))]
    sides = [message_sides(sz, part, col, angular, atom) for col in cols]
    products = [
        (radials[:, span] * jnp.concatenate([xt] * 3, axis=0)).astype(bf16)
        for span, xt in zip(spans, inputs)
    ]
    ch = sz.channels
    got = [
        [nt(both, product[l * ch : (l + 1) * ch]) for l, both in enumerate(side)]
        for side, product in zip(sides, products)
    ]
    out = []
    for span, parts in zip(spans, got):
        halves = [len(x) // 2 for x in parts]
        rows = [parts[0]] + [x[:h] + x[h:] for x, h in zip(parts[1:], halves[1:])]
        message = jnp.concatenate(rows, axis=0)
        out.append((radials[:, span], value[:, span], slope[:, span], message))
    return out


def message_sides(sz, part, col, angular, atom):
    n = sz.slots
    at = atoms_at(sz, atom, part, col)
    blocks = jnp.concatenate(block_rows(angular, part, col, at), axis=0)
    high = blocks.astype(bf16).astype(f32)
    low = blocks - high
    sides = [at.astype(bf16)]
    for rows in (slice(0, 3 * n), slice(3 * n, 8 * n)):
        sides.append(jnp.concatenate([high[rows], low[rows]], axis=0).astype(bf16))
    return sides


def invariants(sz, message):
    n = sz.slots
    squares = message * message
    got = [squares[m * n : (m + 1) * n] for m in range(9)]
    return jnp.concatenate(
        [message[:n], got[1] + got[2] + got[3], got[4] + got[5] + got[6] + got[7] + got[8]],
        axis=1,
    )


def message_grads(sz, message, cotangent):
    ch, n = sz.channels, sz.slots
    twice = 2.0 * cotangent[:, ch:]
    parts = [
        message[m * n : (m + 1) * n] * (twice[:, :ch] if m < 4 else twice[:, ch:])
        for m in range(1, 9)
    ]
    return [cotangent[:, :ch]] + parts


def radial_products(sz, product_grad, radial, xt):
    ch = sz.channels
    products, mine, input_grad = [], [], None
    for l in range(3):
        grad, part = product_grad[l * ch : (l + 1) * ch], radial[l * ch : (l + 1) * ch]
        if l:
            products.append((part * xt).astype(bf16))
        mine.append((grad * xt).astype(bf16))
        term = grad * part
        input_grad = term if input_grad is None else input_grad + term
    return products, jnp.concatenate(mine, axis=0), input_grad.astype(bf16)


def radial_backward(sz, dist_row, radial_grad, value, slope, back_in, back_out):
    weighted_grad = mm(back_out, radial_grad)
    env_row_grad = jnp.sum(weighted_grad * value, axis=0, keepdims=True)
    both = mm(back_in, (weighted_grad * slope).astype(bf16))
    basis_grad = both[: sz.basis] + both[sz.basis : 2 * sz.basis]
    basis, shifted = basis_rows(sz, dist_row)
    spacing = cutoff / (sz.basis - 1)
    dist_row_grad = jnp.sum(
        basis_grad * basis * shifted * (-2.0 / spacing), axis=0, keepdims=True
    )
    return dist_row_grad, env_row_grad


def layer_backward(
    sz, part, cols, angular, dist, atom, back_in, back_out, radials, value, slope, inputs,
    messages, cotangents,
):
    ch, n = sz.channels, sz.slots
    ats = [atoms_at(sz, atom, part, col) for col in cols]
    grads_of = [message_grads(sz, *both) for both in zip(messages, cotangents)]
    lhs = []
    for grads in grads_of:
        turned = jnp.concatenate(grads, axis=0).T
        lane = lax.broadcasted_iota(jnp.int32, turned.shape, 1)
        lhs.append(
            jnp.concatenate(
                [
                    jnp.where(lane < n, turned, 0.0),
                    jnp.where((lane >= n) & (lane < 4 * n), turned, 0.0),
                    jnp.where(lane >= 4 * n, turned, 0.0),
                ],
                axis=0,
            ).astype(bf16)
        )
    blocks = [
        jnp.concatenate([at] + block_rows(angular, part, col, at), axis=0).astype(bf16)
        for col, at in zip(cols, ats)
    ]
    yield
    product_grads = [mm(left, right) for left, right in zip(lhs, blocks)]
    yield
    triples = [
        radial_products(sz, *three_of) for three_of in zip(product_grads, radials, inputs)
    ]
    mine = [triple[1] for triple in triples]
    input_grads = [triple[2] for triple in triples]
    yield
    empty = jnp.zeros((n, ch), f32)
    wides = []
    for grads in grads_of:
        wide = [
            jnp.concatenate([g, empty] if m < 3 else [empty, g], axis=1)
            for m, g in enumerate(grads[1:])
        ]
        wides.append(jnp.concatenate(wide, axis=0).astype(bf16))
    gots = [
        mm(wide, jnp.concatenate(triple[0], axis=0)) for wide, triple in zip(wides, triples)
    ]
    yield
    ang_grads = [
        [jnp.sum(got[m * n : (m + 1) * n] * at, axis=0, keepdims=True) for m in range(8)]
        for got, at in zip(gots, ats)
    ]
    dist_row = jnp.concatenate([dist[part, pl.ds(col, 1), :] for col in cols], axis=1)
    dist_row_grad, env_row_grad = radial_backward(
        sz, dist_row, jnp.concatenate(mine, axis=1), value, slope, back_in, back_out
    )
    out = []
    for k in range(len(cols)):
        span = slice(k * sz.edges, (k + 1) * sz.edges)
        out.append((ang_grads[k], dist_row_grad[:, span], env_row_grad[:, span]))
    yield
    return jnp.concatenate(input_grads, axis=1), out


def store_grads(sz, col, value, ang_grad, dist_grad, env_grad):
    ang_grads, dist_row_grad, env_row_grad = value
    for m in range(8):
        ang_grad[m + 1, pl.ds(col, 1), :] = ang_grads[m]
    dist_grad[pl.ds(col, 1), :] = dist_row_grad
    env_grad[pl.ds(col, 1), :] = env_row_grad


def separation_grads(live, sep, dist, ang_grad, dist_grad, env_grad):
    sep_x, sep_y, sep_z = sep
    ux, uy, uz = sep_x / cutoff, sep_y / cutoff, sep_z / cutoff
    dist_sq = sep_x * sep_x + sep_y * sep_y + sep_z * sep_z
    inside = jnp.maximum(1.0 - dist_sq / (cutoff * cutoff), 0.0)
    sq_grad = dist_grad * (0.5 / dist) - env_grad * live * inside * (2.0 / (cutoff * cutoff))
    g = ang_grad
    r3 = root_three
    grad_x = g[1] + r3 * (uy * g[4] + uz * g[7] + ux * g[8]) - ux * g[6]
    grad_y = g[2] + r3 * (ux * g[4] + uz * g[5] - uy * g[8]) - uy * g[6]
    grad_z = g[3] + r3 * (uy * g[5] + ux * g[7]) + 2.0 * uz * g[6]
    return (
        2.0 * sep_x * sq_grad + grad_x / cutoff,
        2.0 * sep_y * sq_grad + grad_y / cutoff,
        2.0 * sep_z * sq_grad + grad_z / cutoff,
    )


def stacked_seps(rows):
    full = jnp.concatenate(rows + [jnp.zeros((5, rows[0].shape[1]), f32)], axis=0)
    high = full.astype(bf16).astype(f32)
    return jnp.concatenate([high, full - high], axis=0).astype(bf16)


def own_positions(sz, part, code, atom, sep, dist, hot, ang_grad, dist_grad, env_grad, acc_pos):
    owned, n = len(sz.own), sz.slots
    grads = separation_grads(
        live_rows(code[part, :owned]),
        [sep[part, d, :owned] for d in range(3)],
        dist[part, :owned],
        ang_grad,
        dist_grad[...],
        env_grad[...],
    )
    ends = jnp.concatenate([hot, own_atoms(sz, atom[part, :owned])], axis=0)
    got = nt(ends, stacked_seps([wide_rows(grad) for grad in grads]))
    got = got[:, :8] + got[:, 8:]
    atoms = sz.inner * n
    acc_pos[...] += got[:atoms]
    for k, (a, b) in enumerate(sz.own):
        row = sz.inner_row(a, b)
        acc_pos[row : row + n] -= got[atoms + k * n : atoms + (k + 1) * n]


def fetch(sources, targets, sems):
    copies = [
        pltpu.make_async_copy(source, target, sems.at[k])
        for k, (source, target) in enumerate(zip(sources, targets))
    ]
    for copy in copies:
        copy.start()
    return copies


def block_kernel(sz, kinds, *refs):
    sources, block, held, sems = refs[:6], refs[6], refs[7:13], refs[13]
    for copy in fetch(sources, held, sems):
        copy.wait()
    features, positions, species, neighbours, counts, species_gain = held
    ch, n = sz.channels, sz.slots
    gains = species_gain[...]
    gain_high = gains.astype(bf16).astype(f32)
    rest = gains - gain_high
    gain_middle = rest.astype(bf16).astype(f32)
    parts = [gain_high, gain_middle, rest - gain_middle]
    above, below = jnp.zeros((24, ch), f32), jnp.zeros((8 - kinds, ch), f32)
    parts = [jnp.concatenate([above, part, below], axis=0).astype(bf16) for part in parts]
    kind = lax.broadcasted_iota(jnp.int32, (8, n), 0)
    lane = lax.broadcasted_iota(jnp.int32, (n, code_lane), 1)
    gap = jnp.zeros((5, n), f32)
    for a in range(sz.cols_x):
        sides = []
        for b in range(sz.cols_y):
            atoms = positions[a, :, b, :]
            high = atoms.astype(bf16).astype(f32)
            rest = atoms - high
            middle = rest.astype(bf16).astype(f32)
            chosen = (kind == species[a, pl.ds(b, 1), :]).astype(f32)
            last = jnp.where(kind == 7, counts[a, pl.ds(b, 1), :].astype(f32), chosen)
            rows = [high, gap, middle, gap, rest - middle, gap, last]
            turned = jnp.concatenate(rows, axis=0).T
            picked = jnp.where((lane >= 24) & (lane < 24 + kinds), turned, 0.0).astype(bf16)
            gain = mm(picked, parts[0]) + mm(picked, parts[1]) + mm(picked, parts[2])
            place = jnp.where((lane < 24) | (lane == count_lane), turned, 0.0)
            sides.append(jnp.concatenate([place, neighbours[a, b].astype(f32)], axis=1))
            block[a, b] = (features[a, b].astype(f32) * gain).astype(bf16)
        block[a, sz.cols_y] = jnp.concatenate(sides, axis=1).astype(bf16)


def fill_table(sz, strips, table):
    ch, n = sz.channels, sz.slots
    for a in range(sz.cols_x + 4):
        for k, strip in enumerate(strips):
            meta = strip[a, sz.cols_y].astype(f32)
            for b in range(sz.cols_y):
                row = sz.outer_row(a, k * sz.cols_y + b)
                mine = meta if b == 0 else pltpu.roll(meta, ch - b * 2 * code_lane, 1)
                table[row : row + n, :ch] = strip[a, b]
                table[row : row + n, ch:] = mine.astype(bf16)


def first_kernel(
    sz, before, middle, after, wide_in, wide_out, turned_in, turned_out, mixing, readout,
    energy, back, kept, code, atom, sep, inputs_kept, table,
    hot, xt, angular, dist, env, second, second_xt, second_msg, second_radial,
    second_value, second_slope, ang_grad, dist_grad, env_grad, acc, acc_pos,
):
    ch, n = sz.channels, sz.slots
    owned = len(sz.own)
    fill_table(sz, (before, middle, after), table)
    low, high = bounds_of(sz, table)
    most = jnp.maximum(jnp.max(high).astype(jnp.int32), 1)
    parts = (most + sz.edges - 1) // sz.edges
    in_one, out_one = wide_in[0], wide_out[0]
    code[...] = jnp.full_like(code, -1.0)
    kept[...] = jnp.zeros_like(kept)

    def first_part(part, carry):
        gather_columns(sz, part, table, low, high, code, atom, sep, xt)
        shifted_seps(part, code, sep)
        seps = [sep[part, d] for d in range(3)]
        store_geometry(part, live_rows(code[part]), seps, dist, env, angular)

        def one(cols):
            inputs = [xt[col] for col in cols]
            return layer_forward(
                sz, part, cols, angular, dist, env, atom, in_one, out_one, inputs
            )

        def one_store(col, got):
            kept[col] += got[3]

        loop(sz.inner, 8, one, one_store)
        return carry

    lax.fori_loop(0, parts, first_part, 0)
    rows = [None] * sz.inner
    for col, (a, b) in enumerate(sz.order):
        rows[a * sz.inner_y + b] = invariants(sz, kept[col])
    own_rows = [
        table[(a * sz.outer_y + 1) * n : (a * sz.outer_y + 1 + sz.inner_y) * n, :ch]
        for a in range(1, 1 + sz.inner_x)
    ]
    first_out = three(mm, jnp.concatenate(rows, axis=0), mixing[0])
    inputs_kept[...] = jnp.concatenate(own_rows, axis=0)
    first_out = first_out + inputs_kept[...].astype(f32)
    second[...] = first_out.astype(bf16)

    in_two, out_two = wide_in[1], wide_out[1]
    back_in, back_out = turned_in[1], turned_out[1]
    second_msg[...] = jnp.zeros_like(second_msg)
    second_turned = second[...].astype(f32).T.astype(bf16)
    every = list(range(owned))

    def second_part(part, carry):
        one_hot = own_hot(sz, code[part, :owned])
        hot[part] = one_hot
        found = mm(second_turned, one_hot)
        inputs = [found[:, k * sz.edges : (k + 1) * sz.edges] for k in every]
        got = layer_forward(sz, part, every, angular, dist, env, atom, in_two, out_two, inputs)
        for k, (radial, value, slope, message) in zip(every, got):
            second_xt[part, k], second_radial[part, k] = inputs[k], radial
            second_value[part, k], second_slope[part, k] = value, slope
            second_msg[k] += message
        return carry

    lax.fori_loop(0, parts, second_part, 0)
    inv = jnp.concatenate([invariants(sz, second_msg[k]) for k in every], axis=0)
    own_rows = [
        second[(a * sz.inner_y + 1) * n : (a * sz.inner_y + 1 + sz.cols_y) * n, :]
        for a in range(1, 1 + sz.cols_x)
    ]
    out = three(mm, inv, mixing[1]) + jnp.concatenate(own_rows, axis=0).astype(f32)
    gate = sigmoid(out)
    weights = readout[...]
    out_grad = gate * (1.0 + out * (1.0 - gate)) * weights
    cotangents = three(nt, out_grad, mixing[1])
    acc[...] = jnp.zeros_like(acc)
    acc_pos[...] = jnp.zeros_like(acc_pos)
    for a in range(sz.cols_x):
        first = ((a + 1) * sz.inner_y + 1) * n
        acc[first : first + sz.cols_y * n] = out_grad[a * sz.cols_y * n : (a + 1) * sz.cols_y * n]

    def back_steps(part):
        input_grad, got = yield from layer_backward(
            sz, part, every, angular, dist, atom, back_in, back_out,
            [second_radial[part, k] for k in every],
            jnp.concatenate([second_value[part, k] for k in every], axis=1),
            jnp.concatenate([second_slope[part, k] for k in every], axis=1),
            [second_xt[part, k] for k in every],
            [second_msg[k] for k in every],
            [cotangents[k * n : (k + 1) * n] for k in every],
        )
        for k, value in zip(every, got):
            store_grads(sz, k, value, ang_grad, dist_grad, env_grad)
        acc[...] += nt(hot[part], input_grad)
        own_positions(
            sz, part, code, atom, sep, dist, hot[part], ang_grad, dist_grad, env_grad, acc_pos
        )

    def energy_steps():
        yield
        total = three(nt, jnp.ones((8, ch), f32), out * gate * weights)
        yield
        for k, (a, b) in enumerate(sz.own):
            energy[a - 1, b - 1 : b, :] = total[0:1, k * n : (k + 1) * n]

    def back_part(part, carry):
        run_steps(back_steps(part), energy_steps())
        return carry

    lax.fori_loop(0, parts, back_part, 0)
    for a in range(sz.inner_x):
        places = []
        for b in range(sz.inner_y):
            row = sz.inner_row(a, b)
            back[a, b + (b >= 2)] = acc[row : row + n].astype(bf16)
            full = acc_pos[row : row + n]
            high = full.astype(bf16).astype(f32)
            places += [high, full - high]
        filler = jnp.zeros((n, ch - 16 * sz.inner_y), f32)
        back[a, 2] = jnp.concatenate(places + [filler], axis=1).astype(bf16)


def packed_halo(sz, code, target, place):
    rows = len(sz.halo)
    first = len(sz.own)
    row = lax.broadcasted_iota(jnp.int32, (rows, sz.edges), 0)
    at_x, at_y = jnp.zeros_like(row), jnp.zeros_like(row)
    for h, (a, b) in enumerate(sz.halo):
        at_x, at_y = jnp.where(row == h, a, at_x), jnp.where(row == h, b, at_y)
    shape = (sz.edges, sz.edges)
    before = iota(shape, 0) <= iota(shape, 1)
    above = iota((rows, rows), 1) < iota((rows, rows), 0)
    count = jnp.zeros((1, 1), f32)
    for part in range(2):
        codes = code[part, first:].astype(jnp.int32)
        offset = codes >> 4
        step_x = (offset * 11) >> 5
        to_x = at_x + step_x - 2
        to_y = at_y + offset - 3 * step_x - 2
        inside = (to_x >= 0) & (to_x < sz.cols_x) & (to_y >= 0) & (to_y < sz.cols_y)
        flags = (inside & (codes >= 0)).astype(f32)
        wanted = (to_x * sz.cols_y + to_y) * sz.slots + (codes & 15)
        target[part] = flags * wanted.astype(f32)
        flags_bf = flags.astype(bf16)
        running = mm(flags_bf, before.astype(f32).astype(bf16)) - 1.0
        earlier = jnp.sum(mm(above.astype(f32).astype(bf16), flags_bf), axis=1, keepdims=True)
        place[part] = jnp.where(flags > 0.0, running + earlier + count, -1.0)
        count = count + jnp.sum(jnp.sum(flags, axis=1, keepdims=True), axis=0, keepdims=True)
    return (jnp.max(count).astype(jnp.int32) + sz.edges - 1) // sz.edges


def halo_back(
    sz, part, edge_parts, own_turned, atom, sep, gathered, weights, target, place,
    feature_acc, pos_acc,
):
    in_one, out_one, back_in, back_out = weights
    ch, n, lanes = sz.channels, sz.slots, sz.edges
    first = len(sz.own)
    count = len(sz.halo) * n
    wanted = iota((lanes, lanes), 0) + jnp.asarray(part * lanes).astype(f32)
    ones, zeros = jnp.ones((1, lanes), f32), jnp.zeros((2, lanes), f32)

    def packed(edge_part, total):
        picks, sides = [], []
        for h in range(len(sz.halo)):
            pick = place[edge_part, pl.ds(h, 1), :] == wanted
            picks.append(pick.astype(f32).astype(bf16))
            rows = jnp.concatenate(
                [sep[edge_part, d, pl.ds(first + h, 1), :] for d in range(3)]
                + [
                    target[edge_part, pl.ds(h, 1), :],
                    atom[edge_part, pl.ds(first + h, 1), :] + float(h * n),
                    ones,
                    zeros,
                ],
                axis=0,
            )
            high = rows.astype(bf16).astype(f32)
            middle = (rows - high).astype(bf16).astype(f32)
            sides.append(
                jnp.concatenate([high, middle, rows - high - middle], axis=0).astype(bf16)
            )
        middle = len(picks) // 2
        for span in (slice(0, middle), slice(middle, None)):
            total = total + nt(
                jnp.concatenate(sides[span], axis=1), jnp.concatenate(picks[span], axis=1)
            )
        return total

    got = packed(0, jnp.zeros((24, lanes), f32))
    yield
    got = lax.fori_loop(1, edge_parts, packed, got)
    got = got[0:8] + got[8:16] + got[16:24]
    seps = [got[d : d + 1] for d in range(3)]
    target_row, atom_row, valid = got[3:4], got[4:5], got[5:6]
    dist_row, env_row, angular = geometry(valid, seps)
    yield
    weighted, value, slope = hidden_rows(sz, dist_row, env_row, in_one)
    yield
    radial = mm(out_one, weighted)
    chosen = iota((first * n, lanes), 0) == target_row
    one_hot = jnp.where(chosen, valid, 0.0).astype(bf16)
    xt = mm(own_turned, one_hot)
    sources = jnp.where(iota((count, lanes), 0) == atom_row, valid, 0.0).astype(bf16)
    yield
    rows = gathered.shape[0] // 2
    spread = jnp.concatenate([mm(gathered[:rows], sources), mm(gathered[rows:], sources)], axis=0)
    yield
    parts = [spread[m * ch : (m + 1) * ch] for m in range(9)]
    vector = angular[1] * parts[1] + angular[2] * parts[2] + angular[3] * parts[3]
    tensor = angular[4] * parts[4]
    for m in range(5, 9):
        tensor = tensor + angular[m] * parts[m]
    product_grad = jnp.concatenate([parts[0], vector, tensor], axis=0)
    _, radial_grad, input_grad = radial_products(sz, product_grad, radial, xt)
    products = [radial[l * ch : (l + 1) * ch] * xt for l in range(3)]
    ang_grad = [None] + [
        jnp.sum(parts[m] * products[1 if m < 4 else 2], axis=0, keepdims=True)
        for m in range(1, 9)
    ]
    yield
    dist_grad, env_grad = radial_backward(
        sz, dist_row, radial_grad, value, slope, back_in, back_out
    )
    grads = separation_grads(valid, seps, dist_row, ang_grad, dist_grad, env_grad)
    yield
    feature_acc[...] += nt(one_hot, input_grad)
    got = nt(one_hot, stacked_seps(list(grads)))
    pos_acc[...] += got[:, :8] + got[:, 8:]


def second_kernel(
    sz, total, before, after, kept, code, atom, sep, table,
    wide_in, wide_out, turned_in, turned_out, mixing,
    feature_grad, forces,
    angular, dist, env, ang_grad, dist_grad, env_grad,
    acc, acc_pos, halo_acc, halo_pos, target, place, gathered,
):
    ch, n = sz.channels, sz.slots
    cells = []
    for a in range(sz.inner_x):
        for b in range(sz.inner_y):
            far = before[a, b + 1] if b < 2 else after[a, b - 2]
            cells.append(total[a, b + (b >= 2)] + far.astype(f32))
    cotangent = jnp.concatenate(cells, axis=0)
    inv = three(nt, cotangent, mixing[0])
    halo_parts = packed_halo(sz, code, target, place)
    second_used = (jnp.max(code[1]) >= 0.0).astype(jnp.int32)
    edge_parts = 1 + second_used
    in_one, out_one = wide_in[0], wide_out[0]
    back_in, back_out = turned_in[0], turned_out[0]
    owned = len(sz.own)
    every = list(range(owned))
    acc[...] = jnp.zeros_like(acc)
    acc_pos[...] = jnp.zeros_like(acc_pos)
    halo_acc[...] = jnp.zeros_like(halo_acc)
    halo_pos[...] = jnp.zeros_like(halo_pos)

    def inv_rows(a, b):
        row = sz.inner_row(a, b)
        return inv[row : row + n]

    turned = table[...].astype(f32).T.astype(bf16)

    def back_steps(part):
        seps = [sep[part, d, :owned] for d in range(3)]
        store_geometry(part, live_rows(code[part, :owned]), seps, dist, env, angular)
        one_hot = own_hot(sz, code[part, :owned])
        found = mm(turned, one_hot)
        rows = [
            jnp.concatenate([ref[part, pl.ds(k, 1), :] for k in every], axis=1)
            for ref in (dist, env)
        ]
        yield
        weighted, value, slope = hidden_rows(sz, *rows, in_one)
        yield
        radials = mm(out_one, weighted)
        yield
        input_grad, got = yield from layer_backward(
            sz, part, every, angular, dist, atom, back_in, back_out,
            [radials[:, k * sz.edges : (k + 1) * sz.edges] for k in every],
            value, slope,
            [found[:, k * sz.edges : (k + 1) * sz.edges] for k in every],
            [kept[k] for k in every],
            [inv_rows(*sz.own[k]) for k in every],
        )
        for k, value in zip(every, got):
            store_grads(sz, k, value, ang_grad, dist_grad, env_grad)
        acc[...] += nt(one_hot, input_grad)
        own_positions(
            sz, part, code, atom, sep, dist, one_hot, ang_grad, dist_grad, env_grad, acc_pos
        )

    def back_part(part, carry):
        run_steps(back_steps(part))
        return carry

    halo_grads = [
        message_grads(sz, kept[owned + h], inv_rows(a, b)) for h, (a, b) in enumerate(sz.halo)
    ]
    for m in range(9):
        rows = jnp.concatenate([grads[m] for grads in halo_grads], axis=0)
        gathered[m * ch : (m + 1) * ch, :] = rows.T.astype(bf16)
    own_rows = [
        table[sz.inner_row(a + 1, 1) : sz.inner_row(a + 1, 1) + sz.cols_y * n, :]
        for a in range(sz.cols_x)
    ]
    own_turned = jnp.concatenate(own_rows, axis=0).astype(f32).T.astype(bf16)
    weights = (in_one, out_one, back_in, back_out)

    def halo_steps(part):
        return halo_back(
            sz, part, edge_parts, own_turned, atom, sep, gathered, weights, target, place,
            halo_acc, halo_pos,
        )

    def halo_part(part, carry):
        run_steps(halo_steps(part))
        return carry

    run_steps(back_steps(0), halo_steps(0))
    lax.fori_loop(1, edge_parts, back_part, 0)
    lax.fori_loop(1, halo_parts, halo_part, 0)
    for a in range(sz.cols_x):
        inner = sz.inner_row(a + 1, 1)
        rows = sz.cols_y * n
        mine = slice(a * rows, (a + 1) * rows)
        feature_grad[mine] = (
            acc[inner : inner + rows] + cotangent[inner : inner + rows] + halo_acc[mine]
        )
        moved = acc_pos[inner : inner + rows] + halo_pos[mine]
        for b in range(sz.cols_y):
            lane = 16 * (b + 1)
            far, start = (before[a + 1, 0], 16 * (b + 3)) if b < 1 else (after[a + 1, 2], 16 * (b - 1))
            both = total[a + 1, 2][:, lane : lane + 16]
            both = both + far.astype(f32)[:, start : start + 16]
            place_grad = moved[b * n : (b + 1) * n] + both[:, :8] + both[:, 8:]
            forces[a, :, b, :] = -(place_grad.T)[:3]


def both_ways(first, last, axis):
    devices = lax.axis_size(axis)
    near = [(i, i ^ 1) for i in range(devices)]
    far = [(i, (i + 1 if i % 2 else i - 1) % devices) for i in range(devices)]
    even = lax.axis_index(axis) % 2 == 0
    if first is last:
        to_near = to_far = first
    else:
        to_near, to_far = jnp.where(even, last, first), jnp.where(even, first, last)
    from_far = lax.ppermute(to_far, axis, far)
    from_near = lax.ppermute(to_near, axis, near)
    return jnp.where(even, from_far, from_near), jnp.where(even, from_near, from_far)


def shards(
    features, positions, species, neighbours, counts, species_gain, radial_in, radial_out, mixing, readout
):
    cols_x, cols_y, slots, channels = features.shape
    neigh = neighbours.shape[-1]
    basis, hidden = radial_in.shape[1:]
    sz = Sizes(cols_x, cols_y, slots, neigh, channels, basis, hidden)
    vmem = pl.BlockSpec(memory_space=pltpu.VMEM)
    in_hbm = pl.BlockSpec(memory_space=pltpu.HBM)
    params = pltpu.CompilerParams(vmem_limit_bytes=40 * 1024 * 1024)
    given = (features, positions.transpose(0, 2, 1, 3), species, neighbours, counts, species_gain)
    block = pl.pallas_call(
        functools.partial(block_kernel, sz, species_gain.shape[0]),
        out_shape=jax.ShapeDtypeStruct((cols_x, cols_y + 1, slots, channels), bf16),
        in_specs=[in_hbm] * 6,
        out_specs=vmem,
        scratch_shapes=[pltpu.VMEM(x.shape, x.dtype) for x in given]
        + [pltpu.SemaphoreType.DMA((6,))],
        compiler_params=pltpu.CompilerParams(vmem_limit_bytes=60 * 1024 * 1024),
        name="block_of_atoms",
    )(*given)
    assert cols_x == 2 and cols_y == 2
    before, after = both_ways(block, block, "gx")
    middle = jnp.concatenate([before, block, after], axis=0)
    before, after = both_ways(middle, middle, "gy")

    inner_atoms = sz.inner * slots
    owned = cols_x * cols_y
    edges = sz.edges
    columns = sz.inner
    grads = [
        pltpu.VMEM((9, owned, edges), f32),
        pltpu.VMEM((owned, edges), f32),
        pltpu.VMEM((owned, edges), f32),
    ]
    weights = prepared(radial_in, radial_out, mixing)
    assert slots * neigh <= 2 * edges
    kept_shapes = [
        (columns, sz.window, channels),
        (2, columns, edges),
        (2, columns, edges),
        (2, 3, columns, edges),
    ]

    def edge_scratch(count):
        return [
            pltpu.VMEM((2, 9, count, edges), f32),
            pltpu.VMEM((2, count, edges), f32),
            pltpu.VMEM((2, count, edges), f32),
        ]

    energy, back, *kept = pl.pallas_call(
        functools.partial(first_kernel, sz),
        out_shape=[
            jax.ShapeDtypeStruct((cols_x, cols_y, slots), f32),
            jax.ShapeDtypeStruct((sz.inner_x, sz.inner_y + 1, slots, channels), bf16),
        ]
        + [jax.ShapeDtypeStruct(shape, f32) for shape in kept_shapes]
        + [jax.ShapeDtypeStruct((inner_atoms, channels), bf16)],
        in_specs=[vmem] * 9,
        out_specs=[vmem] * 7,
        scratch_shapes=[pltpu.VMEM(((cols_x + 4) * (cols_y + 4) * slots, 2 * channels), bf16)]
        + [
            pltpu.VMEM((2, inner_atoms, owned * edges), bf16),
            pltpu.VMEM((columns, channels, edges), f32),
        ]
        + edge_scratch(columns)
        + [
            pltpu.VMEM((inner_atoms, channels), bf16),
            pltpu.VMEM((2, owned, channels, edges), f32),
            pltpu.VMEM((owned, sz.window, channels), f32),
            pltpu.VMEM((2, owned, 3 * channels, edges), f32),
            pltpu.VMEM((2, owned, hidden, edges), f32),
            pltpu.VMEM((2, owned, hidden, edges), f32),
        ]
        + grads
        + [pltpu.VMEM((inner_atoms, channels), f32), pltpu.VMEM((inner_atoms, 8), f32)],
        compiler_params=params,
        name="forward_and_second_back",
    )(before, middle, after, *weights, readout.reshape(1, -1))

    far = both_ways(back[:2], back[2:], "gx")
    total = back.astype(f32) + jnp.concatenate(far, axis=0).astype(f32)
    sent = total.astype(bf16)
    far = both_ways(sent[:, :3], sent[:, 2:], "gy")
    feature_grad, forces = pl.pallas_call(
        functools.partial(second_kernel, sz),
        out_shape=(
            jax.ShapeDtypeStruct((owned * slots, channels), f32),
            jax.ShapeDtypeStruct((cols_x, 3, cols_y, slots), f32),
        ),
        in_specs=[vmem] * 13,
        out_specs=(vmem,) * 2,
        scratch_shapes=edge_scratch(owned)
        + grads
        + [
            pltpu.VMEM((rows, width), f32)
            for rows in (inner_atoms, owned * slots)
            for width in (channels, 8)
        ]
        + [
            pltpu.VMEM((2, len(sz.halo), edges), f32),
            pltpu.VMEM((2, len(sz.halo), edges), f32),
            pltpu.VMEM((9 * channels, len(sz.halo) * slots), bf16),
        ],
        compiler_params=params,
        name="first_back",
    )(total, *far, *kept, *weights)
    return (
        energy,
        forces.transpose(0, 2, 1, 3),
        feature_grad.reshape(cols_x, cols_y, slots, channels),
    )


def solution(mesh):
    placed = (
        P("gx", "gy", None, None),
        P("gx", "gy", None, None),
        P("gx", "gy", None),
        P("gx", "gy", None, None),
        P("gx", "gy", None),
        P(),
        P(),
        P(),
        P(),
        P(),
    )
    return jax.shard_map(
        shards,
        mesh=mesh,
        in_specs=placed,
        out_specs=(P("gx", "gy", None), P("gx", "gy", None, None), P("gx", "gy", None, None)),
        check_vma=False,
    )
```
